128 devices in a mesh: dp: 32 (over y, x, core), tensor: 4 (over z).
Axes of the slice: x: 4, y: 4, z: 4, core: 2. Of those that a mesh axis runs over, the one named last changes fastest.
Arguments:
- tokens: bfloat16 [16384, 2048], P(('dp', 'tensor')), may hold values from -6 to 6
- gain_attn: float32 [2048], replicated, may hold values from 0.5 to 1.5
- w_qkv: bfloat16 [3, 2048, 2048], P(None, None, 'tensor'), may hold values from -0.1875 to 0.1875
- w_out: bfloat16 [2048, 2048], P('tensor'), may hold values from -0.375 to 0.375
- gain_mlp: float32 [2048], replicated, may hold values from 0.5 to 1.5
- w_gate_up: bfloat16 [2, 2048, 5632], P(None, None, 'tensor'), may hold values from -0.125 to 0.125
- w_down: bfloat16 [5632, 2048], P('tensor'), may hold values from -0.15625 to 0.15625
- cotangent: bfloat16 [16384, 2048], P(('dp', 'tensor')), may hold values from -24 to 24
- lengths: int32 [32], P('dp'), may hold values from 385 to 512, as said below
Outputs:
- output: float32 [16384, 2048], P(('dp', 'tensor'))
- grad_tokens: float32 [16384, 2048], P(('dp', 'tensor'))
- grad_gain_attn: float32 [2048], replicated
- grad_qkv: float32 [3, 2048, 2048], P(None, 'dp', 'tensor')
- grad_out_proj: float32 [2048, 2048], P('tensor', 'dp')
- grad_gain_mlp: float32 [2048], replicated
- grad_gate_up: float32 [2, 2048, 5632], P(None, 'dp', 'tensor')
- grad_down: float32 [5632, 2048], P('tensor', 'dp')
The draws below stay inside these ranges and needn't reach their ends.
Inputs may be any that keep to these rules, and one draw needn't show every extreme that they name: A sequence's live tokens are its first lengths[s] positions; the rest of its 512 rows are padding. Some sequence is full in every draw.
All inputs are finite; a program needn't handle non-finite values.
Results may differ from the reference program's by a relative error of at most 0.025.
Values may be sent and summed in bfloat16 or wider, within the bound.
A program may use at most 192 MiB of HBM per device.

```python
import math
import jax
import jax.numpy as jnp
from jax import lax

D = 2048
H = 16
HD = 128
FF = 5632
SEQ_LEN = 512
SEQS = 32
TOKENS = 16384


def draw_lengths(key, part):
    key = jax.random.fold_in(key, 7)
    first_key, second_key = jax.random.split(key)
    shortfall = jax.random.randint(first_key, (SEQS,), 0, SEQ_LEN // 8 * 2)
    full_one = jax.random.randint(second_key, (), 0, SEQS)
    shortfall = jnp.where(jnp.arange(SEQS) == full_one, 0, shortfall)
    return (SEQ_LEN - shortfall).astype(jnp.int32)


def with_spikes(entries, key, source, target, blocks, factor):
    def block_of(axis_at):
        return (jnp.arange(entries.shape[axis_at]) // (entries.shape[axis_at] // blocks)).reshape((-1,) + (1,) * (entries.ndim - 1 - axis_at))

    near = jax.random.permutation(key, blocks)[block_of(target)]
    far = (block_of(target) + blocks // 2) % blocks
    return jnp.where((block_of(source) == near) | (block_of(source) == far), factor * entries, entries)


def steps_of(rng, dims, cuts, smallest, largest):
    level = 1.0
    for position, parts in cuts:
        steps = jax.random.uniform(jax.random.fold_in(jax.random.fold_in(rng, 6), position), (parts,), jnp.float32, smallest / len(cuts), largest / len(cuts))
        level = level * jnp.repeat(jnp.exp(steps), dims[position] // parts).reshape((-1,) + (1,) * (len(dims) - 1 - position))
    return level


def noise(own_key, dims, deviation, bound, cuts=(), kind=jnp.bfloat16):
    values = jax.random.normal(own_key, dims, jnp.float32) * deviation
    if len(cuts) > 0:
        values = steps_of(own_key, dims, cuts, -0.22, 0.18) * values
    return jnp.clip(values, min=-bound, max=bound).astype(kind)


def bell_draw_with(own_key, extent, width, limit, cuts, heavy, kind=jnp.bfloat16):
    drawn = width * jax.random.normal(own_key, extent, jnp.float32)
    if cuts:
        drawn = drawn * steps_of(own_key, extent, cuts, -0.22, 0.18)
    return jnp.clip(with_spikes(drawn, jax.random.fold_in(own_key, 3), *heavy), -limit, limit).astype(kind)


def setup_inputs(seed: int = 0) -> dict:
    arg_keys = jax.random.split(jax.random.key(seed), 10)
    tokens = noise(arg_keys[0], (TOKENS, D), 1.0, 6.0, ((0, 128),))
    gain_attn = jnp.clip(1.0 + 0.1 * jax.random.normal(arg_keys[1], (D,), jnp.float32), 0.5, 1.5)
    w_qkv = noise(arg_keys[2], (3, D, H * HD), (D // 2) ** -0.5, 0.1875, ((2, 4),))
    w_out = noise(arg_keys[3], (H * HD, D), (H * HD // 8) ** -0.5, 0.375, ((0, 4),))
    gain_mlp = jnp.clip(1.0 + 0.1 * jax.random.normal(arg_keys[4], (D,), jnp.float32), 0.5, 1.5)
    w_gate_up = noise(arg_keys[5], (2, D, FF), D ** -0.5, 0.125, ((2, 4),))
    w_down = noise(arg_keys[6], (FF, D), (FF // 4) ** -0.5, 0.15625, ((0, 4),))
    cotangent = bell_draw_with(arg_keys[7], (TOKENS, D), 1.0, 24.0, ((0, 128),), (0, 1, 128, 5.5))
    lengths = draw_lengths(jax.random.fold_in(arg_keys[9], 71), 0)
    return {"tokens": tokens, "gain_attn": gain_attn, "w_qkv": w_qkv, "w_out": w_out, "gain_mlp": gain_mlp, "w_gate_up": w_gate_up, "w_down": w_down, "cotangent": cotangent, "lengths": lengths}


@jax.custom_vjp
def low(v):
    return lax.optimization_barrier(v.astype(jnp.bfloat16)).astype(jnp.float32)

@jax.custom_vjp
def low_back(v):
    return v

def low_keep(v):
    return (low(v), None)

def low_pass(kept, grad):
    return (grad,)

def back_keep(v):
    return (v, None)

def back_low(kept, grad):
    return (low(grad),)
low.defvjp(low_keep, low_pass)
low_back.defvjp(back_keep, back_low)
epsilon = 1e-05
highest = lax.Precision.HIGHEST

def rotary_tables(length_rows, head_size):
    half_size = head_size // 2
    positions = jnp.arange(length_rows, dtype=jnp.float32)[:, None, None]
    frequency = jnp.exp(jnp.arange(half_size, dtype=jnp.float32) * (-2.0 * math.log(10000.0) / head_size))
    angles = positions * frequency
    return (jnp.cos(angles), jnp.sin(angles))

def rotate(values_in, cos_table, sin_table):
    half_size = values_in.shape[-1] // 2
    first_half = values_in[..., :half_size]
    second_half = values_in[..., half_size:]
    return jnp.concatenate([first_half * cos_table - second_half * sin_table, second_half * cos_table + first_half * sin_table], axis=-1)

def allowed_mask(first_row, block_rows, length_rows, live_rows):
    query_rows = first_row + jnp.arange(block_rows, dtype=jnp.int32)[:, None]
    key_rows = jnp.arange(length_rows, dtype=jnp.int32)[None, :]
    return (key_rows <= query_rows) & (key_rows < live_rows)

def attention(queries, keys_rot, values_in, live_rows):
    length_rows = queries.shape[0]
    block_rows = min(512, length_rows)
    blocks = length_rows // block_rows

    def one_block(block_item):
        query_block, block_index = block_item
        scores = low_back(jnp.einsum('qhd,khd->hqk', query_block, keys_rot, precision=highest))
        allowed = allowed_mask(block_index * block_rows, block_rows, length_rows, live_rows)
        scores = jnp.where(allowed[None], scores, -1e+30)
        row_top = lax.optimization_barrier(jnp.max(scores, axis=-1, keepdims=True))
        exps = jnp.exp(scores - row_top)
        probs = low(exps / lax.optimization_barrier(jnp.sum(exps, axis=-1, keepdims=True)))
        return jnp.einsum('hqk,khd->qhd', probs, values_in, precision=highest)
    pieces = lax.map(jax.checkpoint(one_block), (queries.reshape(blocks, block_rows, H, HD), jnp.arange(blocks, dtype=jnp.int32)))
    return pieces.reshape(length_rows, H, HD)

def layer(stream, gain_attn, w_qkv, w_out, gain_mlp, w_gate_up, w_down, live_rows):
    length_rows = stream.shape[0]
    inv_attn = lax.rsqrt(lax.optimization_barrier(jnp.mean(stream * stream, axis=-1, keepdims=True)) + epsilon)
    normed_attn = low(stream * inv_attn * gain_attn)
    projected = low_back(jnp.einsum('td,jdf->jtf', normed_attn, w_qkv, precision=highest))
    cos_table, sin_table = rotary_tables(length_rows, HD)
    shape_heads = (length_rows, H, HD)
    queries = low(rotate(projected[0].reshape(shape_heads), cos_table, sin_table) * HD ** (-0.5))
    keys_rot = low(rotate(projected[1].reshape(shape_heads), cos_table, sin_table))
    values_in = low(projected[2].reshape(shape_heads))
    attended = attention(queries, keys_rot, values_in, live_rows)
    context = low(low_back(attended.reshape(length_rows, H * HD)))
    middle = stream + low_back(jnp.dot(context, w_out, precision=highest))
    inv_mlp = lax.rsqrt(lax.optimization_barrier(jnp.mean(middle * middle, axis=-1, keepdims=True)) + epsilon)
    normed_mlp = low(middle * inv_mlp * gain_mlp)
    gate_up = low_back(jnp.einsum('td,jdf->jtf', normed_mlp, w_gate_up, precision=highest))
    gate_part = gate_up[0]
    hidden = low(gate_part * jax.nn.sigmoid(gate_part) * gate_up[1])
    return middle + jnp.dot(hidden, w_down, precision=highest)

def reference(tokens, gain_attn, w_qkv, w_out, gain_mlp, w_gate_up, w_down, cotangent, lengths):
    weights = (gain_attn.astype(jnp.float32), w_qkv.astype(jnp.float32), w_out.astype(jnp.float32), gain_mlp.astype(jnp.float32), w_gate_up.astype(jnp.float32), w_down.astype(jnp.float32))
    seq_tokens = tokens.astype(jnp.float32).reshape(SEQS, SEQ_LEN, D)
    seq_grads = cotangent.astype(jnp.float32).reshape(SEQS, SEQ_LEN, D)
    positions = jnp.arange(SEQ_LEN, dtype=jnp.int32)

    def one_sequence(totals, seq_item):
        stream, grad_in, live_rows = seq_item
        valid_rows = (positions < live_rows).astype(jnp.float32)[:, None]

        def forward(block_in, gain_one, proj_qkv, proj_out, gain_two, proj_gate_up, proj_down):
            return layer(block_in, gain_one, proj_qkv, proj_out, gain_two, proj_gate_up, proj_down, live_rows)
        result, pullback = jax.vjp(forward, stream, weights[0], weights[1], weights[2], weights[3], weights[4], weights[5])
        grads = pullback(grad_in * valid_rows)
        totals = tuple((running + extra for running, extra in zip(totals, grads[1:])))
        return (totals, (result, grads[0]))
    empty_grads = tuple((jnp.zeros_like(weight) for weight in weights))
    totals, (results, grad_rows) = lax.scan(one_sequence, empty_grads, (seq_tokens, seq_grads, lengths))
    return (results.reshape(TOKENS, D), grad_rows.reshape(TOKENS, D), totals[0], totals[1], totals[2], totals[3], totals[4], totals[5])
```

```python
import functools
import math

import jax
import jax.numpy as jnp
import numpy as np
from jax import lax
from jax.experimental import pallas as pl
from jax.experimental.pallas import tpu as pltpu
from jax.sharding import PartitionSpec as P

D = 2048
HD = 128
FF = 1408
ROWS = 128
SEQ = 512
HEADS = 4
EPS = 1e-05
BF = jnp.bfloat16
F32 = jnp.float32
MESH = pl.DeviceIdType.MESH
OFFS = (0, 3, 1, 2)

CX = (384, 768, 128, 384)
CY = (384, 640, 128, 384)
COLS = tuple(a + b for a, b in zip(CX, CY))
BASE = (0, 768, 2176, 2432)
ALL = 3200


def nn(a, b):
    return lax.dot_general(a, b, (((1,), (0,)), ((), ())), preferred_element_type=F32)


def nt(a, b):
    return lax.dot_general(a, b, (((1,), (1,)), ((), ())), preferred_element_type=F32)


def tn(a, b):
    return lax.dot_general(a, b, (((0,), (0,)), ((), ())), preferred_element_type=F32)


def rotary_tables():
    half = HD // 2
    freq = np.exp(np.arange(half, dtype=np.float64) * (-2.0 * math.log(10000.0) / HD))
    angles = np.arange(SEQ, dtype=np.float64)[:, None] * freq
    cos, sin = np.cos(angles), np.sin(angles)
    return (
        np.concatenate([cos, cos], axis=1).astype(np.float32),
        np.concatenate([-sin, sin], axis=1).astype(np.float32),
    )


class Place:
    def __init__(self):
        self.dp = lax.axis_index("dp")
        self.t = lax.axis_index("tensor")
        self.c = self.dp % 2
        self.x = (self.dp // 2) % 4
        self.y = self.dp // 8

    def z(self, d):
        return (self.dp, (self.t + d) % 4)

    def xs(self, d):
        return (self.y * 8 + ((self.x + d) % 4) * 2 + self.c, self.t)

    def ys(self, d):
        return (((self.y + d) % 4) * 8 + self.x * 2 + self.c, self.t)

    def core(self):
        return (self.dp + 1 - 2 * self.c, self.t)


def remote(src, dst, ssem, rsem, device):
    return pltpu.make_async_remote_copy(
        src_ref=src, dst_ref=dst, send_sem=ssem, recv_sem=rsem, device_id=device, device_id_type=MESH
    )


class Gather:
    def __init__(self, place, buf, ssem, rsem, relative):
        self.place, self.buf, self.ssem, self.rsem, self.relative = place, buf, ssem, rsem, relative

    def row(self, slot, half):
        if self.relative:
            return pl.ds(slot * 128 + half * 64, 64)
        block = (self.place.t + OFFS[slot]) % 4
        return pl.ds(pl.multiple_of(block * 128 + half * 64, 64), 64)

    def copy(self, k):
        slot, half, to, there = (
            (0, 0, 1, 1),
            (0, 1, 1, 1),
            (0, 1, -1, 2),
            (0, 0, -1, 2),
            (1, 0, 1, 3),
            (2, 1, -1, 3),
        )[k]
        src = self.buf.at[self.row(slot, half)]
        dst = self.buf.at[self.row(there, half)] if self.relative else src
        return remote(src, dst, self.ssem.at[k], self.rsem.at[k], self.place.z(to))

    def start(self):
        for k in (0, 2, 1, 3):
            self.copy(k).start()

    def relay(self):
        self.copy(0).wait_recv()
        self.copy(4).start()
        self.copy(2).wait_recv()
        self.copy(5).start()

    def near(self):
        self.copy(1).wait_recv()
        self.copy(3).wait_recv()

    def far(self):
        self.copy(4).wait_recv()
        self.copy(5).wait_recv()

    def done(self):
        for k in range(6):
            self.copy(k).wait_send()


class Scatter:
    def __init__(self, place, part, relays, recv, ssem, rsem):
        self.place, self.part, self.relays, self.recv = place, part, relays, recv
        self.ssem, self.rsem = ssem, rsem

    def rows(self, slot, half):
        return pl.ds(slot * 128 + half * 64, 64)

    def copy(self, k):
        part, relays, recv = self.part, self.relays, self.recv
        src, dst, to = (
            (part.at[self.rows(3, 0)], relays.at[0], 1),
            (part.at[self.rows(2, 1)], recv.at[0, self.rows(0, 1)], 1),
            (part.at[self.rows(3, 1)], relays.at[1], -1),
            (part.at[self.rows(1, 0)], recv.at[1, self.rows(0, 0)], -1),
            (part.at[self.rows(2, 0)], recv.at[0, self.rows(0, 0)], 1),
            (part.at[self.rows(1, 1)], recv.at[1, self.rows(0, 1)], -1),
        )[k]
        return remote(src, dst, self.ssem.at[k], self.rsem.at[k], self.place.z(to))

    def start(self, *which):
        for k in which:
            self.copy(k).start()

    def relay(self):
        for k, slot, half, out in ((0, 2, 0, 4), (2, 1, 1, 5)):
            self.copy(k).wait_recv()
            index = 0 if k == 0 else 1

            @pl.loop(0, 4)
            def _(r):
                here = pl.ds(pl.multiple_of(slot * 128 + half * 64 + r * 16, 16), 16)
                there = pl.ds(pl.multiple_of(r * 16, 16), 16)
                total = self.part[here, :].astype(F32) + self.relays[index, there, :].astype(F32)
                self.part[here, :] = total.astype(BF)

            self.copy(out).start()

    def finish(self):
        for k in (1, 3, 4, 5):
            self.copy(k).wait_recv()

    def total(self, rows):
        return (
            self.part[rows, :].astype(F32)
            + self.recv[0, rows, :].astype(F32)
            + self.recv[1, rows, :].astype(F32)
        )

    def done(self):
        for k in range(6):
            self.copy(k).wait_send()


def sixteen(r):
    return pl.ds(pl.multiple_of(r * 16, 16), 16)


def own_rows(place, r):
    return pl.ds(pl.multiple_of(place.t * 128 + r * 16, 16), 16)


def kernel(names, *refs):
    ref = dict(zip(names, refs))
    place = Place()
    tok, cot, live = ref["tok"], ref["cot"], ref["lengths"]
    wq, wo, wgu, wd = ref["wq"], ref["wo"], ref["wgu"], ref["wd"]
    attn, qkv, probs, ctx = ref["attn"], ref["qkv"], ref["probs"], ref["ctx"]
    middle, mlp, masked, branch = ref["middle"], ref["mlp"], ref["masked"], ref["branch"]
    hgg, gctx, gproj, gmid = ref["hgg"], ref["gctx"], ref["gproj"], ref["gmid"]
    cos_t, sin_t, gain1, gain2 = ref["cos"], ref["sin"], ref["gain1"], ref["gain2"]
    xa, xb = ref["xa"], [ref[f"xb{g}"] for g in range(4)]
    r1x, r1y = [ref[f"r1x{g}"] for g in range(4)], [ref[f"r1y{g}"] for g in range(4)]
    r2, final, shares = ref["r2"], ref["final"], ref["shares"]
    gacc, grecv = ref["gacc"], ref["grecv"]
    zs, zr, lsem = ref["zs"], ref["zr"], ref["lsem"]
    live_rows = live[0]

    loads = [pltpu.make_async_copy(ref["wq_h"].at[j], wq.at[j], lsem.at[j]) for j in range(3)]
    loads.append(pltpu.make_async_copy(ref["wo_h"], wo, lsem.at[3]))
    loads += [pltpu.make_async_copy(ref["wgu_h"].at[j], wgu.at[j], lsem.at[4 + j]) for j in range(2)]
    loads.append(pltpu.make_async_copy(ref["wd_h"], wd, lsem.at[6]))
    for load in loads:
        load.start()

    barrier = pltpu.get_barrier_semaphore()
    partners = [place.z(d) for d in (1, 2, 3)]
    partners += [place.xs(d) for d in (1, 2, 3)] + [place.ys(d) for d in (1, 2, 3)] + [place.core()]
    for device in partners:
        pl.semaphore_signal(barrier, inc=1, device_id=device, device_id_type=MESH)

    @pl.loop(0, 8)
    def _(r):
        v = tok[sixteen(r), :].astype(F32)
        inv = lax.rsqrt(jnp.mean(v * v, axis=-1, keepdims=True) + EPS)
        attn[own_rows(place, r), :] = (v * inv * gain1[...]).astype(BF)

    pl.semaphore_wait(barrier, len(partners))

    ag1 = Gather(place, attn, zs.at[0], zr.at[0], False)
    agm = Gather(place, masked, zs.at[1], zr.at[1], True)
    ag2 = Gather(place, mlp, zs.at[2], zr.at[2], True)
    ag4 = Gather(place, branch, zs.at[3], zr.at[3], False)
    rs1 = Scatter(place, ref["pa"], ref["relay_a"], ref["recv_a"], zs.at[4], zr.at[4])
    rs3 = Scatter(place, ref["pa"], ref["relay_a"], ref["recv_a"], zs.at[5], zr.at[5])
    rs4 = Scatter(place, ref["pa"], ref["relay_a"], ref["recv_a"], zs.at[6], zr.at[6])
    rs2 = Scatter(place, ref["pb"], ref["relay_b"], ref["recv_b"], zs.at[7], zr.at[7])

    ag1.start()

    @pl.loop(0, 8)
    def _(r):
        at = place.t * ROWS + r * 16 + lax.broadcasted_iota(jnp.int32, (16, 1), 0)
        v = cot[sixteen(r), :].astype(F32)
        masked[sixteen(r), :] = jnp.where(at < live_rows, v, 0.0).astype(BF)

    def project(slot):
        block = (place.t + OFFS[slot]) % 4
        rows = pl.ds(pl.multiple_of(block * 128, 128), 128)
        for j in range(3):
            p = nn(attn[rows, :], wq[j])
            if j == 2:
                qkv[rows, 1024:1536] = p.astype(BF)
                continue
            for h in range(HEADS):
                v = p[:, h * HD : (h + 1) * HD]
                v = v * cos_t[rows, :] + pltpu.roll(v, 64, 1) * sin_t[rows, :]
                if j == 0:
                    v = v * HD ** (-0.5)
                qkv[rows, j * 512 + h * HD : j * 512 + (h + 1) * HD] = v.astype(BF)

    for load in loads[:3]:
        load.wait()
    project(0)
    ag1.relay()
    ag1.near()
    agm.start()
    project(1)
    project(2)
    ag1.far()
    project(3)

    @pl.loop(0, HEADS)
    def _(h):
        def cols(j):
            return pl.ds(pl.multiple_of(j * 512 + h * HD, HD), HD)

        for q in range(2):
            rows, keys = pl.ds(q * 256, 256), (q + 1) * 256
            scores = nt(qkv[rows, cols(0)], qkv[0:keys, cols(1)])
            at = q * 256 + lax.broadcasted_iota(jnp.int32, (256, keys), 0)
            key = lax.broadcasted_iota(jnp.int32, (256, keys), 1)
            scores = jnp.where((key <= at) & (key < live_rows), scores, -1e30)
            e = jnp.exp(scores - jnp.max(scores, axis=-1, keepdims=True))
            p = (e * (1.0 / jnp.sum(e, axis=-1, keepdims=True))).astype(BF)
            probs[h, rows, 0:keys] = p
            ctx[rows, cols(0)] = nn(p, qkv[0:keys, cols(2)]).astype(BF)

    agm.relay()
    loads[3].wait()

    def out_part(slot):
        block = (place.t + OFFS[slot]) % 4
        rows = pl.ds(pl.multiple_of(block * 128, 128), 128)

        @pl.loop(0, 4)
        def _(n):
            at = pl.ds(pl.multiple_of(n * 512, 512), 512)
            rs1.part[slot * 128 : (slot + 1) * 128, at] = nn(ctx[rows, :], wo[:, at]).astype(BF)

    out_part(3)
    rs1.start(0, 2)
    out_part(2)
    rs1.start(1)
    out_part(1)
    rs1.start(3)
    out_part(0)

    other = 1 - place.c
    xs, xr = ref["xs"], ref["xr"]

    def half(group):
        if group == 0:
            return hgg.at[0, :, pl.ds(pl.multiple_of(other * 640, 128), 768)]
        if group == 1:
            return hgg.at[1 + other]
        if group == 2:
            return ctx.at[:, pl.ds(pl.multiple_of(other * 256, 256), 256)]
        return gproj.at[:, pl.ds(pl.multiple_of(other * 768, 256), 768)]

    def swap_a(group):
        src = (masked, mlp, branch, attn)[group]
        return remote(src, xa.at[group], xs.at[group], xr.at[group], place.core())

    def swap_b(group):
        return remote(half(group), xb[group], xs.at[4 + group], xr.at[4 + group], place.core())

    swap_a(3).start()
    swap_b(2).start()

    rs1.relay()
    agm.near()
    agm.far()
    swap_a(0).start()
    rs1.finish()

    @pl.loop(0, 8)
    def _(r):
        rows = sixteen(r)
        v = tok[rows, :].astype(F32) + rs1.total(rows)
        middle[rows, :] = v
        inv = lax.rsqrt(jnp.mean(v * v, axis=-1, keepdims=True) + EPS)
        mlp[rows, :] = (v * inv * gain2[...]).astype(BF)

    rs1.done()
    ag2.start()
    for load in loads[4:]:
        load.wait()

    def feed(first, count):
        rows = slice(first, first + count)
        for n0, n1 in ((0, 512), (512, 1024), (1024, 1408)):
            gate = nn(mlp[rows, :], wgu[0, :, n0:n1])
            up = nn(mlp[rows, :], wgu[1, :, n0:n1])
            grad = nt(masked[rows, :], wd[n0:n1, :])
            sig = jax.nn.sigmoid(gate)
            silu = gate * sig
            hgg[0, rows, n0:n1] = (silu * up).astype(BF)
            hgg[1, rows, n0:n1] = (grad * up * sig * (1.0 + gate * (1.0 - sig))).astype(BF)
            hgg[2, rows, n0:n1] = (grad * silu).astype(BF)

        @pl.loop(0, 4)
        def _(n):
            at = pl.ds(pl.multiple_of(n * 512, 512), 512)
            part = nt(hgg[1, rows, :], wgu[0, at, :]) + nt(hgg[2, rows, :], wgu[1, at, :])
            rs3.part[rows, at] = part.astype(BF)

    feed(0, 128)
    ag2.relay()
    ag2.near()
    feed(128, 256)
    rs3.start(1, 3)
    ag2.far()
    feed(384, 128)
    rs3.start(0, 2)
    swap_a(1).start()
    swap_b(0).start()
    swap_b(1).start()

    @pl.loop(0, 4)
    def _(n):
        at = pl.ds(pl.multiple_of(n * 512, 512), 512)
        rs2.part[:, at] = nn(hgg[0], wd[:, at]).astype(BF)

    rs3.relay()
    rs2.start(0, 2, 1, 3)

    own_b = (
        hgg.at[0, :, pl.ds(pl.multiple_of(place.c * 640, 128), 768)],
        hgg.at[1 + place.c],
        ctx.at[:, pl.ds(pl.multiple_of(place.c * 256, 256), 256)],
        gproj.at[:, pl.ds(pl.multiple_of(place.c * 768, 256), 768)],
    )
    own_a = (masked, mlp, branch, attn)
    other_a = (wd.at[0:512], wd.at[512:1024], wd.at[0:512], wd.at[512:1024])
    other_b = (wgu.at[0, 0:512, 0:768], ref["pa"].at[:, 0:1408], hgg.at[1, :, 0:256], hgg.at[0, :, 0:768])
    osem = ref["osem"]

    def bring(group):
        return (
            pltpu.make_async_copy(xa.at[group], other_a[group], osem.at[group]),
            pltpu.make_async_copy(xb[group], other_b[group], osem.at[4 + group]),
        )

    def piece(group, axis, tile, first, count):
        if group == 3 and axis == 1:
            return mlp.at[pl.ds(first, count), pl.ds(pl.multiple_of(tile * 384, 128), 384)]
        plane, base = ((1, 0), (0, 0), (1, 768), (1, 1024))[group]
        lo = base if axis == 0 else base + CX[group]
        width = CX[group] if axis == 0 else CY[group]
        rows = pl.ds(pl.multiple_of(tile * 512 + first, 128), count)
        return wgu.at[plane, rows, lo : lo + width]

    p1xs, p1xr, p1ys, p1yr = ref["p1xs"], ref["p1xr"], ref["p1ys"], ref["p1yr"]

    def send_x(group, d, tile):
        first = pl.multiple_of(((place.x + d) % 4) * 128, 128)
        dst = r1x[group].at[d - 1, pl.ds(pl.multiple_of(tile * 128, 128), 128)]
        sem = (group * 3 + d - 1) * 4 + tile
        return remote(piece(group, 0, tile, first, 128), dst, p1xs.at[sem], p1xr.at[sem], place.xs(d))

    def send_y(group, d):
        sem = group * 3 + d - 1
        src = piece(group, 1, (place.y + d) % 4, 0, 512)
        return remote(src, r1y[group].at[d - 1], p1ys.at[sem], p1yr.at[sem], place.ys(d))

    def gradient(group, step):
        tile = (place.y + 1 + step) % 4
        at = pl.ds(pl.multiple_of(tile * 512, 512), 512)
        lo = 0
        for axis, width in ((0, CX[group]), (1, CY[group])):
            own, oth = own_b[group].at[:, lo : lo + width], other_b[group].at[:, lo : lo + width]
            out = tn(own_a[group][:, at], own[...]) + tn(other_a[group][:, at], oth[...])
            piece(group, axis, tile, 0, 512)[...] = out.astype(BF)
            lo += width
        for d in (1, 2, 3):
            send_x(group, d, tile).start()

            @pl.when(step == d - 1)
            def _():
                send_y(group, d).start()

    def fetch(group):
        swap_a(group).wait_recv()
        swap_b(group).wait_recv()
        for copy in bring(group):
            copy.start()

    def fetched(group):
        for copy in bring(group):
            copy.wait()

    fetch(0)
    fetched(0)

    @pl.loop(0, 4)
    def _(step):
        gradient(0, step)

    rs3.finish()

    def fold(v):
        return jnp.concatenate([v[:, i * 512 : (i + 1) * 512] for i in range(4)], axis=0)

    def mlp_back(r, total):
        rows = sixteen(r)
        grad = rs3.total(rows)
        v = middle[rows, :]
        inv = lax.rsqrt(jnp.mean(v * v, axis=-1, keepdims=True) + EPS)
        scaled = grad * gain2[...]
        back = (
            masked[rows, :].astype(F32)
            + inv * scaled
            - v * (inv * inv * inv) * jnp.mean(v * scaled, axis=-1, keepdims=True)
        )
        gmid[rows, :] = back
        branch[own_rows(place, r), :] = back.astype(BF)
        return total + jnp.sum(grad * v * inv, axis=0, keepdims=True)

    gain2_part = lax.fori_loop(0, 8, mlp_back, jnp.zeros((1, D), F32))
    gacc[0, 4:8, :] = fold(gain2_part)
    ag4.start()
    rs3.done()
    fetch(1)
    rs2.relay()
    fetched(1)

    @pl.loop(0, 2)
    def _(step):
        gradient(1, step)

    ag4.relay()

    @pl.loop(2, 4)
    def _(step):
        gradient(1, step)

    ag4.near()
    ag4.far()
    swap_a(2).start()

    @pl.loop(0, 2)
    def _(n):
        at = pl.ds(pl.multiple_of(n * 256, 256), 256)
        gctx[:, at] = nt(branch[...], wo[at, :]).astype(BF)

    def turn_back(v, rows):
        return v * cos_t[rows, :] - pltpu.roll(v, 64, 1) * sin_t[rows, :]

    @pl.loop(0, HEADS)
    def _(h):
        def cols(j):
            return pl.ds(pl.multiple_of(j * 512 + h * HD, HD), HD)

        def part(q):
            rows, keys = pl.ds(q * 256, 256), (q + 1) * 256
            p = probs[h, rows, 0:keys]
            grad = gctx[rows, cols(0)]
            wide = p.astype(F32)
            gp = nt(grad, qkv[0:keys, cols(2)])
            gs = (wide * (gp - jnp.sum(wide * gp, axis=-1, keepdims=True))).astype(BF)
            gq = nn(gs, qkv[0:keys, cols(1)])
            gproj[rows, cols(0)] = (turn_back(gq, rows) * HD ** (-0.5)).astype(BF)
            return tn(gs, qkv[rows, cols(0)]), tn(p, grad)

        k1, v1 = part(1)
        k0, v0 = part(0)
        lo, hi = slice(0, 256), slice(256, 512)
        gproj[lo, cols(1)] = turn_back(k0 + k1[lo], lo).astype(BF)
        gproj[hi, cols(1)] = turn_back(k1[hi], hi).astype(BF)
        gproj[lo, cols(2)] = (v0 + v1[lo]).astype(BF)
        gproj[hi, cols(2)] = v1[hi].astype(BF)

    swap_b(3).start()

    def attn_part(slot):
        block = (place.t + OFFS[slot]) % 4
        rows = pl.ds(pl.multiple_of(block * 128, 128), 128)

        @pl.loop(0, 4)
        def _(n):
            at = pl.ds(pl.multiple_of(n * 512, 512), 512)
            part = nt(gproj[rows, 0:512], wq[0, at, :])
            for j in (1, 2):
                part = part + nt(gproj[rows, j * 512 : (j + 1) * 512], wq[j, at, :])
            rs4.part[slot * 128 : (slot + 1) * 128, at] = part.astype(BF)

    attn_part(3)
    rs4.start(0, 2)
    attn_part(2)
    rs4.start(1)
    attn_part(1)
    rs4.start(3)
    attn_part(0)

    rs2.finish()

    @pl.loop(0, 8)
    def _(r):
        rows = sixteen(r)
        middle[rows, :] = middle[rows, :] + rs2.total(rows)

    out_copy = pltpu.make_async_copy(middle, ref["output"], lsem.at[7])
    out_copy.start()
    rs4.relay()

    swap_a(1).wait_send()
    swap_b(0).wait_send()
    swap_b(1).wait_send()
    ag2.done()
    for group in (3, 2):
        fetch(group)
    for group in (3, 2):
        fetched(group)

        @pl.loop(0, 4)
        def _(step):
            gradient(group, step)

    rs4.finish()

    def attn_back(r, total):
        rows = sixteen(r)
        grad = rs4.total(rows)
        v = tok[rows, :].astype(F32)
        inv = lax.rsqrt(jnp.mean(v * v, axis=-1, keepdims=True) + EPS)
        scaled = grad * gain1[...]
        gmid[rows, :] = (
            gmid[rows, :]
            + inv * scaled
            - v * (inv * inv * inv) * jnp.mean(v * scaled, axis=-1, keepdims=True)
        )
        return total + jnp.sum(grad * v * inv, axis=0, keepdims=True)

    gain1_part = lax.fori_loop(0, 8, attn_back, jnp.zeros((1, D), F32))
    gacc[0, 0:4, :] = fold(gain1_part)
    tok_copy = pltpu.make_async_copy(gmid, ref["grad_tokens"], lsem.at[8])
    tok_copy.start()

    gs, gr = ref["gs"], ref["gr"]

    def spread(stage):
        count = 2 if stage == 3 else 4
        me = (place.t, place.x, place.y, place.c)[stage]
        out = []
        for d in range(1, count):
            device = (place.z, place.xs, place.ys, lambda _: place.core())[stage](d)
            k = stage * 3 + d - 1
            out.append(remote(gacc.at[stage], grecv.at[stage * 4 + me], gs.at[k], gr.at[k], device))
        return out, count, me

    def spread_start(stage):
        copies, _, me = spread(stage)
        grecv[stage * 4 + me] = gacc[stage]
        for copy in copies:
            copy.start()

    def spread_end(stage):
        copies, count, _ = spread(stage)
        for copy in copies:
            copy.wait_recv()
        total = grecv[stage * 4]
        for i in range(1, count):
            total = total + grecv[stage * 4 + i]
        gacc[stage + 1] = total

    spread_start(0)

    lands = ref["lands"]
    p2xs, p2xr, p2ys, p2yr = ref["p2xs"], ref["p2xr"], ref["p2ys"], ref["p2yr"]

    def landing(group, axis, d):
        if axis == 0:
            src, dst = r1x[group], hgg.at[d - 1, :, 0 : CX[group]]
        else:
            src, dst = r1y[group], hgg.at[d - 1, :, 768 : 768 + CY[group]]
        return pltpu.make_async_copy(src.at[d - 1], dst, lands.at[(group * 2 + axis) * 3 + d - 1])

    def send_2(group, axis, d):
        sem = group * 3 + d - 1
        own = pl.multiple_of(place.x * 128, 128)
        if axis == 0:
            src = piece(group, 0, (place.y + d) % 4, own, 128)
            dst = r2.at[d - 1, :, BASE[group] : BASE[group] + CX[group]]
            return remote(src, dst, p2xs.at[sem], p2xr.at[sem], place.ys(d))
        src = piece(group, 1, place.y, pl.multiple_of(((place.x + d) % 4) * 128, 128), 128)
        dst = r2.at[d - 1, :, BASE[group] + CX[group] : BASE[group] + COLS[group]]
        return remote(src, dst, p2ys.at[sem], p2yr.at[sem], place.xs(d))

    def land(group):
        for d in (1, 2, 3):
            for tile in range(4):
                send_x(group, d, tile).wait_recv()
            landing(group, 0, d).start()
        for d in (1, 2, 3):
            send_y(group, d).wait_recv()
            landing(group, 1, d).start()

    def first_sum(group):
        for axis in range(2):
            for d in (1, 2, 3):
                landing(group, axis, d).wait()
            lo = 0 if axis == 0 else 768
            width = CX[group] if axis == 0 else CY[group]

            @pl.loop(0, 4)
            def _(i):
                if axis == 0:
                    own = piece(group, 0, i, pl.multiple_of(place.x * 128, 128), 128)
                else:
                    own = piece(group, 1, place.y, pl.multiple_of(i * 128, 128), 128)
                rows = pl.ds(pl.multiple_of(i * 128, 128), 128)
                total = own[...].astype(F32)
                for d in range(3):
                    total = total + hgg[d, rows, lo : lo + width].astype(F32)
                own[...] = total.astype(BF)

            for d in (1, 2, 3):
                send_2(group, axis, d).start()

    def second_sum(group):
        own = pl.multiple_of(place.x * 128, 128)
        for axis in range(2):
            for d in (1, 2, 3):
                send_2(group, axis, d).wait_recv()
            lo = BASE[group] + (0 if axis == 0 else CX[group])
            width = CX[group] if axis == 0 else CY[group]
            total = piece(group, axis, place.y, own, 128)[...].astype(F32)
            for d in range(3):
                total = total + r2[d, :, lo : lo + width].astype(F32)
            final[:, lo : lo + width] = total

    land(0)
    first_sum(0)
    spread_end(0)
    spread_start(1)
    land(1)
    first_sum(1)
    spread_end(1)
    spread_start(2)
    second_sum(0)
    land(2)
    first_sum(2)
    spread_end(2)
    spread_start(3)
    land(3)
    first_sum(3)
    second_sum(1)
    spread_end(3)
    ref["gains"][...] = gacc[4]
    second_sum(2)
    second_sum(3)

    mine = final.at[pl.ds(pl.multiple_of(place.c * 64, 64), 64)]
    theirs = final.at[pl.ds(pl.multiple_of(other * 64, 64), 64)]
    last = remote(theirs, shares.at[place.c], xs.at[8], xr.at[8], place.core())
    last.start()
    keep = pltpu.make_async_copy(mine, shares.at[place.c], lsem.at[9])
    keep.start()

    for gather in (ag1, agm, ag4):
        gather.done()
    rs4.done()
    rs2.done()
    for group in (0, 2, 3):
        swap_a(group).wait_send()
    for group in (2, 3):
        swap_b(group).wait_send()
    for group in range(4):
        for d in (1, 2, 3):
            for tile in range(4):
                send_x(group, d, tile).wait_send()
            send_y(group, d).wait_send()
            for axis in range(2):
                send_2(group, axis, d).wait_send()
    for stage in range(4):
        for copy in spread(stage)[0]:
            copy.wait_send()
    out_copy.wait()
    tok_copy.wait()
    keep.wait()
    last.wait()


def block(tokens, gain_attn, w_qkv, w_out, gain_mlp, w_gate_up, w_down, cotangent, lengths):
    cos_t, sin_t = rotary_tables()
    vmem = pl.BlockSpec(memory_space=pltpu.VMEM)
    smem = pl.BlockSpec(memory_space=pltpu.SMEM)
    hbm = pl.BlockSpec(memory_space=pl.ANY)
    ins = [
        ("tok", tokens, vmem),
        ("gain1", gain_attn.reshape(1, D), vmem),
        ("wq_h", w_qkv, hbm),
        ("wo_h", w_out, hbm),
        ("gain2", gain_mlp.reshape(1, D), vmem),
        ("wgu_h", w_gate_up, hbm),
        ("wd_h", w_down, hbm),
        ("cot", cotangent, vmem),
        ("lengths", lengths, smem),
        ("cos", jnp.asarray(cos_t), vmem),
        ("sin", jnp.asarray(sin_t), vmem),
    ]
    outs = [
        ("output", (ROWS, D), F32, hbm),
        ("grad_tokens", (ROWS, D), F32, hbm),
        ("gains", (8, 512), F32, vmem),
        ("shares", (2, 64, ALL), F32, hbm),
        ("xa", (4, SEQ, D), BF, hbm),
    ]
    outs += [(f"xb{g}", (SEQ, COLS[g]), BF, hbm) for g in range(4)]
    outs += [(f"r1x{g}", (3, SEQ, CX[g]), BF, hbm) for g in range(4)]
    outs += [(f"r1y{g}", (3, SEQ, CY[g]), BF, hbm) for g in range(4)]
    dma = pltpu.SemaphoreType.DMA
    scratch = [
        ("wq", pltpu.VMEM((3, D, 512), BF)),
        ("wo", pltpu.VMEM((512, D), BF)),
        ("wgu", pltpu.VMEM((2, D, FF), BF)),
        ("wd", pltpu.VMEM((FF, D), BF)),
        ("attn", pltpu.VMEM((SEQ, D), BF)),
        ("qkv", pltpu.VMEM((SEQ, 1536), BF)),
        ("probs", pltpu.VMEM((HEADS, SEQ, SEQ), BF)),
        ("ctx", pltpu.VMEM((SEQ, 512), BF)),
        ("middle", pltpu.VMEM((ROWS, D), F32)),
        ("mlp", pltpu.VMEM((SEQ, D), BF)),
        ("masked", pltpu.VMEM((SEQ, D), BF)),
        ("branch", pltpu.VMEM((SEQ, D), BF)),
        ("hgg", pltpu.VMEM((3, SEQ, FF), BF)),
        ("gctx", pltpu.VMEM((SEQ, 512), BF)),
        ("gproj", pltpu.VMEM((SEQ, 1536), BF)),
        ("gmid", pltpu.VMEM((ROWS, D), F32)),
        ("pa", pltpu.VMEM((SEQ, D), BF)),
        ("relay_a", pltpu.VMEM((2, 64, D), BF)),
        ("recv_a", pltpu.VMEM((2, ROWS, D), BF)),
        ("pb", pltpu.VMEM((SEQ, D), BF)),
        ("relay_b", pltpu.VMEM((2, 64, D), BF)),
        ("recv_b", pltpu.VMEM((2, ROWS, D), BF)),
        ("r2", pltpu.VMEM((3, ROWS, ALL), BF)),
        ("final", pltpu.VMEM((ROWS, ALL), F32)),
        ("gacc", pltpu.VMEM((5, 8, 512), F32)),
        ("grecv", pltpu.VMEM((14, 8, 512), F32)),
        ("zs", dma((8, 6))),
        ("zr", dma((8, 6))),
        ("lsem", dma((10,))),
        ("osem", dma((8,))),
        ("xs", dma((9,))),
        ("xr", dma((9,))),
        ("p1xs", dma((48,))),
        ("p1xr", dma((48,))),
        ("p1ys", dma((12,))),
        ("p1yr", dma((12,))),
        ("p2xs", dma((12,))),
        ("p2xr", dma((12,))),
        ("p2ys", dma((12,))),
        ("p2yr", dma((12,))),
        ("lands", dma((24,))),
        ("gs", dma((10,))),
        ("gr", dma((10,))),
    ]
    names = [i[0] for i in ins] + [o[0] for o in outs] + [s[0] for s in scratch]
    results = pl.pallas_call(
        functools.partial(kernel, names),
        out_shape=[jax.ShapeDtypeStruct(o[1], o[2]) for o in outs],
        in_specs=[i[2] for i in ins],
        out_specs=[o[3] for o in outs],
        scratch_shapes=[s[1] for s in scratch],
        compiler_params=pltpu.CompilerParams(
            collective_id=0, has_side_effects=True, vmem_limit_bytes=63 * 1024 * 1024
        ),
        name="block",
    )(*[i[1] for i in ins])
    output, grad_tokens, gains, shares = results[:4]
    gains = gains.reshape(2, D)
    b = BASE
    down = jnp.concatenate([shares[0, :, 0:768], shares[1, :, 128:768]], axis=1)
    gate_up = shares[:, :, b[1] : b[1] + FF]
    out = jnp.concatenate([shares[0, :, b[2] : b[2] + 256], shares[1, :, b[2] : b[2] + 256]], axis=1)
    qkv = jnp.concatenate([shares[0, :, b[3] :], shares[1, :, b[3] :]], axis=1)
    return (
        output,
        grad_tokens,
        gains[0],
        qkv.reshape(64, 3, 512).transpose(1, 0, 2),
        out.T,
        gains[1],
        gate_up,
        down.T,
    )


def solution(mesh):
    placed = (
        P(("dp", "tensor"), None),
        P(),
        P(None, None, "tensor"),
        P("tensor", None),
        P(),
        P(None, None, "tensor"),
        P("tensor", None),
        P(("dp", "tensor"), None),
        P("dp"),
    )
    return jax.shard_map(
        block,
        mesh=mesh,
        in_specs=placed,
        out_specs=(
            P(("dp", "tensor"), None),
            P(("dp", "tensor"), None),
            P(),
            P(None, "dp", "tensor"),
            P("tensor", "dp"),
            P(),
            P(None, "dp", "tensor"),
            P("tensor", "dp"),
        ),
        check_vma=False,
    )
```

```python
import functools
import math

import jax
import jax.numpy as jnp
import numpy as np
from jax import lax
from jax.experimental import pallas as pl
from jax.experimental.pallas import tpu as pltpu
from jax.sharding import PartitionSpec as P

D = 2048
HD = 128
FF = 1408
ROWS = 128
SEQ = 512
HEADS = 4
EPS = 1e-05
BF = jnp.bfloat16
F32 = jnp.float32
MESH = pl.DeviceIdType.MESH
OFFS = (0, 3, 1, 2)
ORDER = ((0, 0), (0, 1), (1, 0), (2, 1), (1, 1), (2, 0), (3, 0), (3, 1))
UNIT = {half: i * 64 for i, half in enumerate(ORDER)}

CX = (384, 768, 128, 384)
CY = (384, 640, 128, 384)
COLS = tuple(a + b for a, b in zip(CX, CY))
BASE = (0, 768, 2176, 2432)
ALL = 3200


def nn(a, b):
    return lax.dot_general(a, b, (((1,), (0,)), ((), ())), preferred_element_type=F32)


def nt(a, b):
    return lax.dot_general(a, b, (((1,), (1,)), ((), ())), preferred_element_type=F32)


def tn(a, b):
    return lax.dot_general(a, b, (((0,), (0,)), ((), ())), preferred_element_type=F32)


def rotary_tables():
    half = HD // 2
    freq = np.exp(np.arange(half, dtype=np.float64) * (-2.0 * math.log(10000.0) / HD))
    angles = np.arange(SEQ, dtype=np.float64)[:, None] * freq
    cos, sin = np.cos(angles), np.sin(angles)
    return (
        np.concatenate([cos, cos], axis=1).astype(np.float32),
        np.concatenate([-sin, sin], axis=1).astype(np.float32),
    )


class Place:
    def __init__(self):
        self.dp = lax.axis_index("dp")
        self.t = lax.axis_index("tensor")
        self.c = self.dp % 2
        self.x = (self.dp // 2) % 4
        self.y = self.dp // 8

    def z(self, d):
        return (self.dp, (self.t + d) % 4)

    def xs(self, d):
        return (self.y * 8 + ((self.x + d) % 4) * 2 + self.c, self.t)

    def ys(self, d):
        return (((self.y + d) % 4) * 8 + self.x * 2 + self.c, self.t)

    def core(self):
        return (self.dp + 1 - 2 * self.c, self.t)


def remote(src, dst, ssem, rsem, device):
    return pltpu.make_async_remote_copy(
        src_ref=src, dst_ref=dst, send_sem=ssem, recv_sem=rsem, device_id=device, device_id_type=MESH
    )


def half_rows(place, slot, half):
    block = (place.t + OFFS[slot]) % 4
    return pl.ds(pl.multiple_of(block * 128 + half * 64, 64), 64)


def in_order(place, ref, cols):
    return jnp.concatenate([ref[half_rows(place, *half), cols] for half in ORDER], axis=0)


class Gather:
    def __init__(self, place, buf, ssem, rsem, relative):
        self.place, self.buf, self.ssem, self.rsem, self.relative = place, buf, ssem, rsem, relative

    def row(self, slot, half):
        if self.relative:
            return pl.ds(UNIT[slot, half], 64)
        return half_rows(self.place, slot, half)

    def copy(self, k):
        slot, half, to, there = (
            (0, 0, 1, 1),
            (0, 1, 1, 1),
            (0, 1, -1, 2),
            (0, 0, -1, 2),
            (1, 0, 1, 3),
            (2, 1, -1, 3),
        )[k]
        src = self.buf.at[self.row(slot, half)]
        dst = self.buf.at[self.row(there, half)] if self.relative else src
        return remote(src, dst, self.ssem.at[k], self.rsem.at[k], self.place.z(to))

    def start(self):
        for k in (0, 2, 1, 3):
            self.copy(k).start()

    def relay(self):
        self.copy(0).wait_recv()
        self.copy(4).start()
        self.copy(2).wait_recv()
        self.copy(5).start()

    def near(self):
        self.copy(1).wait_recv()
        self.copy(3).wait_recv()

    def far(self):
        self.copy(4).wait_recv()
        self.copy(5).wait_recv()

    def done(self):
        for k in range(6):
            self.copy(k).wait_send()


class Scatter:
    def __init__(self, place, part, relays, recv, ssem, rsem):
        self.place, self.part, self.relays, self.recv = place, part, relays, recv
        self.ssem, self.rsem = ssem, rsem

    def rows(self, slot, half):
        return pl.ds(UNIT[slot, half], 64)

    def copy(self, k, n):
        part, relays, recv = self.part, self.relays, self.recv
        cols = pl.ds(pl.multiple_of(n * 512, 512), 512)
        src, dst, to = (
            (part.at[self.rows(3, 0), cols], relays.at[0, :, cols], 1),
            (part.at[self.rows(2, 1), cols], recv.at[0, self.rows(0, 1), cols], 1),
            (part.at[self.rows(3, 1), cols], relays.at[1, :, cols], -1),
            (part.at[self.rows(1, 0), cols], recv.at[1, self.rows(0, 0), cols], -1),
            (part.at[self.rows(2, 0), cols], recv.at[0, self.rows(0, 0), cols], 1),
            (part.at[self.rows(1, 1), cols], recv.at[1, self.rows(0, 1), cols], -1),
        )[k]
        sem = k * 4 + n
        return remote(src, dst, self.ssem.at[sem], self.rsem.at[sem], self.place.z(to))

    def start(self, n, *which):
        for k in which:
            self.copy(k, n).start()

    def relay(self, first, last):
        @pl.loop(first, last)
        def _(n):
            cols = pl.ds(pl.multiple_of(n * 512, 512), 512)
            for index, slot, half, out in ((0, 2, 0, 4), (1, 1, 1, 5)):
                self.copy(2 * index, n).wait_recv()
                rows = self.rows(slot, half)
                total = self.part[rows, cols].astype(F32) + self.relays[index, :, cols].astype(F32)
                self.part[rows, cols] = total.astype(BF)
                self.copy(out, n).start()

    def finish(self):
        @pl.loop(0, 4)
        def _(n):
            for k in (1, 3, 4, 5):
                self.copy(k, n).wait_recv()

    def total(self, rows):
        return (
            self.part[rows, :].astype(F32)
            + self.recv[0, rows, :].astype(F32)
            + self.recv[1, rows, :].astype(F32)
        )

    def done(self):
        @pl.loop(0, 4)
        def _(n):
            for k in range(6):
                self.copy(k, n).wait_send()


def sixteen(r):
    return pl.ds(pl.multiple_of(r * 16, 16), 16)


def own_rows(place, r):
    return pl.ds(pl.multiple_of(place.t * 128 + r * 16, 16), 16)


def kernel(names, *refs):
    ref = dict(zip(names, refs))
    place = Place()
    tok, cot, live = ref["tok"], ref["cot"], ref["lengths"]
    wq, wo, wgu, wd = ref["wq"], ref["wo"], ref["wgu"], ref["wd"]
    attn, qkv, probs, ctx = ref["attn"], ref["qkv"], ref["probs"], ref["ctx"]
    middle, mlp, masked, branch = ref["middle"], ref["mlp"], ref["masked"], ref["branch"]
    hid, ggu, gctx, gproj, gmid = ref["hid"], ref["ggu"], ref["gctx"], ref["qkv"], ref["gmid"]
    cos_t, sin_t, gain1, gain2 = ref["cos"], ref["sin"], ref["gain1"], ref["gain2"]
    xa, xa0, xb0, xb1, xb2 = ref["xa"], ref["xa0"], ref["xb0"], ref["xb1"], ref["xb2"]
    relx, rely = [ref[f"relx{g}"] for g in range(4)], [ref[f"rely{g}"] for g in range(4)]
    recx, recy = [ref[f"recx{g}"] for g in range(4)], [ref[f"recy{g}"] for g in range(4)]
    r2, final, shares = ref["r2"], ref["final"], ref["shares"]
    gacc, grecv, gsum = ref["gacc"], ref["grecv"], ref["gsum"]
    zs, zr, lsem = ref["zs"], ref["zr"], ref["lsem"]
    live_rows = live[0]

    cot_load = pltpu.make_async_copy(cot, masked.at[0:ROWS], lsem.at[7])
    cot_load.start()

    loads = [pltpu.make_async_copy(ref["wq_h"].at[j], wq.at[:, j * 512 : (j + 1) * 512], lsem.at[j]) for j in range(3)]
    loads.append(pltpu.make_async_copy(ref["wo_h"], wo, lsem.at[3]))
    loads += [pltpu.make_async_copy(ref["wgu_h"].at[j], wgu.at[:, j * FF : (j + 1) * FF], lsem.at[4 + j]) for j in range(2)]
    loads.append(pltpu.make_async_copy(ref["wd_h"], wd, lsem.at[6]))
    for load in loads:
        load.start()

    barrier = pltpu.get_barrier_semaphore()
    partners = [place.z(d) for d in (1, 2, 3)]
    partners += [place.xs(d) for d in (1, 2, 3)] + [place.ys(d) for d in (1, 2, 3)] + [place.core()]
    for device in partners:
        pl.semaphore_signal(barrier, inc=1, device_id=device, device_id_type=MESH)

    @pl.loop(0, 8)
    def _(r):
        v = tok[sixteen(r), :].astype(F32)
        inv = lax.rsqrt(jnp.mean(v * v, axis=-1, keepdims=True) + EPS)
        attn[own_rows(place, r), :] = (v * inv * gain1[...]).astype(BF)

    pl.semaphore_wait(barrier, len(partners))

    ag1 = Gather(place, attn, zs.at[0], zr.at[0], False)
    agm = Gather(place, masked, zs.at[1], zr.at[1], True)
    ag2 = Gather(place, mlp, zs.at[2], zr.at[2], True)
    ag4 = Gather(place, branch, zs.at[3], zr.at[3], False)
    rs1 = Scatter(place, ref["pa"], ref["relay_a"], ref["recv_a"], zs.at[4], zr.at[4])
    rs3 = Scatter(place, ref["pa"], ref["relay_a"], ref["recv_a"], zs.at[5], zr.at[5])
    rs4 = Scatter(place, ref["pa"], ref["relay_a"], ref["recv_a"], zs.at[6], zr.at[6])
    rs2 = Scatter(place, ref["pb"], ref["relay_b"], ref["recv_b"], zs.at[7], zr.at[7])

    ag1.start()

    cot_load.wait()

    @pl.loop(0, 8)
    def _(r):
        at = place.t * ROWS + r * 16 + lax.broadcasted_iota(jnp.int32, (16, 1), 0)
        v = masked[sixteen(r), :].astype(F32)
        masked[sixteen(r), :] = jnp.where(at < live_rows, v, 0.0).astype(BF)

    def project(slot):
        block = (place.t + OFFS[slot]) % 4
        rows = pl.ds(pl.multiple_of(block * 128, 128), 128)
        for j in range(3):
            p = nn(attn[rows, :], wq[:, j * 512 : (j + 1) * 512])
            if j == 2:
                qkv[rows, 1024:1536] = p.astype(BF)
                continue
            for h in range(HEADS):
                v = p[:, h * HD : (h + 1) * HD]
                v = v * cos_t[rows, :] + pltpu.roll(v, 64, 1) * sin_t[rows, :]
                if j == 0:
                    v = v * HD ** (-0.5)
                qkv[rows, j * 512 + h * HD : j * 512 + (h + 1) * HD] = v.astype(BF)

    for load in loads[:3]:
        load.wait()
    project(0)
    ag1.relay()
    ag1.near()
    agm.start()
    project(1)
    project(2)
    ag1.far()
    project(3)

    @pl.loop(0, HEADS)
    def _(h):
        def cols(j):
            return pl.ds(pl.multiple_of(j * 512 + h * HD, HD), HD)

        for q in range(2):
            rows, keys = pl.ds(q * 256, 256), (q + 1) * 256
            scores = nt(qkv[rows, cols(0)], qkv[0:keys, cols(1)])
            at = q * 256 + lax.broadcasted_iota(jnp.int32, (256, keys), 0)
            key = lax.broadcasted_iota(jnp.int32, (256, keys), 1)
            scores = jnp.where((key <= at) & (key < live_rows), scores, -1e30)
            e = jnp.exp(scores - jnp.max(scores, axis=-1, keepdims=True))
            p = (e * (1.0 / jnp.sum(e, axis=-1, keepdims=True))).astype(BF)
            probs[h, rows, 0:keys] = p
            ctx[rows, cols(0)] = nn(p, qkv[0:keys, cols(2)]).astype(BF)

    loads[3].wait()

    @pl.loop(0, 4)
    def _(n):
        at = pl.ds(pl.multiple_of(n * 512, 512), 512)
        rs1.part[:, at] = nn(in_order(place, ctx, slice(None)), wo[:, at]).astype(BF)
        rs1.start(n, 0, 2, 1, 3)

    other = 1 - place.c
    xs, xr = ref["xs"], ref["xr"]

    def swap_a(group):
        src = (masked, mlp, branch, attn)[group]
        return remote(src, xa.at[group], xs.at[group], xr.at[group], place.core())

    def swap_masked(part):
        rows = (slice(0, 384), slice(384, 512))[part]
        sem = (0, 14)[part]
        return remote(masked.at[rows], xa0.at[rows], xs.at[sem], xr.at[sem], place.core())

    def swap_b(k):
        rows = pl.ds((0, 256, 0, 256, 0, 0)[k], 256 if k < 4 else 512)
        if k < 2:
            src = hid.at[rows, pl.ds(pl.multiple_of(other * 640, 128), 768)]
        elif k < 4:
            src = ggu.at[rows, pl.ds(pl.multiple_of(other * FF, 128), FF)]
        elif k == 4:
            src = ctx.at[rows, pl.ds(pl.multiple_of(other * 256, 256), 256)]
        else:
            src = gproj.at[rows, pl.ds(pl.multiple_of(other * 768, 256), 768)]
        dst = (xb0, xb0, xb1, xb1, xb2, xb0)[k].at[rows]
        return remote(src, dst, xs.at[4 + k], xr.at[4 + k], place.core())

    swap_a(3).start()
    swap_b(4).start()

    rs1.relay(0, 4)
    rs1.finish()

    @pl.loop(0, 8)
    def _(r):
        rows = sixteen(r)
        v = tok[rows, :].astype(F32) + rs1.total(rows)
        middle[rows, :] = v
        inv = lax.rsqrt(jnp.mean(v * v, axis=-1, keepdims=True) + EPS)
        mlp[rows, :] = (v * inv * gain2[...]).astype(BF)

    rs1.done()
    ag2.start()
    for load in loads[4:]:
        load.wait()

    own_b = (
        hid.at[:, pl.ds(pl.multiple_of(place.c * 640, 128), 768)],
        ggu.at[:, pl.ds(pl.multiple_of(place.c * FF, 128), FF)],
        ctx.at[:, pl.ds(pl.multiple_of(place.c * 256, 256), 256)],
        gproj.at[:, pl.ds(pl.multiple_of(place.c * 768, 256), 768)],
    )
    own_a = (masked, mlp, branch, attn)
    other_a = (xa0, ref["pb"], wd.at[0:512], wd.at[512:1024])
    other_b = (xb0, xb1, xb2, xb0)
    osem = ref["osem"]

    def bring(group):
        return pltpu.make_async_copy(xa.at[group], other_a[group], osem.at[group])

    def fetch(group):
        swap_a(group).wait_recv()
        bring(group).start()

    def piece(group, axis, tile, first, count):
        if group == 3 and axis == 1:
            return mlp.at[pl.ds(first, count), pl.ds(pl.multiple_of(tile * 384, 128), 384)]
        base = (FF, 0, FF + 768, FF + 1024)[group]
        lo = base if axis == 0 else base + CX[group]
        width = CX[group] if axis == 0 else CY[group]
        rows = pl.ds(pl.multiple_of(tile * 512 + first, min(count, 128)), count)
        return wgu.at[rows, lo : lo + width]

    p1xs, p1xr, p1ys, p1yr = ref["p1xs"], ref["p1xr"], ref["p1ys"], ref["p1yr"]

    def send_x(group, kind, tile):
        to = 1 - 2 * (tile // 2)
        rows = pl.ds(pl.multiple_of(tile * 128, 128), 128)
        if kind == 0:
            block, dst = place.x + 2, relx[group].at[rows]
        elif kind == 1:
            block, dst, to = place.x + 4 - to, recx[group].at[(1 + to) // 2, rows], -to
        else:
            block, dst = place.x + 4 + to, recx[group].at[(1 - to) // 2, rows]
        src = piece(group, 0, tile, pl.multiple_of((block % 4) * 128, 128), 128)
        sem = (group * 3 + kind) * 4 + tile
        return remote(src, dst, p1xs.at[sem], p1xr.at[sem], place.xs(4 + to))

    def send_y(group, k):
        offset, first, dst, to = (
            (2, 0, rely[group].at[0:256], 1),
            (1, 256, recy[group].at[0, 256:512], 1),
            (2, 256, rely[group].at[256:512], 3),
            (3, 0, recy[group].at[1, 0:256], 3),
            (1, 0, recy[group].at[0, 0:256], 1),
            (3, 256, recy[group].at[1, 256:512], 3),
        )[k]
        src = piece(group, 1, (place.y + offset) % 4, first, 256)
        return remote(src, dst, p1ys.at[group * 6 + k], p1yr.at[group * 6 + k], place.ys(to))

    def gradient(group, step):
        tile = (place.y + jnp.where(step == 0, 2, jnp.where(step == 1, 1, jnp.where(step == 2, 3, 0)))) % 4
        at = pl.ds(pl.multiple_of(tile * 512, 512), 512)
        lo = 0
        for axis, width in ((0, CX[group]), (1, CY[group])):
            own, oth = own_b[group].at[:, lo : lo + width], other_b[group].at[:, lo : lo + width]
            out = tn(own_a[group][:, at], own[...]) + tn(other_a[group][:, at], oth[...])
            piece(group, axis, tile, 0, 512)[...] = out.astype(BF)
            lo += width
        send_x(group, 0, tile).start()
        send_x(group, 1, tile).start()
        for k, when in ((0, 0), (2, 0), (1, 1), (3, 2)):

            @pl.when(step == when)
            def _():
                send_y(group, k).start()

    lands = ref["lands"]

    def mid_copies(group):
        return (
            pltpu.make_async_copy(relx[group], hid.at[:, 0 : CX[group]], lands.at[16 + group]),
            pltpu.make_async_copy(rely[group], hid.at[:, 768 : 768 + CY[group]], lands.at[20 + group]),
        )

    def mid_start(group):
        for tile in range(4):
            send_x(group, 0, tile).wait_recv()
        for k in (0, 2):
            send_y(group, k).wait_recv()
        for copy in mid_copies(group):
            copy.start()

    def mid_end(group):
        for copy in mid_copies(group):
            copy.wait()

        def add(axis, tile, first, rows, lo, width, count):
            @pl.loop(0, count // 32)
            def _(i):
                own = piece(group, axis, tile, pl.multiple_of(first + i * 32, 32), 32)
                got = hid[pl.ds(pl.multiple_of(rows + i * 32, 32), 32), lo : lo + width]
                own[...] = (own[...].astype(F32) + got.astype(F32)).astype(BF)

        for tile in range(4):
            to = 1 if tile < 2 else 3
            add(0, tile, ((place.x + to) % 4) * 128, tile * 128, 0, CX[group], 128)
            send_x(group, 2, tile).start()
        for k, offset, first in ((4, 1, 0), (5, 3, 256)):
            add(1, (place.y + offset) % 4, first, first, 768, CY[group], 256)
            send_y(group, k).start()

    def feed(first, count):
        rows = slice(first, first + count)
        for n0, n1 in ((0, 512), (512, 1024), (1024, 1408)):
            gate = nn(mlp[rows, :], wgu[:, n0:n1])
            up = nn(mlp[rows, :], wgu[:, FF + n0 : FF + n1])
            sig = jax.nn.sigmoid(gate)
            silu = gate * sig
            hid[rows, n0:n1] = (silu * up).astype(BF)
            ggu[rows, n0:n1] = (up * sig * (1.0 + gate * (1.0 - sig))).astype(BF)
            ggu[rows, FF + n0 : FF + n1] = silu.astype(BF)

    def feed_back(first, count, *sends):
        rows = slice(first, first + count)
        for n0, n1 in ((0, 512), (512, 1024), (1024, 1408)):
            grad = nt(masked[rows, :], wd[n0:n1, :])
            for lo in (0, FF):
                ggu[rows, lo + n0 : lo + n1] = (grad * ggu[rows, lo + n0 : lo + n1].astype(F32)).astype(BF)

        @pl.loop(0, 4)
        def _(n):
            at = pl.ds(pl.multiple_of(n * 512, 512), 512)
            rs3.part[rows, at] = nt(ggu[rows, :], wgu[at, :]).astype(BF)
            rs3.start(n, *sends)

    feed(0, 128)
    feed_back(0, 128)
    ag2.relay()
    agm.near()
    agm.relay()
    swap_masked(0).start()
    feed(128, 128)
    feed_back(128, 128, 1, 3)
    swap_b(0).start()
    swap_b(2).start()
    ag2.near()
    ag2.far()
    swap_a(1).start()
    feed(256, 256)
    swap_b(1).start()
    agm.far()
    swap_masked(1).start()
    feed_back(256, 256, 0, 2)
    swap_b(3).start()
    fetch(1)

    p2xs, p2xr, p2ys, p2yr = ref["p2xs"], ref["p2xr"], ref["p2ys"], ref["p2yr"]

    def landing(group):
        copies = []
        for d in range(2):
            for axis, src in ((0, recx[group]), (1, recy[group])):
                lo = d * FF + axis * 768
                width = CX[group] if axis == 0 else CY[group]
                sem = lands.at[group * 4 + d * 2 + axis]
                copies.append(pltpu.make_async_copy(src.at[d], ggu.at[:, lo : lo + width], sem))
        return copies

    def send_2(group, axis, d):
        sem = group * 3 + d - 1
        own = pl.multiple_of(place.x * 128, 128)
        if axis == 0:
            src = piece(group, 0, (place.y + d) % 4, own, 128)
            dst = r2.at[d - 1, :, BASE[group] : BASE[group] + CX[group]]
            return remote(src, dst, p2xs.at[sem], p2xr.at[sem], place.ys(d))
        src = piece(group, 1, place.y, pl.multiple_of(((place.x + d) % 4) * 128, 128), 128)
        dst = r2.at[d - 1, :, BASE[group] + CX[group] : BASE[group] + COLS[group]]
        return remote(src, dst, p2ys.at[sem], p2yr.at[sem], place.xs(d))

    def land(group):
        for tile in range(4):
            for kind in (1, 2):
                send_x(group, kind, tile).wait_recv()
        for k in (1, 3, 4, 5):
            send_y(group, k).wait_recv()
        for copy in landing(group):
            copy.start()

    def first_sum(group):
        for copy in landing(group):
            copy.wait()
        for axis in range(2):
            lo = axis * 768
            width = CX[group] if axis == 0 else CY[group]

            @pl.loop(0, 16)
            def _(i):
                if axis == 0:
                    own = piece(group, 0, i // 4, pl.multiple_of(place.x * 128 + (i % 4) * 32, 32), 32)
                else:
                    own = piece(group, 1, place.y, pl.multiple_of(i * 32, 32), 32)
                rows = pl.ds(pl.multiple_of(i * 32, 32), 32)
                total = own[...].astype(F32)
                for d in range(2):
                    total = total + ggu[rows, d * FF + lo : d * FF + lo + width].astype(F32)
                own[...] = total.astype(BF)

            for d in (2, 1, 3):
                send_2(group, axis, d).start()

    def whole_of(group):
        return ((final, 0), (middle, 0), (final, 768), (final, 1024))[group]

    def ending(group):
        ref_at, first = whole_of(group)
        cols = slice(first, first + COLS[group])
        mine = ref_at.at[pl.ds(pl.multiple_of(place.c * 64, 64), 64), cols]
        theirs = ref_at.at[pl.ds(pl.multiple_of(other * 64, 64), 64), cols]
        dst = shares.at[place.c, :, BASE[group] : BASE[group] + COLS[group]]
        return (
            remote(theirs, dst, xs.at[10 + group], xr.at[10 + group], place.core()),
            pltpu.make_async_copy(mine, dst, lsem.at[9 + group]),
        )

    def second_sum(group):
        for axis in range(2):
            for d in (1, 2, 3):
                send_2(group, axis, d).wait_recv()
            lo = BASE[group] + (0 if axis == 0 else CX[group])
            width = CX[group] if axis == 0 else CY[group]
            whole, first = whole_of(group)
            first += lo - BASE[group]

            @pl.loop(0, 4)
            def _(i):
                rows = pl.ds(pl.multiple_of(i * 32, 32), 32)
                own = piece(group, axis, place.y, pl.multiple_of(place.x * 128 + i * 32, 32), 32)
                total = own[...].astype(F32)
                for d in range(3):
                    total = total + r2[d, rows, lo : lo + width].astype(F32)
                whole[rows, first : first + width] = total
        for copy in ending(group):
            copy.start()

    swap_b(0).wait_recv()
    swap_b(1).wait_recv()
    swap_masked(0).wait_recv()
    swap_masked(1).wait_recv()

    @pl.loop(0, 2)
    def _(step):
        gradient(0, step)

    rs3.relay(0, 2)

    @pl.loop(2, 4)
    def _(step):
        gradient(0, step)

    rs3.relay(2, 4)
    bring(1).wait()
    swap_b(2).wait_recv()
    swap_b(3).wait_recv()

    @pl.loop(0, 2)
    def _(step):
        gradient(1, step)

    rs3.finish()

    def fold(v):
        return jnp.concatenate([v[:, i * 512 : (i + 1) * 512] for i in range(4)], axis=0)

    def mlp_back(r, total):
        rows = sixteen(r)
        grad = rs3.total(rows)
        v = middle[rows, :]
        inv = lax.rsqrt(jnp.mean(v * v, axis=-1, keepdims=True) + EPS)
        scaled = grad * gain2[...]
        back = (
            masked[rows, :].astype(F32)
            + inv * scaled
            - v * (inv * inv * inv) * jnp.mean(v * scaled, axis=-1, keepdims=True)
        )
        gmid[rows, :] = back
        branch[own_rows(place, r), :] = back.astype(BF)
        return total + jnp.sum(grad * v * inv, axis=0, keepdims=True)

    gain2_part = lax.fori_loop(0, 8, mlp_back, jnp.zeros((1, D), F32))
    gacc[0, 4:8, :] = fold(gain2_part)
    ag4.start()
    rs3.done()

    @pl.loop(2, 4)
    def _(step):
        gradient(1, step)

    @pl.loop(0, 4)
    def _(n):
        at = pl.ds(pl.multiple_of(n * 512, 512), 512)
        rs2.part[:, at] = nn(hid[...], wd[:, at]).astype(BF)

    fetch(3)
    for k in (0, 1, 2, 3):
        swap_b(k).wait_send()
    mid_start(0)
    ag4.relay()

    @pl.loop(0, 4)
    def _(n):
        rs2.start(n, 0, 2, 1, 3)

    mid_end(0)
    mid_start(1)
    mid_end(1)
    ag4.near()
    ag4.far()
    swap_a(2).start()

    @pl.loop(0, 2)
    def _(n):
        at = pl.ds(pl.multiple_of(n * 256, 256), 256)
        gctx[:, at] = nt(branch[...], wo[at, :]).astype(BF)


    def turn_back(v, rows):
        return v * cos_t[rows, :] - pltpu.roll(v, 64, 1) * sin_t[rows, :]

    @pl.loop(0, HEADS)
    def _(h):
        def cols(j):
            return pl.ds(pl.multiple_of(j * 512 + h * HD, HD), HD)

        def part(q):
            rows, keys = pl.ds(q * 256, 256), (q + 1) * 256
            p = probs[h, rows, 0:keys]
            grad = gctx[rows, cols(0)]
            wide = p.astype(F32)
            gp = nt(grad, qkv[0:keys, cols(2)])
            gs = (wide * (gp - jnp.sum(wide * gp, axis=-1, keepdims=True))).astype(BF)
            gq = (turn_back(nn(gs, qkv[0:keys, cols(1)]), rows) * HD ** (-0.5)).astype(BF)
            return gq, tn(gs, qkv[rows, cols(0)]), tn(p, grad)

        q1, k1, v1 = part(1)
        q0, k0, v0 = part(0)
        lo, hi = slice(0, 256), slice(256, 512)
        k0, k1 = turn_back(k0 + k1[lo], lo).astype(BF), turn_back(k1[hi], hi).astype(BF)
        v0, v1 = (v0 + v1[lo]).astype(BF), v1[hi].astype(BF)
        for j, low, high in ((0, q0, q1), (1, k0, k1), (2, v0, v1)):
            gproj[lo, cols(j)] = low
            gproj[hi, cols(j)] = high

    fetch(2)
    swap_b(5).start()

    def attn_part(n):
        at = pl.ds(pl.multiple_of(n * 512, 512), 512)
        part = nt(in_order(place, gproj, slice(None)), wq[at, :])
        rs4.part[:, at] = part.astype(BF)
        rs4.start(n, 0, 2, 1, 3)
        seen = jnp.sum(part * in_order(place, attn, at).astype(F32), axis=0, keepdims=True)
        gsum[n] = jnp.broadcast_to(seen, (8, 512))

    @pl.loop(0, 2)
    def _(n):
        attn_part(n)

    rs2.relay(0, 4)
    land(0)
    first_sum(0)
    swap_a(1).wait_send()
    ag2.done()
    bring(3).wait()
    swap_b(5).wait_recv()

    @pl.loop(0, 4)
    def _(step):
        gradient(3, step)

    @pl.loop(2, 4)
    def _(n):
        attn_part(n)

    for n in range(4):
        at = slice(n * 512, (n + 1) * 512)
        gacc[0, n : n + 1, :] = gsum[n, 0:1, :] / gain1[:, at]
    gs, gr = ref["gs"], ref["gr"]

    def spread(stage):
        count = 2 if stage == 3 else 4
        me = (place.t, place.x, place.y, place.c)[stage]
        out = []
        for d in range(1, count):
            device = (place.z, place.xs, place.ys, lambda _: place.core())[stage](d)
            k = stage * 3 + d - 1
            out.append(remote(gacc.at[stage], grecv.at[stage * 4 + me], gs.at[k], gr.at[k], device))
        return out, count, me

    def spread_start(stage):
        copies, _, me = spread(stage)
        grecv[stage * 4 + me] = gacc[stage]
        for copy in copies:
            copy.start()

    def spread_end(stage):
        copies, count, _ = spread(stage)
        for copy in copies:
            copy.wait_recv()
        total = grecv[stage * 4]
        for i in range(1, count):
            total = total + grecv[stage * 4 + i]
        gacc[stage + 1] = total

    spread_start(0)
    swap_b(4).wait_recv()
    bring(2).wait()

    @pl.loop(0, 4)
    def _(step):
        gradient(2, step)

    land(1)
    first_sum(1)
    rs4.relay(0, 4)
    rs2.finish()

    @pl.loop(0, 8)
    def _(r):
        rows = sixteen(r)
        middle[rows, :] = middle[rows, :] + rs2.total(rows)

    out_copy = pltpu.make_async_copy(middle, ref["output"], lsem.at[7])
    out_copy.start()
    mid_start(3)
    spread_end(0)
    spread_start(1)
    mid_end(3)
    mid_start(2)
    second_sum(0)
    mid_end(2)
    spread_end(1)
    spread_start(2)
    land(3)
    first_sum(3)
    land(2)
    first_sum(2)
    out_copy.wait()
    second_sum(1)
    spread_end(2)
    spread_start(3)
    rs4.finish()

    @pl.loop(0, 8)
    def _(r):
        rows = sixteen(r)
        grad = rs4.total(rows)
        v = tok[rows, :].astype(F32)
        inv = lax.rsqrt(jnp.mean(v * v, axis=-1, keepdims=True) + EPS)
        scaled = grad * gain1[...]
        gmid[rows, :] = (
            gmid[rows, :]
            + inv * scaled
            - v * (inv * inv * inv) * jnp.mean(v * scaled, axis=-1, keepdims=True)
        )

    tok_copy = pltpu.make_async_copy(gmid, ref["grad_tokens"], lsem.at[8])
    tok_copy.start()
    second_sum(3)
    second_sum(2)
    spread_end(3)
    ref["gains"][...] = gacc[4]

    for gather in (ag1, agm, ag4):
        gather.done()
    rs4.done()
    rs2.done()
    for group in (2, 3):
        swap_a(group).wait_send()
    swap_masked(0).wait_send()
    swap_masked(1).wait_send()
    for k in (4, 5):
        swap_b(k).wait_send()
    for group in range(4):
        for tile in range(4):
            for kind in range(3):
                send_x(group, kind, tile).wait_send()
        for k in range(6):
            send_y(group, k).wait_send()
        for d in (1, 2, 3):
            for axis in range(2):
                send_2(group, axis, d).wait_send()
    for stage in range(4):
        for copy in spread(stage)[0]:
            copy.wait_send()
    tok_copy.wait()
    for group in range(4):
        for copy in ending(group):
            copy.wait()


def block(tokens, gain_attn, w_qkv, w_out, gain_mlp, w_gate_up, w_down, cotangent, lengths):
    cos_t, sin_t = rotary_tables()
    vmem = pl.BlockSpec(memory_space=pltpu.VMEM)
    smem = pl.BlockSpec(memory_space=pltpu.SMEM)
    hbm = pl.BlockSpec(memory_space=pl.ANY)
    ins = [
        ("tok", tokens, vmem),
        ("gain1", gain_attn.reshape(1, D), vmem),
        ("wq_h", w_qkv, hbm),
        ("wo_h", w_out, hbm),
        ("gain2", gain_mlp.reshape(1, D), vmem),
        ("wgu_h", w_gate_up, hbm),
        ("wd_h", w_down, hbm),
        ("cot", cotangent, hbm),
        ("lengths", lengths, smem),
        ("cos", jnp.asarray(cos_t), vmem),
        ("sin", jnp.asarray(sin_t), vmem),
    ]
    outs = [
        ("output", (ROWS, D), F32, hbm),
        ("grad_tokens", (ROWS, D), F32, hbm),
        ("gains", (8, 512), F32, vmem),
        ("shares", (2, 64, ALL), F32, hbm),
        ("xa", (4, SEQ, D), BF, hbm),
    ]
    outs += [(f"relx{g}", (SEQ, CX[g]), BF, hbm) for g in range(4)]
    outs += [(f"rely{g}", (SEQ, CY[g]), BF, hbm) for g in range(4)]
    outs += [(f"recx{g}", (2, SEQ, CX[g]), BF, hbm) for g in range(4)]
    outs += [(f"recy{g}", (2, SEQ, CY[g]), BF, hbm) for g in range(4)]
    dma = pltpu.SemaphoreType.DMA
    scratch = [
        ("wq", pltpu.VMEM((D, 1536), BF)),
        ("wo", pltpu.VMEM((512, D), BF)),
        ("wgu", pltpu.VMEM((D, 2 * FF), BF)),
        ("wd", pltpu.VMEM((FF, D), BF)),
        ("attn", pltpu.VMEM((SEQ, D), BF)),
        ("qkv", pltpu.VMEM((SEQ, 1536), BF)),
        ("probs", pltpu.VMEM((HEADS, SEQ, SEQ), BF)),
        ("ctx", pltpu.VMEM((SEQ, 512), BF)),
        ("middle", pltpu.VMEM((ROWS, D), F32)),
        ("mlp", pltpu.VMEM((SEQ, D), BF)),
        ("masked", pltpu.VMEM((SEQ, D), BF)),
        ("branch", pltpu.VMEM((SEQ, D), BF)),
        ("hid", pltpu.VMEM((SEQ, FF), BF)),
        ("ggu", pltpu.VMEM((SEQ, 2 * FF), BF)),
        ("gctx", pltpu.VMEM((SEQ, 512), BF)),
        ("xa0", pltpu.VMEM((SEQ, D), BF)),
        ("xb0", pltpu.VMEM((SEQ, COLS[0]), BF)),
        ("xb1", pltpu.VMEM((SEQ, COLS[1]), BF)),
        ("xb2", pltpu.VMEM((SEQ, COLS[2]), BF)),
        ("gmid", pltpu.VMEM((ROWS, D), F32)),
        ("pa", pltpu.VMEM((SEQ, D), BF)),
        ("relay_a", pltpu.VMEM((2, 64, D), BF)),
        ("recv_a", pltpu.VMEM((2, ROWS, D), BF)),
        ("pb", pltpu.VMEM((SEQ, D), BF)),
        ("relay_b", pltpu.VMEM((2, 64, D), BF)),
        ("recv_b", pltpu.VMEM((2, ROWS, D), BF)),
        ("r2", pltpu.VMEM((3, ROWS, ALL), BF)),
        ("final", pltpu.VMEM((ROWS, 1792), F32)),
        ("gacc", pltpu.VMEM((5, 8, 512), F32)),
        ("gsum", pltpu.VMEM((4, 8, 512), F32)),
        ("grecv", pltpu.VMEM((14, 8, 512), F32)),
        ("zs", dma((8, 24))),
        ("zr", dma((8, 24))),
        ("lsem", dma((13,))),
        ("osem", dma((4,))),
        ("xs", dma((15,))),
        ("xr", dma((15,))),
        ("p1xs", dma((48,))),
        ("p1xr", dma((48,))),
        ("p1ys", dma((24,))),
        ("p1yr", dma((24,))),
        ("p2xs", dma((12,))),
        ("p2xr", dma((12,))),
        ("p2ys", dma((12,))),
        ("p2yr", dma((12,))),
        ("lands", dma((24,))),
        ("gs", dma((10,))),
        ("gr", dma((10,))),
    ]
    names = [i[0] for i in ins] + [o[0] for o in outs] + [s[0] for s in scratch]
    results = pl.pallas_call(
        functools.partial(kernel, names),
        out_shape=[jax.ShapeDtypeStruct(o[1], o[2]) for o in outs],
        in_specs=[i[2] for i in ins],
        out_specs=[o[3] for o in outs],
        scratch_shapes=[s[1] for s in scratch],
        compiler_params=pltpu.CompilerParams(
            collective_id=0, has_side_effects=True, vmem_limit_bytes=63 * 1024 * 1024
        ),
        name="block",
    )(*[i[1] for i in ins])
    return arrange(*results[:4])


def arrange_kernel(out_in, tok_in, gains, shares, output, grad_tokens, gain1, qkv, out, gain2, gate_up, down, *scratch):
    out_v, tok_v, shares_v, sem = scratch
    down_at, gu_at, out_at, qkv_at = BASE
    loads = [
        pltpu.make_async_copy(src, dst, sem.at[i])
        for i, (src, dst) in enumerate(((out_in, out_v), (tok_in, tok_v), (shares, shares_v)))
    ]
    for load in loads:
        load.start()

    def columns(core, first, count):
        return shares_v.at[core, :, first : first + count]

    moves = (
        ((out_v, output),),
        ((tok_v, grad_tokens),),
        (
            (columns(0, gu_at, FF), gate_up.at[0]),
            (columns(1, gu_at, FF), gate_up.at[1]),
            (columns(0, qkv_at, 512), qkv.at[0]),
            (columns(0, qkv_at + 512, 256), qkv.at[1, :, 0:256]),
            (columns(1, qkv_at, 256), qkv.at[1, :, 256:512]),
            (columns(1, qkv_at + 256, 512), qkv.at[2]),
            (columns(0, down_at, 768), down.at[:, 0:768]),
            (columns(1, down_at + 128, 640), down.at[:, 768:1408]),
            (columns(0, out_at, 256), out.at[:, 0:256]),
            (columns(1, out_at, 256), out.at[:, 256:512]),
        ),
    )
    for i in range(4):
        at = slice(i * 512, (i + 1) * 512)
        gain1[:, at] = gains[i : i + 1, :]
        gain2[:, at] = gains[4 + i : 5 + i, :]
    stores = []
    for load, group in zip(loads, moves):
        load.wait()
        for src, dst in group:
            stores.append(pltpu.make_async_copy(src, dst, sem.at[3 + len(stores)]))
            stores[-1].start()
    for store in stores:
        store.wait()


def arrange(output, grad_tokens, gains, shares):
    vmem = pl.BlockSpec(memory_space=pltpu.VMEM)
    hbm = pl.BlockSpec(memory_space=pl.ANY)
    outs = (
        ((ROWS, D), hbm),
        ((ROWS, D), hbm),
        ((1, D), vmem),
        ((3, 64, 512), hbm),
        ((64, 512), hbm),
        ((1, D), vmem),
        ((2, 64, FF), hbm),
        ((64, FF), hbm),
    )
    results = pl.pallas_call(
        arrange_kernel,
        out_shape=[jax.ShapeDtypeStruct(o[0], F32) for o in outs],
        in_specs=[hbm, hbm, vmem, hbm],
        out_specs=[o[1] for o in outs],
        scratch_shapes=[
            pltpu.VMEM((ROWS, D), F32),
            pltpu.VMEM((ROWS, D), F32),
            pltpu.VMEM((2, 64, ALL), F32),
            pltpu.SemaphoreType.DMA((15,)),
        ],
        compiler_params=pltpu.CompilerParams(vmem_limit_bytes=63 * 1024 * 1024),
        name="arrange",
    )(output, grad_tokens, gains, shares)
    output, grad_tokens, gain1, qkv, out, gain2, gate_up, down = results
    return output, grad_tokens, gain1.reshape(D), qkv, out.T, gain2.reshape(D), gate_up, down.T


def solution(mesh):
    placed = (
        P(("dp", "tensor"), None),
        P(),
        P(None, None, "tensor"),
        P("tensor", None),
        P(),
        P(None, None, "tensor"),
        P("tensor", None),
        P(("dp", "tensor"), None),
        P("dp"),
    )
    return jax.shard_map(
        block,
        mesh=mesh,
        in_specs=placed,
        out_specs=(
            P(("dp", "tensor"), None),
            P(("dp", "tensor"), None),
            P(),
            P(None, "dp", "tensor"),
            P("tensor", "dp"),
            P(),
            P(None, "dp", "tensor"),
            P("tensor", "dp"),
        ),
        check_vma=False,
    )
```

```python
import functools
import math

import jax
import jax.numpy as jnp
import numpy as np
from jax import lax
from jax.experimental import pallas as pl
from jax.experimental.pallas import tpu as pltpu
from jax.sharding import PartitionSpec as P

D = 2048
HD = 128
FF = 1408
ROWS = 128
SEQ = 512
HEADS = 4
EPS = 1e-05
BF = jnp.bfloat16
F32 = jnp.float32
MESH = pl.DeviceIdType.MESH
OFFS = (0, 3, 1, 2)
ORDER = ((0, 0), (0, 1), (1, 0), (2, 1), (1, 1), (2, 0), (3, 0), (3, 1))
UNIT = {half: i * 64 for i, half in enumerate(ORDER)}

CX = (384, 768, 128, 384)
CY = (384, 640, 128, 384)
COLS = tuple(a + b for a, b in zip(CX, CY))
BASE = (0, 768, 2176, 2432)
ALL = 3200


def nn(a, b):
    return lax.dot_general(a, b, (((1,), (0,)), ((), ())), preferred_element_type=F32)


def nt(a, b):
    return lax.dot_general(a, b, (((1,), (1,)), ((), ())), preferred_element_type=F32)


def tn(a, b):
    return lax.dot_general(a, b, (((0,), (0,)), ((), ())), preferred_element_type=F32)


def rotary_tables():
    half = HD // 2
    freq = np.exp(np.arange(half, dtype=np.float64) * (-2.0 * math.log(10000.0) / HD))
    angles = np.arange(SEQ, dtype=np.float64)[:, None] * freq
    cos, sin = np.cos(angles), np.sin(angles)
    return (
        np.concatenate([cos, cos], axis=1).astype(np.float32),
        np.concatenate([-sin, sin], axis=1).astype(np.float32),
    )


class Place:
    def __init__(self):
        self.dp = lax.axis_index("dp")
        self.t = lax.axis_index("tensor")
        self.c = self.dp % 2
        self.x = (self.dp // 2) % 4
        self.y = self.dp // 8

    def z(self, d):
        return (self.dp, (self.t + d) % 4)

    def xs(self, d):
        return (self.y * 8 + ((self.x + d) % 4) * 2 + self.c, self.t)

    def ys(self, d):
        return (((self.y + d) % 4) * 8 + self.x * 2 + self.c, self.t)

    def core(self):
        return (self.dp + 1 - 2 * self.c, self.t)


def remote(src, dst, ssem, rsem, device):
    return pltpu.make_async_remote_copy(
        src_ref=src, dst_ref=dst, send_sem=ssem, recv_sem=rsem, device_id=device, device_id_type=MESH
    )


def half_rows(place, slot, half):
    block = (place.t + OFFS[slot]) % 4
    return pl.ds(pl.multiple_of(block * 128 + half * 64, 64), 64)


def in_order(place, ref, cols):
    return jnp.concatenate([ref[half_rows(place, *half), cols] for half in ORDER], axis=0)


class Gather:
    def __init__(self, place, buf, ssem, rsem, relative):
        self.place, self.buf, self.ssem, self.rsem, self.relative = place, buf, ssem, rsem, relative

    def row(self, slot, half):
        if self.relative:
            return pl.ds(UNIT[slot, half], 64)
        return half_rows(self.place, slot, half)

    def copy(self, k):
        slot, half, to, there = (
            (0, 0, 1, 1),
            (0, 1, 1, 1),
            (0, 1, -1, 2),
            (0, 0, -1, 2),
            (1, 0, 1, 3),
            (2, 1, -1, 3),
        )[k]
        src = self.buf.at[self.row(slot, half)]
        dst = self.buf.at[self.row(there, half)] if self.relative else src
        return remote(src, dst, self.ssem.at[k], self.rsem.at[k], self.place.z(to))

    def start(self, *which):
        for k in which or (0, 2, 1, 3):
            self.copy(k).start()

    def relay(self):
        self.copy(0).wait_recv()
        self.copy(4).start()
        self.copy(2).wait_recv()
        self.copy(5).start()

    def near(self):
        self.copy(1).wait_recv()
        self.copy(3).wait_recv()

    def far(self):
        self.copy(4).wait_recv()
        self.copy(5).wait_recv()

    def done(self):
        for k in range(6):
            self.copy(k).wait_send()


class Scatter:
    def __init__(self, place, part, relays, recv, ssem, rsem):
        self.place, self.part, self.relays, self.recv = place, part, relays, recv
        self.ssem, self.rsem = ssem, rsem

    def rows(self, slot, half):
        return pl.ds(UNIT[slot, half], 64)

    def copy(self, k, n):
        part, relays, recv = self.part, self.relays, self.recv
        cols = pl.ds(pl.multiple_of(n * 512, 512), 512)
        src, dst, to = (
            (part.at[self.rows(3, 0), cols], relays.at[0, :, cols], 1),
            (part.at[self.rows(2, 1), cols], recv.at[0, self.rows(0, 1), cols], 1),
            (part.at[self.rows(3, 1), cols], relays.at[1, :, cols], -1),
            (part.at[self.rows(1, 0), cols], recv.at[1, self.rows(0, 0), cols], -1),
            (part.at[self.rows(2, 0), cols], recv.at[0, self.rows(0, 0), cols], 1),
            (part.at[self.rows(1, 1), cols], recv.at[1, self.rows(0, 1), cols], -1),
        )[k]
        sem = k * 4 + n
        return remote(src, dst, self.ssem.at[sem], self.rsem.at[sem], self.place.z(to))

    def start(self, n, *which):
        for k in which:
            self.copy(k, n).start()

    def relay(self, first, last):
        @pl.loop(first, last)
        def _(n):
            cols = pl.ds(pl.multiple_of(n * 512, 512), 512)
            for index, slot, half, out in ((0, 2, 0, 4), (1, 1, 1, 5)):
                self.copy(2 * index, n).wait_recv()
                rows = self.rows(slot, half)
                total = self.part[rows, cols].astype(F32) + self.relays[index, :, cols].astype(F32)
                self.part[rows, cols] = total.astype(BF)
                self.copy(out, n).start()

    def finish(self):
        @pl.loop(0, 4)
        def _(n):
            for k in (1, 3, 4, 5):
                self.copy(k, n).wait_recv()

    def total(self, rows):
        return (
            self.part[rows, :].astype(F32)
            + self.recv[0, rows, :].astype(F32)
            + self.recv[1, rows, :].astype(F32)
        )

    def done(self):
        @pl.loop(0, 4)
        def _(n):
            for k in range(6):
                self.copy(k, n).wait_send()


def sixteen(r):
    return pl.ds(pl.multiple_of(r * 16, 16), 16)


def own_rows(place, r):
    return pl.ds(pl.multiple_of(place.t * 128 + r * 16, 16), 16)


def kernel(names, *refs):
    ref = dict(zip(names, refs))
    place = Place()
    tok, cot, live = ref["tok"], ref["cot"], ref["lengths"]
    wq, wo, wgu, wd = ref["wq"], ref["wo"], ref["wgu"], ref["wd"]
    attn, qkv, probs, ctx = ref["attn"], ref["qkv"], ref["probs"], ref["ctx"]
    middle, mlp, masked, w3 = ref["middle"], ref["mlp"], ref["masked"], ref["w3"]
    pa, pb, branch = w3.at[0], w3.at[1], w3.at[2]
    hid, ggu, gctx, gproj, gmid = ref["hid"], ref["ggu"], ref["gctx"], ref["qkv"], ref["gmid"]
    cos_t, sin_t, gain1, gain2 = ref["cos"], ref["sin"], ref["gain1"], ref["gain2"]
    xa, xa0, xb0, xb1, xb2 = ref["xa"], ref["xa0"], ref["xb0"], ref["xb1"], ref["xb2"]
    r2, final, shares = ref["r2"], ref["final"], ref["shares"]
    gacc, grecv, gsum = ref["gacc"], ref["grecv"], ref["gsum"]
    zs, zr, lsem = ref["zs"], ref["zr"], ref["lsem"]
    live_rows = live[0]

    cot_load = pltpu.make_async_copy(cot, masked.at[0:ROWS], lsem.at[7])
    cot_load.start()

    loads = [pltpu.make_async_copy(ref["wq_h"].at[j], wq.at[:, j * 512 : (j + 1) * 512], lsem.at[j]) for j in range(3)]
    tables = [pltpu.make_async_copy(ref["cos_h"], cos_t, lsem.at[8])]
    tables.append(pltpu.make_async_copy(ref["sin_h"], sin_t, lsem.at[9]))
    loads.append(pltpu.make_async_copy(ref["wo_h"], wo, lsem.at[3]))
    loads += [pltpu.make_async_copy(ref["wgu_h"].at[j], wgu.at[:, j * FF : (j + 1) * FF], lsem.at[4 + j]) for j in range(2)]
    loads.append(pltpu.make_async_copy(ref["wd_h"], wd, lsem.at[6]))
    for load in tables + loads:
        load.start()

    barrier = pltpu.get_barrier_semaphore()
    partners = [place.z(d) for d in (1, 2, 3)]
    partners += [place.xs(d) for d in (1, 2, 3)] + [place.ys(d) for d in (1, 2, 3)] + [place.core()]
    for device in partners:
        pl.semaphore_signal(barrier, inc=1, device_id=device, device_id_type=MESH)

    @pl.loop(0, 8)
    def _(r):
        v = tok[sixteen(r), :].astype(F32)
        inv = lax.rsqrt(jnp.mean(v * v, axis=-1, keepdims=True) + EPS)
        attn[own_rows(place, r), :] = (v * inv * gain1[...]).astype(BF)

    pl.semaphore_wait(barrier, len(partners))

    ag1 = Gather(place, attn, zs.at[0], zr.at[0], False)
    agm = Gather(place, masked, zs.at[1], zr.at[1], True)
    ag2 = Gather(place, mlp, zs.at[2], zr.at[2], True)
    ag4 = Gather(place, branch, zs.at[3], zr.at[3], False)
    rs3 = Scatter(place, pa, ref["relay_a"], ref["recv_a"], zs.at[5], zr.at[5])
    rs4 = Scatter(place, pa, ref["relay_a"], ref["recv_a"], zs.at[6], zr.at[6])
    rs2 = Scatter(place, pb, ref["relay_b"], ref["recv_b"], zs.at[7], zr.at[7])

    ws, wr = ref["ws"], ref["wr"]
    halves = (slice(0, 1024), slice(1024, 2048))
    minor, major = (place.x, place.y), (place.y, place.x)

    def w_rows(half, at, count):
        first = (at * 2 + place.c) * 64
        if count == 16:
            first = first + minor[half] * 16
        return pl.ds(pl.multiple_of(first, 16), count)

    def w_first(half, d):
        rows, k = w_rows(half, major[half], 16), half * 3 + d - 1
        dst = w3.at[d - 1, rows, halves[half]]
        return remote(ref["wo_h"].at[rows, halves[half]], dst, ws.at[k], wr.at[k], place.z(d))

    def w_plane(half, phase, d):
        part = w3.at[:, w_rows(half, major[half], (16, 64)[phase]), halves[half]]
        k = 6 + (phase * 2 + half) * 3 + d - 1
        device = (place.xs, place.ys)[half ^ phase](d)
        return remote(part, part, ws.at[k], wr.at[k], device)

    def w_core(half, d):
        part = w3.at[:, w_rows(half, (major[half] + d) % 4, 64), halves[half]]
        return remote(part, part, ws.at[18 + half * 4 + d], wr.at[18 + half * 4 + d], place.core())

    both = [(half, d) for half in range(2) for d in (1, 2, 3)]
    for half, d in both:
        w_first(half, d).start()
    ag1.start()
    cot_load.wait()

    @pl.loop(0, 8)
    def _(r):
        at = place.t * ROWS + r * 16 + lax.broadcasted_iota(jnp.int32, (16, 1), 0)
        v = masked[sixteen(r), :].astype(F32)
        masked[sixteen(r), :] = jnp.where(at < live_rows, v, 0.0).astype(BF)

    def project(slot):
        block = (place.t + OFFS[slot]) % 4
        rows = pl.ds(pl.multiple_of(block * 128, 128), 128)
        for j in range(3):
            p = nn(attn[rows, :], wq[:, j * 512 : (j + 1) * 512])
            if j == 2:
                qkv[rows, 1024:1536] = p.astype(BF)
                continue
            for h in range(HEADS):
                v = p[:, h * HD : (h + 1) * HD]
                v = v * cos_t[rows, :] + pltpu.roll(v, 64, 1) * sin_t[rows, :]
                if j == 0:
                    v = v * HD ** (-0.5)
                qkv[rows, j * 512 + h * HD : j * 512 + (h + 1) * HD] = v.astype(BF)

    for load in tables + loads[:3]:
        load.wait()
    project(0)
    for half, d in both:
        w_first(half, d).wait_recv()
    for half, d in both:
        w_plane(half, 0, d).start()
    ag1.relay()
    for half, d in both:
        w_plane(half, 0, d).wait_recv()
    for half, d in both:
        w_plane(half, 1, d).start()
    for half in range(2):
        w_core(half, 0).start()
    ag1.near()
    agm.start(0, 2)
    project(1)
    project(2)
    ag1.far()
    project(3)

    @pl.loop(0, HEADS)
    def _(h):
        def cols(j):
            return pl.ds(pl.multiple_of(j * 512 + h * HD, HD), HD)

        for q in range(2):
            rows, keys = pl.ds(q * 256, 256), (q + 1) * 256
            scores = nt(qkv[rows, cols(0)], qkv[0:keys, cols(1)])
            at = q * 256 + lax.broadcasted_iota(jnp.int32, (256, keys), 0)
            key = lax.broadcasted_iota(jnp.int32, (256, keys), 1)
            scores = jnp.where((key <= at) & (key < live_rows), scores, -1e30)
            e = jnp.exp(scores - jnp.max(scores, axis=-1, keepdims=True))
            p = (e * (1.0 / jnp.sum(e, axis=-1, keepdims=True))).astype(BF)
            probs[h, rows, 0:keys] = p
            ctx[rows, cols(0)] = nn(p, qkv[0:keys, cols(2)]).astype(BF)

    heads = ref["recv_a"].at[0]

    def to_rows(d):
        src = ctx.at[pl.ds(pl.multiple_of(((place.t + d) % 4) * 128, 128), 128)]
        dst = heads.at[:, pl.ds(pl.multiple_of(place.t * 512, 512), 512)]
        return remote(src, dst, zs.at[4, d - 1], zr.at[4, d - 1], place.z(d))

    for d in (1, 3, 2):
        to_rows(d).start()
    agm.start(1, 3)
    own = pl.ds(pl.multiple_of(place.t * 128, 128), 128)
    heads[:, pl.ds(pl.multiple_of(place.t * 512, 512), 512)] = ctx[own, :]
    for half, d in both:
        w_plane(half, 1, d).wait_recv()
        w_core(half, (4 - d) % 4).start()
    loads[3].wait()

    other = 1 - place.c
    xs, xr = ref["xs"], ref["xr"]

    def swap_a(group):
        src = (masked, mlp, branch, attn)[group]
        return remote(src, xa.at[group], xs.at[group], xr.at[group], place.core())

    def swap_branch(slot):
        block = (place.t + OFFS[slot]) % 4
        rows = pl.ds(pl.multiple_of(block * 128, 128), 128)
        sem = (2, 15, 16, 17)[slot]
        return remote(branch.at[rows], xa.at[2, rows], xs.at[sem], xr.at[sem], place.core())

    def swap_masked(part):
        rows = (slice(0, 384), slice(384, 512))[part]
        sem = (0, 14)[part]
        return remote(masked.at[rows], xa0.at[rows], xs.at[sem], xr.at[sem], place.core())

    def swap_b(k):
        rows = pl.ds((0, 256, 0, 256, 0, 0)[k], 256 if k < 4 else 512)
        if k < 2:
            src = hid.at[rows, pl.ds(pl.multiple_of(other * 640, 128), 768)]
        elif k < 4:
            src = ggu.at[rows, pl.ds(pl.multiple_of(other * FF, 128), FF)]
        elif k == 4:
            src = ctx.at[rows, pl.ds(pl.multiple_of(other * 256, 256), 256)]
        else:
            src = gproj.at[rows, pl.ds(pl.multiple_of(other * 768, 256), 768)]
        dst = (xb0, xb0, xb1, xb1, xb2, xb0)[k].at[rows]
        return remote(src, dst, xs.at[4 + k], xr.at[4 + k], place.core())

    swap_a(3).start()
    swap_b(4).start()

    for half in range(2):
        for d in range(4):
            w_core(half, d).wait_recv()
    for d in (1, 2, 3):
        to_rows(d).wait_recv()

    @pl.loop(0, 4)
    def _(n):
        at = pl.ds(pl.multiple_of(n * 512, 512), 512)

        def share(d, weights):
            return nn(heads[:, pl.ds(pl.multiple_of(((place.t + d) % 4) * 512, 512), 512)], weights)

        out = share(0, wo[:, at]) + share(3, w3[0, :, at]) + share(2, w3[1, :, at]) + share(1, w3[2, :, at])
        middle[:, at] = tok[:, at].astype(F32) + out

    @pl.loop(0, 8)
    def _(r):
        rows = sixteen(r)
        v = middle[rows, :]
        inv = lax.rsqrt(jnp.mean(v * v, axis=-1, keepdims=True) + EPS)
        mlp[rows, :] = (v * inv * gain2[...]).astype(BF)

    for d in (1, 2, 3):
        to_rows(d).wait_send()
    for half, d in both:
        w_first(half, d).wait_send()
        w_plane(half, 0, d).wait_send()
        w_plane(half, 1, d).wait_send()
    for half in range(2):
        for d in range(4):
            w_core(half, d).wait_send()
    ag2.start()
    for load in loads[4:]:
        load.wait()

    own_b = (
        hid.at[:, pl.ds(pl.multiple_of(place.c * 640, 128), 768)],
        ggu.at[:, pl.ds(pl.multiple_of(place.c * FF, 128), FF)],
        ctx.at[:, pl.ds(pl.multiple_of(place.c * 256, 256), 256)],
        gproj.at[:, pl.ds(pl.multiple_of(place.c * 768, 256), 768)],
    )
    own_a = (masked, mlp, branch, attn)
    other_a = (xa0, pb, wd.at[0:512], wd.at[512:1024])
    other_b = (xb0, xb1, xb2, xb0)
    osem = ref["osem"]

    def bring(group):
        return pltpu.make_async_copy(xa.at[group], other_a[group], osem.at[group])

    def fetch(group):
        if group == 2:
            for slot in range(4):
                swap_branch(slot).wait_recv()
        else:
            swap_a(group).wait_recv()
        bring(group).start()

    def piece(group, axis, tile, first, count):
        if group == 3 and axis == 1:
            return mlp.at[pl.ds(first, count), pl.ds(pl.multiple_of(tile * 384, 128), 384)]
        base = (FF, 0, FF + 768, FF + 1024)[group]
        lo = base if axis == 0 else base + CX[group]
        width = CX[group] if axis == 0 else CY[group]
        rows = pl.ds(pl.multiple_of(tile * 512 + first, min(count, 128)), count)
        return wgu.at[rows, lo : lo + width]

    p1xs, p1xr, p1ys, p1yr = ref["p1xs"], ref["p1xr"], ref["p1ys"], ref["p1yr"]

    def relayed(group, axis):
        if group < 2:
            return ref[("relx", "rely")[axis] + str(group)]
        lo = ((768, 896), (0, 384))[group - 2][axis]
        return xb1.at[:, lo : lo + CX[group]]

    def arrived(group, axis, side):
        if group < 2:
            return ref[("recx", "recy")[axis] + str(group)].at[side]
        width = CX[group]
        lo = ((1536, 1792), (0, 768))[group - 2][axis] + side * width
        return xa0.at[:, pl.ds(lo if isinstance(lo, int) else pl.multiple_of(lo, 128), width)]

    def tile_of(step):
        return (place.y + jnp.where(step == 0, 2, jnp.where(step == 1, 1, jnp.where(step == 2, 3, 0)))) % 4

    def send_x(group, kind, step):
        tile, to = tile_of(step), 1 - 2 * (step % 2)
        rows = pl.ds(pl.multiple_of(tile * 128, 128), 128)
        if kind == 0:
            block, dst = place.x + 2, relayed(group, 0).at[rows]
        elif kind == 1:
            block, dst, to = place.x + 4 - to, arrived(group, 0, (1 + to) // 2).at[rows], -to
        else:
            block, dst = place.x + 4 + to, arrived(group, 0, (1 - to) // 2).at[rows]
        src = piece(group, 0, tile, pl.multiple_of((block % 4) * 128, 128), 128)
        sem = (group * 3 + kind) * 4 + step
        return remote(src, dst, p1xs.at[sem], p1xr.at[sem], place.xs(4 + to))

    def send_y(group, k):
        offset, first, dst, to = (
            (2, 0, relayed(group, 1).at[0:256], 1),
            (1, 256, arrived(group, 1, 0).at[256:512], 1),
            (2, 256, relayed(group, 1).at[256:512], 3),
            (3, 0, arrived(group, 1, 1).at[0:256], 3),
            (1, 0, arrived(group, 1, 0).at[0:256], 1),
            (3, 256, arrived(group, 1, 1).at[256:512], 3),
        )[k]
        src = piece(group, 1, (place.y + offset) % 4, first, 256)
        return remote(src, dst, p1ys.at[group * 6 + k], p1yr.at[group * 6 + k], place.ys(to))

    def gradient(group, step):
        tile = tile_of(step)
        at = pl.ds(pl.multiple_of(tile * 512, 512), 512)
        lo = 0
        for axis, width in ((0, CX[group]), (1, CY[group])):
            own, oth = own_b[group].at[:, lo : lo + width], other_b[group].at[:, lo : lo + width]
            out = tn(own_a[group][:, at], own[...]) + tn(other_a[group][:, at], oth[...])
            piece(group, axis, tile, 0, 512)[...] = out.astype(BF)
            lo += width
        send_x(group, 0, step).start()

        @pl.when(step == 0)
        def _():
            send_y(group, 0).start()
            send_y(group, 2).start()

    def near_x(group, step):
        send_x(group, 1, step).start()

    def near_y(group, step):
        for when in (1, 2):

            @pl.when(step == when)
            def _():
                send_y(group, 2 * when - 1).start()

    def all_near(group, *axes):
        @pl.loop(0, 4)
        def _(step):
            for axis in axes:
                (near_x, near_y)[axis](group, step)

    lands = ref["lands"]

    def mid_copies(group):
        if group > 1:
            return ()
        return (
            pltpu.make_async_copy(relayed(group, 0), hid.at[:, 0 : CX[group]], lands.at[16 + group]),
            pltpu.make_async_copy(relayed(group, 1), hid.at[:, 768 : 768 + CY[group]], lands.at[20 + group]),
        )

    def mid_start(group):
        for step in range(4):
            send_x(group, 0, step).wait_recv()
        for k in (0, 2):
            send_y(group, k).wait_recv()
        for copy in mid_copies(group):
            copy.start()

    def mid_end(group):
        for copy in mid_copies(group):
            copy.wait()

        def add(axis, tile, first, rows, lo, width, count):
            src = hid.at[:, lo : lo + width] if group < 2 else relayed(group, axis)

            @pl.loop(0, count // 32)
            def _(i):
                own = piece(group, axis, tile, pl.multiple_of(first + i * 32, 32), 32)
                got = src[pl.ds(pl.multiple_of(rows + i * 32, 32), 32), :]
                own[...] = (own[...].astype(F32) + got.astype(F32)).astype(BF)

        for step in range(4):
            to, tile = (1, 3)[step % 2], tile_of(step)
            add(0, tile, ((place.x + to) % 4) * 128, tile * 128, 0, CX[group], 128)
            send_x(group, 2, step).start()
        for k, offset, first in ((4, 1, 0), (5, 3, 256)):
            add(1, (place.y + offset) % 4, first, first, 768, CY[group], 256)
            send_y(group, k).start()

    def feed(first, count):
        rows = slice(first, first + count)
        for n0, n1 in ((0, 512), (512, 1024), (1024, 1408)):
            gate = nn(mlp[rows, :], wgu[:, n0:n1])
            up = nn(mlp[rows, :], wgu[:, FF + n0 : FF + n1])
            sig = jax.nn.sigmoid(gate)
            silu = gate * sig
            hid[rows, n0:n1] = (silu * up).astype(BF)
            ggu[rows, n0:n1] = (up * sig * (1.0 + gate * (1.0 - sig))).astype(BF)
            ggu[rows, FF + n0 : FF + n1] = silu.astype(BF)

    def feed_back(first, count):
        rows = slice(first, first + count)
        for n0, n1 in ((0, 512), (512, 1024), (1024, 1408)):
            grad = nt(masked[rows, :], wd[n0:n1, :])
            for lo in (0, FF):
                ggu[rows, lo + n0 : lo + n1] = (grad * ggu[rows, lo + n0 : lo + n1].astype(F32)).astype(BF)

    def feed_part(first, count, *sends):
        rows = slice(first, first + count)

        @pl.loop(0, 4)
        def _(n):
            at = pl.ds(pl.multiple_of(n * 512, 512), 512)
            rs3.part[rows, at] = nt(ggu[rows, :], wgu[at, :]).astype(BF)
            rs3.start(n, *sends)

    feed(0, 128)
    feed_back(0, 128)
    feed_part(0, 128)
    ag2.relay()
    agm.near()
    agm.relay()
    swap_masked(0).start()
    feed(128, 128)
    feed_back(128, 128)
    feed_part(128, 128, 1, 3)
    swap_b(0).start()
    swap_b(2).start()
    ag2.near()
    ag2.far()
    swap_a(1).start()
    feed(256, 256)
    swap_b(1).start()
    agm.far()
    swap_masked(1).start()
    feed_back(256, 256)
    swap_b(3).start()
    fetch(1)
    feed_part(256, 256, 0, 2)
    swap_b(0).wait_recv()
    swap_b(1).wait_recv()
    swap_masked(0).wait_recv()
    swap_masked(1).wait_recv()

    @pl.loop(0, 4)
    def _(step):
        gradient(0, step)
        near_x(0, step)
        near_y(0, step)

        @pl.when(step < 3)
        def _():
            rs3.relay(jnp.where(step == 2, 3, step), jnp.where(step == 0, 1, jnp.where(step == 1, 3, 4)))
    bring(1).wait()
    swap_b(2).wait_recv()
    swap_b(3).wait_recv()

    @pl.loop(0, 2)
    def _(step):
        gradient(1, step)

    p2xs, p2xr, p2ys, p2yr = ref["p2xs"], ref["p2xr"], ref["p2ys"], ref["p2yr"]

    def landing(group):
        copies = []
        for d in range(2 if group < 2 else 0):
            for axis in range(2):
                lo = d * FF + axis * 768
                width = CX[group] if axis == 0 else CY[group]
                sem = lands.at[group * 4 + d * 2 + axis]
                copies.append(pltpu.make_async_copy(arrived(group, axis, d), ggu.at[:, lo : lo + width], sem))
        return copies

    def send_2(group, axis, d):
        sem = group * 3 + d - 1
        own = pl.multiple_of(place.x * 128, 128)
        if axis == 0:
            src = piece(group, 0, (place.y + d) % 4, own, 128)
            dst = r2.at[d - 1, :, BASE[group] : BASE[group] + CX[group]]
            return remote(src, dst, p2xs.at[sem], p2xr.at[sem], place.ys(d))
        src = piece(group, 1, place.y, pl.multiple_of(((place.x + d) % 4) * 128, 128), 128)
        dst = r2.at[d - 1, :, BASE[group] + CX[group] : BASE[group] + COLS[group]]
        return remote(src, dst, p2ys.at[sem], p2yr.at[sem], place.xs(d))

    def land(group):
        for step in range(4):
            for kind in (1, 2):
                send_x(group, kind, step).wait_recv()
        for k in (1, 3, 4, 5):
            send_y(group, k).wait_recv()
        for copy in landing(group):
            copy.start()

    def first_sum(group):
        for copy in landing(group):
            copy.wait()
        for axis in range(2):
            lo = axis * 768
            width = CX[group] if axis == 0 else CY[group]
            if group < 2:
                got = [ggu.at[:, d * FF + lo : d * FF + lo + width] for d in range(2)]
            else:
                got = [arrived(group, axis, d) for d in range(2)]

            @pl.loop(0, 16)
            def _(i):
                if axis == 0:
                    own = piece(group, 0, i // 4, pl.multiple_of(place.x * 128 + (i % 4) * 32, 32), 32)
                else:
                    own = piece(group, 1, place.y, pl.multiple_of(i * 32, 32), 32)
                rows = pl.ds(pl.multiple_of(i * 32, 32), 32)
                total = own[...].astype(F32)
                for d in range(2):
                    total = total + got[d][rows, :].astype(F32)
                own[...] = total.astype(BF)

            for d in (2, 1, 3):
                send_2(group, axis, d).start()

    def whole_of(group):
        return ((final, 0), (middle, 0), (final, 768), (final, 1024))[group]

    def ending(group):
        ref_at, first = whole_of(group)
        cols = slice(first, first + COLS[group])
        mine = ref_at.at[pl.ds(pl.multiple_of(place.c * 64, 64), 64), cols]
        theirs = ref_at.at[pl.ds(pl.multiple_of(other * 64, 64), 64), cols]
        dst = shares.at[place.c, :, BASE[group] : BASE[group] + COLS[group]]
        return (
            remote(theirs, dst, xs.at[10 + group], xr.at[10 + group], place.core()),
            pltpu.make_async_copy(mine, dst, lsem.at[9 + group]),
        )

    def second_sum(group):
        for axis in range(2):
            for d in (1, 2, 3):
                send_2(group, axis, d).wait_recv()
            lo = BASE[group] + (0 if axis == 0 else CX[group])
            width = CX[group] if axis == 0 else CY[group]
            whole, first = whole_of(group)
            first += lo - BASE[group]

            @pl.loop(0, 4)
            def _(i):
                rows = pl.ds(pl.multiple_of(i * 32, 32), 32)
                own = piece(group, axis, place.y, pl.multiple_of(place.x * 128 + i * 32, 32), 32)
                total = own[...].astype(F32)
                for d in range(3):
                    total = total + r2[d, rows, lo : lo + width].astype(F32)
                whole[rows, first : first + width] = total
        for copy in ending(group):
            copy.start()

    rs3.finish()

    def fold(v):
        return jnp.concatenate([v[:, i * 512 : (i + 1) * 512] for i in range(4)], axis=0)

    def mlp_back(r, total):
        rows = sixteen(r)
        grad = rs3.total(rows)
        v = middle[rows, :]
        inv = lax.rsqrt(jnp.mean(v * v, axis=-1, keepdims=True) + EPS)
        scaled = grad * gain2[...]
        back = (
            masked[rows, :].astype(F32)
            + inv * scaled
            - v * (inv * inv * inv) * jnp.mean(v * scaled, axis=-1, keepdims=True)
        )
        gmid[rows, :] = back
        branch[own_rows(place, r), :] = back.astype(BF)
        return total + jnp.sum(grad * v * inv, axis=0, keepdims=True)

    gain2_part = lax.fori_loop(0, 8, mlp_back, jnp.zeros((1, D), F32))
    gacc[0, 4:8, :] = fold(gain2_part)
    ag4.start()
    swap_branch(0).start()
    rs3.done()

    @pl.loop(2, 4)
    def _(step):
        gradient(1, step)

    all_near(1, 0)
    @pl.loop(0, 4)
    def _(n):
        at = pl.ds(pl.multiple_of(n * 512, 512), 512)
        rs2.part[:, at] = nn(hid[...], wd[:, at]).astype(BF)

    fetch(3)
    for k in (0, 1, 2, 3):
        swap_b(k).wait_send()
    mid_start(0)
    ag4.relay()

    mid_end(0)
    mid_start(1)
    mid_end(1)
    all_near(1, 1)
    ag4.near()
    swap_branch(1).start()
    swap_branch(2).start()
    ag4.far()
    swap_branch(3).start()

    @pl.loop(0, 4)
    def _(n):
        rs2.start(n, 0, 2)

    @pl.loop(0, 4)
    def _(n):
        rs2.start(n, 1, 3)


    @pl.loop(0, 2)
    def _(n):
        at = pl.ds(pl.multiple_of(n * 256, 256), 256)
        gctx[:, at] = nt(branch[...], wo[at, :]).astype(BF)


    def turn_back(v, rows):
        return v * cos_t[rows, :] - pltpu.roll(v, 64, 1) * sin_t[rows, :]

    def heads_back(h):
        def cols(j):
            return pl.ds(pl.multiple_of(j * 512 + h * HD, HD), HD)

        def part(q):
            rows, keys = pl.ds(q * 256, 256), (q + 1) * 256
            p = probs[h, rows, 0:keys]
            grad = gctx[rows, cols(0)]
            wide = p.astype(F32)
            gp = nt(grad, qkv[0:keys, cols(2)])
            gs = (wide * (gp - jnp.sum(wide * gp, axis=-1, keepdims=True))).astype(BF)
            gq = (turn_back(nn(gs, qkv[0:keys, cols(1)]), rows) * HD ** (-0.5)).astype(BF)
            return gq, tn(gs, qkv[rows, cols(0)]), tn(p, grad)

        q1, k1, v1 = part(1)
        q0, k0, v0 = part(0)
        lo, hi = slice(0, 256), slice(256, 512)
        k0, k1 = turn_back(k0 + k1[lo], lo).astype(BF), turn_back(k1[hi], hi).astype(BF)
        v0, v1 = (v0 + v1[lo]).astype(BF), v1[hi].astype(BF)
        for j, low, high in ((0, q0, q1), (1, k0, k1), (2, v0, v1)):
            gproj[lo, cols(j)] = low
            gproj[hi, cols(j)] = high

    pl.loop(0, HEADS // 2)(heads_back)
    fetch(2)
    pl.loop(HEADS // 2, HEADS)(heads_back)
    swap_b(5).start()
    @pl.loop(0, 4)
    def _(n):
        at = pl.ds(pl.multiple_of(n * 512, 512), 512)
        part = nt(in_order(place, gproj, slice(None)), wq[at, :])
        rs4.part[:, at] = part.astype(BF)
        seen = jnp.sum(part * in_order(place, attn, at).astype(F32), axis=0, keepdims=True)
        gsum[n] = jnp.broadcast_to(seen, (8, 512))

    for n in range(4):
        at = slice(n * 512, (n + 1) * 512)
        gacc[0, n : n + 1, :] = gsum[n, 0:1, :] / gain1[:, at]
    gs, gr = ref["gs"], ref["gr"]

    def spread(stage):
        count = 2 if stage == 3 else 4
        me = (place.t, place.x, place.y, place.c)[stage]
        out = []
        for d in range(1, count):
            device = (place.z, place.xs, place.ys, lambda _: place.core())[stage](d)
            k = stage * 3 + d - 1
            out.append(remote(gacc.at[stage], grecv.at[stage * 4 + me], gs.at[k], gr.at[k], device))
        return out, count, me

    def spread_start(stage):
        copies, _, me = spread(stage)
        grecv[stage * 4 + me] = gacc[stage]
        for copy in copies:
            copy.start()

    def spread_end(stage):
        copies, count, _ = spread(stage)
        for copy in copies:
            copy.wait_recv()
        total = grecv[stage * 4]
        for i in range(1, count):
            total = total + grecv[stage * 4 + i]
        gacc[stage + 1] = total

    spread_start(0)

    @pl.loop(0, 4)
    def _(n):
        rs4.start(n, 0, 2)

    @pl.loop(0, 4)
    def _(n):
        rs4.start(n, 1, 3)

    land(0)
    first_sum(0)
    swap_a(1).wait_send()
    ag2.done()
    bring(3).wait()
    swap_b(5).wait_recv()

    @pl.loop(0, 4)
    def _(step):
        gradient(3, step)

    all_near(3, 0, 1)
    rs2.relay(0, 4)
    spread_end(0)
    spread_start(1)
    swap_b(4).wait_recv()
    bring(2).wait()

    @pl.loop(0, 4)
    def _(step):
        gradient(2, step)

    all_near(2, 0, 1)
    mid_start(3)
    mid_end(3)
    spread_end(1)
    spread_start(2)
    rs4.relay(0, 4)
    mid_start(2)
    mid_end(2)
    land(1)
    first_sum(1)
    spread_end(2)
    spread_start(3)
    rs2.finish()

    @pl.loop(0, 8)
    def _(r):
        rows = sixteen(r)
        middle[rows, :] = middle[rows, :] + rs2.total(rows)

    out_copy = pltpu.make_async_copy(middle, ref["output"], lsem.at[7])
    out_copy.start()
    land(3)
    first_sum(3)
    land(2)
    first_sum(2)
    second_sum(0)
    rs4.finish()

    @pl.loop(0, 8)
    def _(r):
        rows = sixteen(r)
        grad = rs4.total(rows)
        v = tok[rows, :].astype(F32)
        inv = lax.rsqrt(jnp.mean(v * v, axis=-1, keepdims=True) + EPS)
        scaled = grad * gain1[...]
        gmid[rows, :] = (
            gmid[rows, :]
            + inv * scaled
            - v * (inv * inv * inv) * jnp.mean(v * scaled, axis=-1, keepdims=True)
        )

    tok_copy = pltpu.make_async_copy(gmid, ref["grad_tokens"], lsem.at[8])
    tok_copy.start()
    spread_end(3)
    ref["gains"][...] = gacc[4]
    out_copy.wait()
    second_sum(1)
    second_sum(3)
    second_sum(2)

    for gather in (ag1, agm, ag4):
        gather.done()
    rs4.done()
    rs2.done()
    swap_a(3).wait_send()
    for slot in range(4):
        swap_branch(slot).wait_send()
    swap_masked(0).wait_send()
    swap_masked(1).wait_send()
    for k in (4, 5):
        swap_b(k).wait_send()
    for group in range(4):
        for step in range(4):
            for kind in range(3):
                send_x(group, kind, step).wait_send()
        for k in range(6):
            send_y(group, k).wait_send()
        for d in (1, 2, 3):
            for axis in range(2):
                send_2(group, axis, d).wait_send()
    for stage in range(4):
        for copy in spread(stage)[0]:
            copy.wait_send()
    tok_copy.wait()
    for group in range(4):
        for copy in ending(group):
            copy.wait()


def block(tokens, gain_attn, w_qkv, w_out, gain_mlp, w_gate_up, w_down, cotangent, lengths):
    cos_t, sin_t = rotary_tables()
    vmem = pl.BlockSpec(memory_space=pltpu.VMEM)
    smem = pl.BlockSpec(memory_space=pltpu.SMEM)
    hbm = pl.BlockSpec(memory_space=pl.ANY)
    ins = [
        ("tok", tokens, vmem),
        ("gain1", gain_attn.reshape(1, D), vmem),
        ("wq_h", w_qkv, hbm),
        ("wo_h", w_out, hbm),
        ("gain2", gain_mlp.reshape(1, D), vmem),
        ("wgu_h", w_gate_up, hbm),
        ("wd_h", w_down, hbm),
        ("cot", cotangent, hbm),
        ("lengths", lengths, smem),
        ("cos_h", jnp.asarray(cos_t), hbm),
        ("sin_h", jnp.asarray(sin_t), hbm),
    ]
    outs = [
        ("output", (ROWS, D), F32, hbm),
        ("grad_tokens", (ROWS, D), F32, hbm),
        ("gains", (8, 512), F32, vmem),
        ("shares", (2, 64, ALL), F32, hbm),
        ("xa", (4, SEQ, D), BF, hbm),
    ]
    outs += [(f"relx{g}", (SEQ, CX[g]), BF, hbm) for g in range(2)]
    outs += [(f"rely{g}", (SEQ, CY[g]), BF, hbm) for g in range(2)]
    outs += [(f"recx{g}", (2, SEQ, CX[g]), BF, hbm) for g in range(2)]
    outs += [(f"recy{g}", (2, SEQ, CY[g]), BF, hbm) for g in range(2)]
    dma = pltpu.SemaphoreType.DMA
    scratch = [
        ("wq", pltpu.VMEM((D, 1536), BF)),
        ("wo", pltpu.VMEM((512, D), BF)),
        ("wgu", pltpu.VMEM((D, 2 * FF), BF)),
        ("wd", pltpu.VMEM((FF, D), BF)),
        ("attn", pltpu.VMEM((SEQ, D), BF)),
        ("qkv", pltpu.VMEM((SEQ, 1536), BF)),
        ("probs", pltpu.VMEM((HEADS, SEQ, SEQ), BF)),
        ("ctx", pltpu.VMEM((SEQ, 512), BF)),
        ("middle", pltpu.VMEM((ROWS, D), F32)),
        ("mlp", pltpu.VMEM((SEQ, D), BF)),
        ("masked", pltpu.VMEM((SEQ, D), BF)),
        ("hid", pltpu.VMEM((SEQ, FF), BF)),
        ("ggu", pltpu.VMEM((SEQ, 2 * FF), BF)),
        ("gctx", pltpu.VMEM((SEQ, 512), BF)),
        ("xa0", pltpu.VMEM((SEQ, D), BF)),
        ("xb0", pltpu.VMEM((SEQ, COLS[0]), BF)),
        ("xb1", pltpu.VMEM((SEQ, COLS[1]), BF)),
        ("xb2", pltpu.VMEM((SEQ, COLS[2]), BF)),
        ("gmid", pltpu.VMEM((ROWS, D), F32)),
        ("w3", pltpu.VMEM((3, SEQ, D), BF)),
        ("relay_a", pltpu.VMEM((2, 64, D), BF)),
        ("recv_a", pltpu.VMEM((2, ROWS, D), BF)),
        ("relay_b", pltpu.VMEM((2, 64, D), BF)),
        ("recv_b", pltpu.VMEM((2, ROWS, D), BF)),
        ("r2", pltpu.VMEM((3, ROWS, ALL), BF)),
        ("final", pltpu.VMEM((ROWS, 1792), F32)),
        ("gacc", pltpu.VMEM((5, 8, 512), F32)),
        ("cos", pltpu.VMEM((SEQ, HD), F32)),
        ("sin", pltpu.VMEM((SEQ, HD), F32)),
        ("gsum", pltpu.VMEM((4, 8, 512), F32)),
        ("grecv", pltpu.VMEM((14, 8, 512), F32)),
        ("zs", dma((8, 24))),
        ("zr", dma((8, 24))),
        ("lsem", dma((13,))),
        ("osem", dma((4,))),
        ("xs", dma((18,))),
        ("xr", dma((18,))),
        ("p1xs", dma((48,))),
        ("p1xr", dma((48,))),
        ("p1ys", dma((24,))),
        ("p1yr", dma((24,))),
        ("p2xs", dma((12,))),
        ("p2xr", dma((12,))),
        ("p2ys", dma((12,))),
        ("p2yr", dma((12,))),
        ("lands", dma((24,))),
        ("gs", dma((10,))),
        ("ws", dma((26,))),
        ("wr", dma((26,))),
        ("gr", dma((10,))),
    ]
    names = [i[0] for i in ins] + [o[0] for o in outs] + [s[0] for s in scratch]
    results = pl.pallas_call(
        functools.partial(kernel, names),
        out_shape=[jax.ShapeDtypeStruct(o[1], o[2]) for o in outs],
        in_specs=[i[2] for i in ins],
        out_specs=[o[3] for o in outs],
        scratch_shapes=[s[1] for s in scratch],
        compiler_params=pltpu.CompilerParams(
            collective_id=0, has_side_effects=True, vmem_limit_bytes=63 * 1024 * 1024
        ),
        name="block",
    )(*[i[1] for i in ins])
    return arrange(*results[:4])


def arrange_kernel(out_in, tok_in, gains, shares, output, grad_tokens, gain1, qkv, out, gain2, gate_up, down, *scratch):
    out_v, tok_v, shares_v, sem = scratch
    down_at, gu_at, out_at, qkv_at = BASE

    def columns(core, first, count):
        return shares_v.at[core, :, first : first + count]

    def through(src, buf, dst, half):
        rows = slice(half * 64, half * 64 + 64)
        return (src.at[rows], buf.at[rows]), ((buf.at[rows], dst.at[rows]),)

    def of_shares(first, count, *stores):
        cols = slice(first, first + count)
        return (shares.at[:, :, cols], shares_v.at[:, :, cols]), stores

    moves = (
        through(out_in, out_v, output, 0),
        through(out_in, out_v, output, 1),
        through(tok_in, tok_v, grad_tokens, 0),
        through(tok_in, tok_v, grad_tokens, 1),
        of_shares(gu_at, FF, (columns(0, gu_at, FF), gate_up.at[0]), (columns(1, gu_at, FF), gate_up.at[1])),
        of_shares(
            qkv_at,
            768,
            (columns(0, qkv_at, 512), qkv.at[0]),
            (columns(0, qkv_at + 512, 256), qkv.at[1, :, 0:256]),
            (columns(1, qkv_at, 256), qkv.at[1, :, 256:512]),
            (columns(1, qkv_at + 256, 512), qkv.at[2]),
        ),
        of_shares(
            down_at,
            768,
            (columns(0, down_at, 768), down.at[:, 0:768]),
            (columns(1, down_at + 128, 640), down.at[:, 768:1408]),
        ),
        of_shares(
            out_at,
            256,
            (columns(0, out_at, 256), out.at[:, 0:256]),
            (columns(1, out_at, 256), out.at[:, 256:512]),
        ),
    )
    loads = [pltpu.make_async_copy(*move[0], sem.at[i]) for i, move in enumerate(moves)]
    for load in loads:
        load.start()
    for i in range(4):
        at = slice(i * 512, (i + 1) * 512)
        gain1[:, at] = gains[i : i + 1, :]
        gain2[:, at] = gains[4 + i : 5 + i, :]
    stores = []
    for load, move in zip(loads, moves):
        load.wait()
        for src, dst in move[1]:
            stores.append(pltpu.make_async_copy(src, dst, sem.at[len(moves) + len(stores)]))
            stores[-1].start()
    for store in stores:
        store.wait()


def arrange(output, grad_tokens, gains, shares):
    vmem = pl.BlockSpec(memory_space=pltpu.VMEM)
    hbm = pl.BlockSpec(memory_space=pl.ANY)
    outs = (
        ((ROWS, D), hbm),
        ((ROWS, D), hbm),
        ((1, D), vmem),
        ((3, 64, 512), hbm),
        ((64, 512), hbm),
        ((1, D), vmem),
        ((2, 64, FF), hbm),
        ((64, FF), hbm),
    )
    results = pl.pallas_call(
        arrange_kernel,
        out_shape=[jax.ShapeDtypeStruct(o[0], F32) for o in outs],
        in_specs=[hbm, hbm, vmem, hbm],
        out_specs=[o[1] for o in outs],
        scratch_shapes=[
            pltpu.VMEM((ROWS, D), F32),
            pltpu.VMEM((ROWS, D), F32),
            pltpu.VMEM((2, 64, ALL), F32),
            pltpu.SemaphoreType.DMA((22,)),
        ],
        compiler_params=pltpu.CompilerParams(vmem_limit_bytes=63 * 1024 * 1024),
        name="arrange",
    )(output, grad_tokens, gains, shares)
    output, grad_tokens, gain1, qkv, out, gain2, gate_up, down = results
    return output, grad_tokens, gain1.reshape(D), qkv, out.T, gain2.reshape(D), gate_up, down.T


def solution(mesh):
    placed = (
        P(("dp", "tensor"), None),
        P(),
        P(None, None, "tensor"),
        P("tensor", None),
        P(),
        P(None, None, "tensor"),
        P("tensor", None),
        P(("dp", "tensor"), None),
        P("dp"),
    )
    return jax.shard_map(
        block,
        mesh=mesh,
        in_specs=placed,
        out_specs=(
            P(("dp", "tensor"), None),
            P(("dp", "tensor"), None),
            P(),
            P(None, "dp", "tensor"),
            P("tensor", "dp"),
            P(),
            P(None, "dp", "tensor"),
            P("tensor", "dp"),
        ),
        check_vma=False,
    )
```

```python
import functools
import math

import jax
import jax.numpy as jnp
import numpy as np
from jax import lax
from jax.experimental import pallas as pl
from jax.experimental.pallas import tpu as pltpu
from jax.sharding import PartitionSpec as P

D = 2048
HD = 128
FF = 1408
ROWS = 128
SEQ = 512
HEADS = 4
EPS = 1e-05
BF = jnp.bfloat16
F32 = jnp.float32
MESH = pl.DeviceIdType.MESH
OFFS = (0, 3, 1, 2)
ORDER = ((0, 0), (0, 1), (1, 0), (2, 1), (1, 1), (2, 0), (3, 0), (3, 1))
UNIT = {half: i * 64 for i, half in enumerate(ORDER)}

CX = (384, 768, 128, 384)
CY = (384, 640, 128, 384)
COLS = tuple(a + b for a, b in zip(CX, CY))
BASE = (0, 768, 2176, 2432)
ALL = 3200


def nn(a, b):
    return lax.dot_general(a, b, (((1,), (0,)), ((), ())), preferred_element_type=F32)


def nt(a, b):
    return lax.dot_general(a, b, (((1,), (1,)), ((), ())), preferred_element_type=F32)


def tn(a, b):
    return lax.dot_general(a, b, (((0,), (0,)), ((), ())), preferred_element_type=F32)


def rotary_tables():
    half = HD // 2
    freq = np.exp(np.arange(half, dtype=np.float64) * (-2.0 * math.log(10000.0) / HD))
    angles = np.arange(SEQ, dtype=np.float64)[:, None] * freq
    cos, sin = np.cos(angles), np.sin(angles)
    return (
        np.concatenate([cos, cos], axis=1).astype(np.float32),
        np.concatenate([-sin, sin], axis=1).astype(np.float32),
    )


class Place:
    def __init__(self):
        self.dp = lax.axis_index("dp")
        self.t = lax.axis_index("tensor")
        self.c = self.dp % 2
        self.x = (self.dp // 2) % 4
        self.y = self.dp // 8

    def z(self, d):
        return (self.dp, (self.t + d) % 4)

    def xs(self, d):
        return (self.y * 8 + ((self.x + d) % 4) * 2 + self.c, self.t)

    def ys(self, d):
        return (((self.y + d) % 4) * 8 + self.x * 2 + self.c, self.t)

    def core(self):
        return (self.dp + 1 - 2 * self.c, self.t)


def remote(src, dst, ssem, rsem, device):
    return pltpu.make_async_remote_copy(
        src_ref=src, dst_ref=dst, send_sem=ssem, recv_sem=rsem, device_id=device, device_id_type=MESH
    )


def half_rows(place, slot, half):
    block = (place.t + OFFS[slot]) % 4
    return pl.ds(pl.multiple_of(block * 128 + half * 64, 64), 64)


def in_order(place, ref, cols):
    return jnp.concatenate([ref[half_rows(place, *half), cols] for half in ORDER], axis=0)


class Gather:
    def __init__(self, place, buf, ssem, rsem, relative):
        self.place, self.buf, self.ssem, self.rsem, self.relative = place, buf, ssem, rsem, relative

    def row(self, slot, half):
        if self.relative:
            return pl.ds(UNIT[slot, half], 64)
        return half_rows(self.place, slot, half)

    def copy(self, k):
        slot, half, to, there = (
            (0, 0, 1, 1),
            (0, 1, 1, 1),
            (0, 1, -1, 2),
            (0, 0, -1, 2),
            (1, 0, 1, 3),
            (2, 1, -1, 3),
        )[k]
        src = self.buf.at[self.row(slot, half)]
        dst = self.buf.at[self.row(there, half)] if self.relative else src
        return remote(src, dst, self.ssem.at[k], self.rsem.at[k], self.place.z(to))

    def start(self, *which):
        for k in which or (0, 2, 1, 3):
            self.copy(k).start()

    def relay(self):
        self.copy(0).wait_recv()
        self.copy(4).start()
        self.copy(2).wait_recv()
        self.copy(5).start()

    def near(self):
        self.copy(1).wait_recv()
        self.copy(3).wait_recv()

    def far(self):
        self.copy(4).wait_recv()
        self.copy(5).wait_recv()

    def done(self):
        for k in range(6):
            self.copy(k).wait_send()


class Scatter:
    def __init__(self, place, part, relays, recv, ssem, rsem):
        self.place, self.part, self.relays, self.recv = place, part, relays, recv
        self.ssem, self.rsem = ssem, rsem

    def rows(self, slot, half):
        return pl.ds(UNIT[slot, half], 64)

    def copy(self, k, n):
        part, relays, recv = self.part, self.relays, self.recv
        cols = pl.ds(pl.multiple_of(n * 512, 512), 512)
        src, dst, to = (
            (part.at[self.rows(3, 0), cols], relays.at[0, :, cols], 1),
            (part.at[self.rows(2, 1), cols], recv.at[0, self.rows(0, 1), cols], 1),
            (part.at[self.rows(3, 1), cols], relays.at[1, :, cols], -1),
            (part.at[self.rows(1, 0), cols], recv.at[1, self.rows(0, 0), cols], -1),
            (part.at[self.rows(2, 0), cols], recv.at[0, self.rows(0, 0), cols], 1),
            (part.at[self.rows(1, 1), cols], recv.at[1, self.rows(0, 1), cols], -1),
        )[k]
        sem = k * 4 + n
        return remote(src, dst, self.ssem.at[sem], self.rsem.at[sem], self.place.z(to))

    def start(self, n, *which):
        for k in which:
            self.copy(k, n).start()

    def relay(self, first, last):
        @pl.loop(first, last)
        def _(n):
            cols = pl.ds(pl.multiple_of(n * 512, 512), 512)
            for index, slot, half, out in ((0, 2, 0, 4), (1, 1, 1, 5)):
                self.copy(2 * index, n).wait_recv()
                rows = self.rows(slot, half)
                total = self.part[rows, cols].astype(F32) + self.relays[index, :, cols].astype(F32)
                self.part[rows, cols] = total.astype(BF)
                self.copy(out, n).start()

    def finish(self):
        @pl.loop(0, 4)
        def _(n):
            for k in (1, 3, 4, 5):
                self.copy(k, n).wait_recv()

    def total(self, rows):
        return (
            self.part[rows, :].astype(F32)
            + self.recv[0, rows, :].astype(F32)
            + self.recv[1, rows, :].astype(F32)
        )

    def done(self):
        @pl.loop(0, 4)
        def _(n):
            for k in range(6):
                self.copy(k, n).wait_send()


def sixteen(r):
    return pl.ds(pl.multiple_of(r * 16, 16), 16)


def own_rows(place, r):
    return pl.ds(pl.multiple_of(place.t * 128 + r * 16, 16), 16)


def kernel(names, *refs):
    ref = dict(zip(names, refs))
    place = Place()
    tok, cot, live = ref["tok"], ref["cot"], ref["lengths"]
    wq, wo, wgu, wd = ref["wq"], ref["wo"], ref["wgu"], ref["wd"]
    attn, qkv, probs, ctx = ref["attn"], ref["qkv"], ref["probs"], ref["ctx"]
    middle, mlp, masked, w3 = ref["middle"], ref["mlp"], ref["masked"], ref["w3"]
    pa, pb, branch = w3.at[0], w3.at[1], w3.at[2]
    hid, ggu, gctx, gproj, gmid = ref["hid"], ref["ggu"], ref["gctx"], ref["qkv"], ref["gmid"]
    cos_t, sin_t, gain1, gain2 = ref["cos"], ref["sin"], ref["gain1"], ref["gain2"]
    xa, xa0, xb0, xb1, xb2 = ref["xa"], ref["xa0"], ref["xb0"], ref["xb1"], ref["xb2"]
    r2, final, shares = ref["r2"], ref["final"], ref["shares"]
    gacc, grecv, gsum = ref["gacc"], ref["grecv"], ref["gsum"]
    zs, zr, lsem = ref["zs"], ref["zr"], ref["lsem"]
    live_rows = live[0]

    cot_load = pltpu.make_async_copy(cot, masked.at[0:ROWS], lsem.at[7])
    cot_load.start()

    loads = [pltpu.make_async_copy(ref["wq_h"].at[j], wq.at[:, j * 512 : (j + 1) * 512], lsem.at[j]) for j in range(3)]
    tables = [pltpu.make_async_copy(ref["cos_h"], cos_t, lsem.at[8])]
    tables.append(pltpu.make_async_copy(ref["sin_h"], sin_t, lsem.at[9]))
    loads.append(pltpu.make_async_copy(ref["wo_h"], wo, lsem.at[3]))
    loads += [pltpu.make_async_copy(ref["wgu_h"].at[j], wgu.at[:, j * FF : (j + 1) * FF], lsem.at[4 + j]) for j in range(2)]
    loads.append(pltpu.make_async_copy(ref["wd_h"], wd, lsem.at[6]))
    for load in tables + loads:
        load.start()

    barrier = pltpu.get_barrier_semaphore()
    partners = [place.z(d) for d in (1, 2, 3)]
    partners += [place.xs(d) for d in (1, 2, 3)] + [place.ys(d) for d in (1, 2, 3)] + [place.core()]
    for device in partners:
        pl.semaphore_signal(barrier, inc=1, device_id=device, device_id_type=MESH)

    @pl.loop(0, 8)
    def _(r):
        v = tok[sixteen(r), :].astype(F32)
        inv = lax.rsqrt(jnp.mean(v * v, axis=-1, keepdims=True) + EPS)
        attn[own_rows(place, r), :] = (v * inv * gain1[...]).astype(BF)

    pl.semaphore_wait(barrier, len(partners))

    ag1 = Gather(place, attn, zs.at[0], zr.at[0], False)
    agm = Gather(place, masked, zs.at[1], zr.at[1], True)
    ag2 = Gather(place, mlp, zs.at[2], zr.at[2], True)
    ag4 = Gather(place, branch, zs.at[3], zr.at[3], False)
    rs3 = Scatter(place, pa, ref["relay_a"], ref["recv_a"], zs.at[5], zr.at[5])
    rs4 = Scatter(place, pa, ref["relay_a"], ref["recv_a"], zs.at[6], zr.at[6])
    rs2 = Scatter(place, pb, ref["relay_b"], ref["recv_b"], zs.at[7], zr.at[7])

    ws, wr = ref["ws"], ref["wr"]
    halves = (slice(0, 1024), slice(1024, 2048))
    minor, major = (place.x, place.y), (place.y, place.x)

    def w_rows(half, at, count):
        first = (at * 2 + place.c) * 64
        if count == 16:
            first = first + minor[half] * 16
        return pl.ds(pl.multiple_of(first, 16), count)

    def w_first(half, d):
        rows, k = w_rows(half, major[half], 16), half * 3 + d - 1
        dst = w3.at[d - 1, rows, halves[half]]
        return remote(ref["wo_h"].at[rows, halves[half]], dst, ws.at[k], wr.at[k], place.z(d))

    def w_plane(half, phase, d):
        part = w3.at[:, w_rows(half, major[half], (16, 64)[phase]), halves[half]]
        k = 6 + (phase * 2 + half) * 3 + d - 1
        device = (place.xs, place.ys)[half ^ phase](d)
        return remote(part, part, ws.at[k], wr.at[k], device)

    def w_core(half, d):
        part = w3.at[:, w_rows(half, (major[half] + d) % 4, 64), halves[half]]
        return remote(part, part, ws.at[18 + half * 4 + d], wr.at[18 + half * 4 + d], place.core())

    both = [(half, d) for d in (1, 3, 2) for half in range(2)]
    for half, d in both:
        w_first(half, d).start()
    ag1.start()
    cot_load.wait()

    @pl.loop(0, 8)
    def _(r):
        at = place.t * ROWS + r * 16 + lax.broadcasted_iota(jnp.int32, (16, 1), 0)
        v = masked[sixteen(r), :].astype(F32)
        masked[sixteen(r), :] = jnp.where(at < live_rows, v, 0.0).astype(BF)

    def project(slot):
        block = (place.t + OFFS[slot]) % 4
        rows = pl.ds(pl.multiple_of(block * 128, 128), 128)
        for j in range(3):
            p = nn(attn[rows, :], wq[:, j * 512 : (j + 1) * 512])
            if j == 2:
                qkv[rows, 1024:1536] = p.astype(BF)
                continue
            for h in range(HEADS):
                v = p[:, h * HD : (h + 1) * HD]
                v = v * cos_t[rows, :] + pltpu.roll(v, 64, 1) * sin_t[rows, :]
                if j == 0:
                    v = v * HD ** (-0.5)
                qkv[rows, j * 512 + h * HD : j * 512 + (h + 1) * HD] = v.astype(BF)

    for load in tables + loads[:3]:
        load.wait()
    project(0)
    for half, d in both:
        w_first(half, d).wait_recv()
    for half, d in both:
        w_plane(half, 0, d).start()
    ag1.relay()
    for half, d in both:
        w_plane(half, 0, d).wait_recv()
    for half, d in both:
        w_plane(half, 1, d).start()
    for half in range(2):
        w_core(half, 0).start()
    ag1.near()
    agm.start(0, 2)
    project(1)
    project(2)
    ag1.far()
    project(3)
    for half, d in both[:4]:
        w_plane(half, 1, d).wait_recv()
        w_core(half, 4 - d).start()

    heads = ref["recv_a"].at[0]

    def to_rows(d, pair):
        src = ctx.at[pl.ds(pl.multiple_of(((place.t + d) % 4) * 128, 128), 128), pair * 256 : pair * 256 + 256]
        dst = heads.at[:, pl.ds(pl.multiple_of(place.t * 512 + pair * 256, 256), 256)]
        sem = pair * 3 + d - 1
        return remote(src, dst, zs.at[4, sem], zr.at[4, sem], place.z(d))

    def heads_forward(h):
        def cols(j):
            return pl.ds(pl.multiple_of(j * 512 + h * HD, HD), HD)

        for q in range(2):
            rows, keys = pl.ds(q * 256, 256), (q + 1) * 256
            scores = nt(qkv[rows, cols(0)], qkv[0:keys, cols(1)])
            at = q * 256 + lax.broadcasted_iota(jnp.int32, (256, keys), 0)
            key = lax.broadcasted_iota(jnp.int32, (256, keys), 1)
            scores = jnp.where((key <= at) & (key < live_rows), scores, -1e30)
            e = jnp.exp(scores - jnp.max(scores, axis=-1, keepdims=True))
            p = (e * (1.0 / jnp.sum(e, axis=-1, keepdims=True))).astype(BF)
            probs[h, rows, 0:keys] = p
            ctx[rows, cols(0)] = nn(p, qkv[0:keys, cols(2)]).astype(BF)

    for pair in range(2):
        pl.loop(2 * pair, 2 * pair + 2)(heads_forward)
        for d in (2, 1, 3):
            to_rows(d, pair).start()
    own = pl.ds(pl.multiple_of(place.t * 128, 128), 128)
    heads[:, pl.ds(pl.multiple_of(place.t * 512, 512), 512)] = ctx[own, :]
    for half, d in both[4:]:
        w_plane(half, 1, d).wait_recv()
        w_core(half, 4 - d).start()
    loads[3].wait()
    agm.start(1, 3)

    other = 1 - place.c
    xs, xr = ref["xs"], ref["xr"]

    def swap_a(group):
        src = (masked, mlp, branch, attn)[group]
        return remote(src, xa.at[group], xs.at[group], xr.at[group], place.core())

    def swap_branch(slot):
        block = (place.t + OFFS[slot]) % 4
        rows = pl.ds(pl.multiple_of(block * 128, 128), 128)
        sem = (2, 15, 16, 17)[slot]
        return remote(branch.at[rows], xa.at[2, rows], xs.at[sem], xr.at[sem], place.core())

    def swap_masked(part):
        rows = (slice(0, 384), slice(384, 512))[part]
        sem = (0, 14)[part]
        return remote(masked.at[rows], xa0.at[rows], xs.at[sem], xr.at[sem], place.core())

    def swap_b(k):
        rows = pl.ds((0, 256, 0, 256, 0, 0)[k], 256 if k < 4 else 512)
        if k < 2:
            src = hid.at[rows, pl.ds(pl.multiple_of(other * 640, 128), 768)]
        elif k < 4:
            src = ggu.at[rows, pl.ds(pl.multiple_of(other * FF, 128), FF)]
        elif k == 4:
            src = ctx.at[rows, pl.ds(pl.multiple_of(other * 256, 256), 256)]
        else:
            src = gproj.at[rows, pl.ds(pl.multiple_of(other * 768, 256), 768)]
        dst = (xb0, xb0, xb1, xb1, xb2, xb0)[k].at[rows]
        return remote(src, dst, xs.at[4 + k], xr.at[4 + k], place.core())

    swap_a(3).start()
    swap_b(4).start()

    for half in range(2):
        for d in range(4):
            w_core(half, d).wait_recv()
    w3_keep = pltpu.make_async_copy(w3, ref["w3_h"], lsem.at[8])
    w3_keep.start()
    for pair in range(2):
        for d in (1, 2, 3):
            to_rows(d, pair).wait_recv()

    @pl.loop(0, 4)
    def _(n):
        at = pl.ds(pl.multiple_of(n * 512, 512), 512)

        def share(d, weights):
            return nn(heads[:, pl.ds(pl.multiple_of(((place.t + d) % 4) * 512, 512), 512)], weights)

        out = share(0, wo[:, at]) + share(3, w3[0, :, at]) + share(2, w3[1, :, at]) + share(1, w3[2, :, at])
        middle[:, at] = tok[:, at].astype(F32) + out

    @pl.loop(0, 8)
    def _(r):
        rows = sixteen(r)
        v = middle[rows, :]
        inv = lax.rsqrt(jnp.mean(v * v, axis=-1, keepdims=True) + EPS)
        mlp[rows, :] = (v * inv * gain2[...]).astype(BF)

    for pair in range(2):
        for d in (1, 2, 3):
            to_rows(d, pair).wait_send()
    for half, d in both:
        w_first(half, d).wait_send()
        w_plane(half, 0, d).wait_send()
        w_plane(half, 1, d).wait_send()
    for half in range(2):
        for d in range(4):
            w_core(half, d).wait_send()
    ag2.start()
    for load in loads[4:]:
        load.wait()

    own_b = (
        hid.at[:, pl.ds(pl.multiple_of(place.c * 640, 128), 768)],
        ggu.at[:, pl.ds(pl.multiple_of(place.c * FF, 128), FF)],
        ctx.at[:, pl.ds(pl.multiple_of(place.c * 256, 256), 256)],
        gproj.at[:, pl.ds(pl.multiple_of(place.c * 768, 256), 768)],
    )
    own_a = (masked, mlp, branch, attn)
    other_a = (xa0, pb, wd.at[0:512], wd.at[512:1024])
    other_b = (xb0, xb1, xb2, xb0)
    osem = ref["osem"]

    def bring(group):
        return pltpu.make_async_copy(xa.at[group], other_a[group], osem.at[group])

    def fetch(group):
        if group == 2:
            for slot in range(1, 4):
                swap_branch(slot).wait_recv()
        else:
            swap_a(group).wait_recv()
        bring(group).start()

    def piece(group, axis, tile, first, count):
        if group == 3 and axis == 1:
            return mlp.at[pl.ds(first, count), pl.ds(pl.multiple_of(tile * 384, 128), 384)]
        base = (FF, 0, FF + 768, FF + 1024)[group]
        lo = base if axis == 0 else base + CX[group]
        width = CX[group] if axis == 0 else CY[group]
        rows = pl.ds(pl.multiple_of(tile * 512 + first, min(count, 128)), count)
        return wgu.at[rows, lo : lo + width]

    p1xs, p1xr, p1ys, p1yr = ref["p1xs"], ref["p1xr"], ref["p1ys"], ref["p1yr"]

    def relayed(group, axis):
        if group < 2:
            return ref[("relx", "rely")[axis] + str(group)]
        lo = ((768, 896), (0, 384))[group - 2][axis]
        return xb1.at[:, lo : lo + CX[group]]

    def arrived(group, axis, side):
        if group < 2:
            return ref[("recx", "recy")[axis] + str(group)].at[side]
        width = CX[group]
        lo = ((1536, 1792), (0, 768))[group - 2][axis] + side * width
        return xa0.at[:, pl.ds(lo if isinstance(lo, int) else pl.multiple_of(lo, 128), width)]

    def tile_of(step):
        return (place.y + jnp.where(step == 0, 2, jnp.where(step == 1, 1, jnp.where(step == 2, 3, 0)))) % 4

    def send_x(group, kind, step):
        tile, to = tile_of(step), 1 - 2 * (step % 2)
        rows = pl.ds(pl.multiple_of(tile * 128, 128), 128)
        if kind == 0:
            block, dst = place.x + 2, relayed(group, 0).at[rows]
        elif kind == 1:
            block, dst, to = place.x + 4 - to, arrived(group, 0, (1 + to) // 2).at[rows], -to
        else:
            block, dst = place.x + 4 + to, arrived(group, 0, (1 - to) // 2).at[rows]
        src = piece(group, 0, tile, pl.multiple_of((block % 4) * 128, 128), 128)
        sem = (group * 3 + kind) * 4 + step
        return remote(src, dst, p1xs.at[sem], p1xr.at[sem], place.xs(4 + to))

    def send_y(group, k):
        offset, first, dst, to = (
            (2, 0, relayed(group, 1).at[0:256], 1),
            (1, 256, arrived(group, 1, 0).at[256:512], 1),
            (2, 256, relayed(group, 1).at[256:512], 3),
            (3, 0, arrived(group, 1, 1).at[0:256], 3),
            (1, 0, arrived(group, 1, 0).at[0:256], 1),
            (3, 256, arrived(group, 1, 1).at[256:512], 3),
        )[k]
        src = piece(group, 1, (place.y + offset) % 4, first, 256)
        return remote(src, dst, p1ys.at[group * 6 + k], p1yr.at[group * 6 + k], place.ys(to))

    def gradient(group, step):
        tile = tile_of(step)
        at = pl.ds(pl.multiple_of(tile * 512, 512), 512)
        lo = 0
        for axis, width in ((0, CX[group]), (1, CY[group])):
            own, oth = own_b[group].at[:, lo : lo + width], other_b[group].at[:, lo : lo + width]
            out = tn(own_a[group][:, at], own[...]) + tn(other_a[group][:, at], oth[...])
            piece(group, axis, tile, 0, 512)[...] = out.astype(BF)
            lo += width
        send_x(group, 0, step).start()

        @pl.when(step == 0)
        def _():
            send_y(group, 0).start()
            send_y(group, 2).start()

    def near_x(group, step):
        send_x(group, 1, step).start()

    def near_y(group, step):
        for when in (1, 2):

            @pl.when(step == when)
            def _():
                send_y(group, 2 * when - 1).start()

    def all_near(group, *axes):
        @pl.loop(0, 4)
        def _(step):
            for axis in axes:
                (near_x, near_y)[axis](group, step)

    lands = ref["lands"]

    def mid_copies(group):
        if group > 1:
            return ()
        return (
            pltpu.make_async_copy(relayed(group, 0), hid.at[:, 0 : CX[group]], lands.at[16 + group]),
            pltpu.make_async_copy(relayed(group, 1), hid.at[:, 768 : 768 + CY[group]], lands.at[20 + group]),
        )

    def mid_start(group):
        for step in range(4):
            send_x(group, 0, step).wait_recv()
        for k in (0, 2):
            send_y(group, k).wait_recv()
        for copy in mid_copies(group):
            copy.start()

    def mid_end(group):
        for copy in mid_copies(group):
            copy.wait()

        def add(axis, tile, first, rows, lo, width, count):
            src = hid.at[:, lo : lo + width] if group < 2 else relayed(group, axis)

            @pl.loop(0, count // 32)
            def _(i):
                own = piece(group, axis, tile, pl.multiple_of(first + i * 32, 32), 32)
                got = src[pl.ds(pl.multiple_of(rows + i * 32, 32), 32), :]
                own[...] = (own[...].astype(F32) + got.astype(F32)).astype(BF)

        for step in range(4):
            to, tile = (1, 3)[step % 2], tile_of(step)
            add(0, tile, ((place.x + to) % 4) * 128, tile * 128, 0, CX[group], 128)
            send_x(group, 2, step).start()
        for k, offset, first in ((4, 1, 0), (5, 3, 256)):
            add(1, (place.y + offset) % 4, first, first, 768, CY[group], 256)
            send_y(group, k).start()

    def feed(first, count):
        rows = slice(first, first + count)
        for n0, n1 in ((0, 512), (512, 1024), (1024, 1408)):
            gate = nn(mlp[rows, :], wgu[:, n0:n1])
            up = nn(mlp[rows, :], wgu[:, FF + n0 : FF + n1])
            sig = jax.nn.sigmoid(gate)
            silu = gate * sig
            hid[rows, n0:n1] = (silu * up).astype(BF)
            ggu[rows, n0:n1] = (up * sig * (1.0 + gate * (1.0 - sig))).astype(BF)
            ggu[rows, FF + n0 : FF + n1] = silu.astype(BF)

    def feed_back(first, count):
        rows = slice(first, first + count)
        for n0, n1 in ((0, 512), (512, 1024), (1024, 1408)):
            grad = nt(masked[rows, :], wd[n0:n1, :])
            for lo in (0, FF):
                ggu[rows, lo + n0 : lo + n1] = (grad * ggu[rows, lo + n0 : lo + n1].astype(F32)).astype(BF)

    def feed_part(first, count, *sends):
        rows = slice(first, first + count)

        @pl.loop(0, 4)
        def _(n):
            at = pl.ds(pl.multiple_of(n * 512, 512), 512)
            rs3.part[rows, at] = nt(ggu[rows, :], wgu[at, :]).astype(BF)
            rs3.start(n, *sends)

    feed(0, 128)
    feed_back(0, 128)
    w3_keep.wait()
    feed_part(0, 128)
    w3_back = []
    for j in range(3):
        rows, cols = slice(j * 512, (j + 1) * 512), slice(j * 512, (j + 1) * 512)
        kept = ref["w3_h"].at[j]
        w3_back.append(pltpu.make_async_copy(kept.at[:, 0:1536], wq.at[rows], osem.at[4 + j]))
        w3_back.append(pltpu.make_async_copy(kept.at[:, 1536:2048], wq.at[1536:2048, cols], osem.at[7 + j]))
    for copy in w3_back:
        copy.start()
    ag2.relay()
    agm.near()
    agm.relay()
    swap_masked(0).start()
    feed(128, 128)
    feed_back(128, 128)
    feed_part(128, 128, 1, 3)
    swap_b(0).start()
    swap_b(2).start()
    ag2.near()
    ag2.far()
    swap_a(1).start()
    feed(256, 256)
    swap_b(1).start()
    agm.far()
    swap_masked(1).start()
    feed_back(256, 256)
    swap_b(3).start()
    fetch(1)
    late, taken = slice(256, 512), slice(FF, FF + COLS[0])

    @pl.loop(0, 4)
    def _(n):
        at = pl.ds(pl.multiple_of(n * 512, 512), 512)
        rs3.part[late, at] = nt(ggu[late, taken], wgu[at, taken]).astype(BF)

    swap_b(0).wait_recv()
    swap_b(1).wait_recv()
    swap_masked(0).wait_recv()
    swap_masked(1).wait_recv()

    @pl.loop(0, 2)
    def _(step):
        gradient(0, step)
        near_x(0, step)
        near_y(0, step)

    @pl.loop(0, 4)
    def _(n):
        at = pl.ds(pl.multiple_of(n * 512, 512), 512)
        part = nt(ggu[late, 0:FF], wgu[at, 0:FF]) + nt(ggu[late, FF + COLS[0] :], wgu[at, FF + COLS[0] :])
        rs3.part[late, at] = (part + rs3.part[late, at].astype(F32)).astype(BF)
        rs3.start(n, 0, 2)

    @pl.loop(2, 4)
    def _(step):
        gradient(0, step)
        near_x(0, step)
        near_y(0, step)

    rs3.relay(0, 3)
    bring(1).wait()
    swap_b(2).wait_recv()
    swap_b(3).wait_recv()

    def gate_up(step):
        gradient(1, step)
        near_x(1, step)
        near_y(1, step)

    gate_up(0)
    rs3.relay(3, 4)
    pl.loop(1, 3)(gate_up)
    p2xs, p2xr, p2ys, p2yr = ref["p2xs"], ref["p2xr"], ref["p2ys"], ref["p2yr"]

    def landing(group):
        copies = []
        for d in range(2 if group < 2 else 0):
            for axis in range(2):
                lo = d * FF + axis * 768
                width = CX[group] if axis == 0 else CY[group]
                sem = lands.at[group * 4 + d * 2 + axis]
                copies.append(pltpu.make_async_copy(arrived(group, axis, d), ggu.at[:, lo : lo + width], sem))
        return copies

    def send_2(group, axis, d):
        sem = group * 3 + d - 1
        own = pl.multiple_of(place.x * 128, 128)
        if axis == 0:
            src = piece(group, 0, (place.y + d) % 4, own, 128)
            dst = r2.at[d - 1, :, BASE[group] : BASE[group] + CX[group]]
            return remote(src, dst, p2xs.at[sem], p2xr.at[sem], place.ys(d))
        src = piece(group, 1, place.y, pl.multiple_of(((place.x + d) % 4) * 128, 128), 128)
        dst = r2.at[d - 1, :, BASE[group] + CX[group] : BASE[group] + COLS[group]]
        return remote(src, dst, p2ys.at[sem], p2yr.at[sem], place.xs(d))

    def land(group):
        for step in range(4):
            for kind in (1, 2):
                send_x(group, kind, step).wait_recv()
        for k in (1, 3, 4, 5):
            send_y(group, k).wait_recv()
        for copy in landing(group):
            copy.start()

    def first_sum(group):
        for copy in landing(group):
            copy.wait()
        for axis in range(2):
            lo = axis * 768
            width = CX[group] if axis == 0 else CY[group]
            if group < 2:
                got = [ggu.at[:, d * FF + lo : d * FF + lo + width] for d in range(2)]
            else:
                got = [arrived(group, axis, d) for d in range(2)]

            @pl.loop(0, 16)
            def _(i):
                if axis == 0:
                    own = piece(group, 0, i // 4, pl.multiple_of(place.x * 128 + (i % 4) * 32, 32), 32)
                else:
                    own = piece(group, 1, place.y, pl.multiple_of(i * 32, 32), 32)
                rows = pl.ds(pl.multiple_of(i * 32, 32), 32)
                total = own[...].astype(F32)
                for d in range(2):
                    total = total + got[d][rows, :].astype(F32)
                own[...] = total.astype(BF)

            for d in (2, 1, 3):
                send_2(group, axis, d).start()

    def whole_of(group):
        return ((final, 0), (middle, 0), (final, 768), (final, 1024))[group]

    def ending(group):
        ref_at, first = whole_of(group)
        cols = slice(first, first + COLS[group])
        mine = ref_at.at[pl.ds(pl.multiple_of(place.c * 64, 64), 64), cols]
        theirs = ref_at.at[pl.ds(pl.multiple_of(other * 64, 64), 64), cols]
        dst = shares.at[place.c, :, BASE[group] : BASE[group] + COLS[group]]
        return (
            remote(theirs, dst, xs.at[10 + group], xr.at[10 + group], place.core()),
            pltpu.make_async_copy(mine, dst, lsem.at[9 + group]),
        )

    def second_sum(group):
        for axis in range(2):
            for d in (1, 2, 3):
                send_2(group, axis, d).wait_recv()
            lo = BASE[group] + (0 if axis == 0 else CX[group])
            width = CX[group] if axis == 0 else CY[group]
            whole, first = whole_of(group)
            first += lo - BASE[group]

            @pl.loop(0, 4)
            def _(i):
                rows = pl.ds(pl.multiple_of(i * 32, 32), 32)
                own = piece(group, axis, place.y, pl.multiple_of(place.x * 128 + i * 32, 32), 32)
                total = own[...].astype(F32)
                for d in range(3):
                    total = total + r2[d, rows, lo : lo + width].astype(F32)
                whole[rows, first : first + width] = total
        for copy in ending(group):
            copy.start()

    rs3.finish()

    def fold(v):
        return jnp.concatenate([v[:, i * 512 : (i + 1) * 512] for i in range(4)], axis=0)

    def mlp_back(r, total):
        rows = sixteen(r)
        grad = rs3.total(rows)
        v = middle[rows, :]
        inv = lax.rsqrt(jnp.mean(v * v, axis=-1, keepdims=True) + EPS)
        scaled = grad * gain2[...]
        back = (
            masked[rows, :].astype(F32)
            + inv * scaled
            - v * (inv * inv * inv) * jnp.mean(v * scaled, axis=-1, keepdims=True)
        )
        gmid[rows, :] = back
        branch[own_rows(place, r), :] = back.astype(BF)
        return total + jnp.sum(grad * v * inv, axis=0, keepdims=True)

    gain2_part = lax.fori_loop(0, 8, mlp_back, jnp.zeros((1, D), F32))
    gacc[0, 4:8, :] = fold(gain2_part)
    agm.done()
    swap_masked(0).wait_send()
    swap_masked(1).wait_send()
    for copy in w3_back:
        copy.wait()
    own = pl.ds(pl.multiple_of(place.t * 128, 128), 128)

    def to_heads(j):
        src = masked.at[128:256, j * 512 : (j + 1) * 512]
        return remote(src, gctx.at[own], zs.at[4, 6 + j], zr.at[4, 6 + j], place.z(3 - j))

    for j in (1, 0, 2):
        at = slice(j * 512, (j + 1) * 512)
        part = nt(branch[own, 0:1536], wq[at, :]) + nt(branch[own, 1536:2048], wq[1536:2048, at])
        masked[128:256, at] = part.astype(BF)
        to_heads(j).start()
    gctx[own, :] = nt(branch[own, :], wo[...]).astype(BF)
    ag4.start()
    for load in loads[:3]:
        load.start()
    swap_branch(0).start()
    rs3.done()

    gate_up(3)

    @pl.loop(0, 4)
    def _(n):
        at = pl.ds(pl.multiple_of(n * 512, 512), 512)
        rs2.part[:, at] = nn(hid[...], wd[:, at]).astype(BF)

    fetch(3)
    for k in (0, 1, 2, 3):
        swap_b(k).wait_send()
    mid_start(0)
    mid_end(0)
    mid_start(1)
    mid_end(1)
    ag4.relay()
    for pair in ((0, 2), (1, 3)):

        @pl.loop(0, 4)
        def _(n):
            rs2.start(n, *pair)

    for j in range(3):
        to_heads(j).wait_recv()

    def turn_back(v, rows):
        return v * cos_t[rows, :] - pltpu.roll(v, 64, 1) * sin_t[rows, :]

    def heads_back(h):
        def cols(j):
            return pl.ds(pl.multiple_of(j * 512 + h * HD, HD), HD)

        def part(q):
            rows, keys = pl.ds(q * 256, 256), (q + 1) * 256
            p = probs[h, rows, 0:keys]
            grad = gctx[rows, cols(0)]
            wide = p.astype(F32)
            gp = nt(grad, qkv[0:keys, cols(2)])
            gs = (wide * (gp - jnp.sum(wide * gp, axis=-1, keepdims=True))).astype(BF)
            gq = (turn_back(nn(gs, qkv[0:keys, cols(1)]), rows) * HD ** (-0.5)).astype(BF)
            return gq, tn(gs, qkv[rows, cols(0)]), tn(p, grad)

        q1, k1, v1 = part(1)
        q0, k0, v0 = part(0)
        lo, hi = slice(0, 256), slice(256, 512)
        k0, k1 = turn_back(k0 + k1[lo], lo).astype(BF), turn_back(k1[hi], hi).astype(BF)
        v0, v1 = (v0 + v1[lo]).astype(BF), v1[hi].astype(BF)
        for j, low, high in ((0, q0, q1), (1, k0, k1), (2, v0, v1)):
            gproj[lo, cols(j)] = low
            gproj[hi, cols(j)] = high

    pl.loop(0, HEADS)(heads_back)
    swap_branch(0).wait_recv()
    swap_b(5).start()
    land(0)
    for load in loads[:3]:
        load.wait()
    first_sum(0)
    swap_a(1).wait_send()
    ag2.done()
    bring(3).wait()
    swap_b(5).wait_recv()

    @pl.loop(0, 4)
    def _(step):
        gradient(3, step)

    all_near(3, 0, 1)
    ag4.near()
    ag4.far()
    for slot in (1, 2, 3):
        swap_branch(slot).start()
    @pl.loop(0, 4)
    def _(n):
        at = pl.ds(pl.multiple_of(n * 512, 512), 512)
        part = nt(in_order(place, gproj, slice(None)), wq[at, :])
        rs4.part[:, at] = part.astype(BF)
        seen = jnp.sum(part * in_order(place, attn, at).astype(F32), axis=0, keepdims=True)
        gsum[n] = jnp.broadcast_to(seen, (8, 512))

    for n in range(4):
        at = slice(n * 512, (n + 1) * 512)
        gacc[0, n : n + 1, :] = gsum[n, 0:1, :] / gain1[:, at]
    gs, gr = ref["gs"], ref["gr"]

    def spread(stage):
        count = 2 if stage == 3 else 4
        me = (place.t, place.x, place.y, place.c)[stage]
        out = []
        for d in range(1, count):
            device = (place.z, place.xs, place.ys, lambda _: place.core())[stage](d)
            k = stage * 3 + d - 1
            out.append(remote(gacc.at[stage], grecv.at[stage * 4 + me], gs.at[k], gr.at[k], device))
        return out, count, me

    def spread_start(stage):
        copies, _, me = spread(stage)
        grecv[stage * 4 + me] = gacc[stage]
        for copy in copies:
            copy.start()

    def spread_end(stage):
        copies, count, _ = spread(stage)
        for copy in copies:
            copy.wait_recv()
        total = grecv[stage * 4]
        for i in range(1, count):
            total = total + grecv[stage * 4 + i]
        gacc[stage + 1] = total

    spread_start(0)
    rs2.relay(0, 4)

    for pair in ((0, 2), (1, 3)):

        @pl.loop(0, 4)
        def _(n):
            rs4.start(n, *pair)

    fetch(2)
    mid_start(3)
    mid_end(3)
    swap_b(4).wait_recv()
    bring(2).wait()

    @pl.loop(0, 4)
    def _(step):
        gradient(2, step)

    all_near(2, 0, 1)
    spread_end(0)
    spread_start(1)
    land(1)
    first_sum(1)
    mid_start(2)
    mid_end(2)
    spread_end(1)
    spread_start(2)
    land(3)
    first_sum(3)
    rs4.relay(0, 4)
    rs2.finish()

    @pl.loop(0, 8)
    def _(r):
        rows = sixteen(r)
        middle[rows, :] = middle[rows, :] + rs2.total(rows)

    out_copy = pltpu.make_async_copy(middle, ref["output"], lsem.at[7])
    out_copy.start()
    second_sum(0)
    spread_end(2)
    spread_start(3)
    land(2)
    first_sum(2)
    out_copy.wait()
    second_sum(1)
    rs4.finish()

    @pl.loop(0, 8)
    def _(r):
        rows = sixteen(r)
        grad = rs4.total(rows)
        v = tok[rows, :].astype(F32)
        inv = lax.rsqrt(jnp.mean(v * v, axis=-1, keepdims=True) + EPS)
        scaled = grad * gain1[...]
        gmid[rows, :] = (
            gmid[rows, :]
            + inv * scaled
            - v * (inv * inv * inv) * jnp.mean(v * scaled, axis=-1, keepdims=True)
        )

    tok_copy = pltpu.make_async_copy(gmid, ref["grad_tokens"], lsem.at[8])
    tok_copy.start()
    spread_end(3)
    ref["gains"][...] = gacc[4]
    second_sum(3)
    second_sum(2)

    for j in range(3):
        to_heads(j).wait_send()
    for gather in (ag1, ag4):
        gather.done()
    rs4.done()
    rs2.done()
    swap_a(3).wait_send()
    for slot in range(4):
        swap_branch(slot).wait_send()
    for k in (4, 5):
        swap_b(k).wait_send()
    for group in range(4):
        for step in range(4):
            for kind in range(3):
                send_x(group, kind, step).wait_send()
        for k in range(6):
            send_y(group, k).wait_send()
        for d in (1, 2, 3):
            for axis in range(2):
                send_2(group, axis, d).wait_send()
    for stage in range(4):
        for copy in spread(stage)[0]:
            copy.wait_send()
    tok_copy.wait()
    for group in range(4):
        for copy in ending(group):
            copy.wait()


def block(tokens, gain_attn, w_qkv, w_out, gain_mlp, w_gate_up, w_down, cotangent, lengths):
    cos_t, sin_t = rotary_tables()
    vmem = pl.BlockSpec(memory_space=pltpu.VMEM)
    smem = pl.BlockSpec(memory_space=pltpu.SMEM)
    hbm = pl.BlockSpec(memory_space=pl.ANY)
    ins = [
        ("tok", tokens, vmem),
        ("gain1", gain_attn.reshape(1, D), vmem),
        ("wq_h", w_qkv, hbm),
        ("wo_h", w_out, hbm),
        ("gain2", gain_mlp.reshape(1, D), vmem),
        ("wgu_h", w_gate_up, hbm),
        ("wd_h", w_down, hbm),
        ("cot", cotangent, hbm),
        ("lengths", lengths, smem),
        ("cos_h", jnp.asarray(cos_t), hbm),
        ("sin_h", jnp.asarray(sin_t), hbm),
    ]
    outs = [
        ("output", (ROWS, D), F32, hbm),
        ("grad_tokens", (ROWS, D), F32, hbm),
        ("gains", (8, 512), F32, vmem),
        ("shares", (2, 64, ALL), F32, hbm),
        ("xa", (4, SEQ, D), BF, hbm),
        ("w3_h", (3, SEQ, D), BF, hbm),
    ]
    outs += [(f"relx{g}", (SEQ, CX[g]), BF, hbm) for g in range(2)]
    outs += [(f"rely{g}", (SEQ, CY[g]), BF, hbm) for g in range(2)]
    outs += [(f"recx{g}", (2, SEQ, CX[g]), BF, hbm) for g in range(2)]
    outs += [(f"recy{g}", (2, SEQ, CY[g]), BF, hbm) for g in range(2)]
    dma = pltpu.SemaphoreType.DMA
    scratch = [
        ("wq", pltpu.VMEM((D, 1536), BF)),
        ("wo", pltpu.VMEM((512, D), BF)),
        ("wgu", pltpu.VMEM((D, 2 * FF), BF)),
        ("wd", pltpu.VMEM((FF, D), BF)),
        ("attn", pltpu.VMEM((SEQ, D), BF)),
        ("qkv", pltpu.VMEM((SEQ, 1536), BF)),
        ("probs", pltpu.VMEM((HEADS, SEQ, SEQ), BF)),
        ("ctx", pltpu.VMEM((SEQ, 512), BF)),
        ("middle", pltpu.VMEM((ROWS, D), F32)),
        ("mlp", pltpu.VMEM((SEQ, D), BF)),
        ("masked", pltpu.VMEM((SEQ, D), BF)),
        ("hid", pltpu.VMEM((SEQ, FF), BF)),
        ("ggu", pltpu.VMEM((SEQ, 2 * FF), BF)),
        ("gctx", pltpu.VMEM((SEQ, 512), BF)),
        ("xa0", pltpu.VMEM((SEQ, D), BF)),
        ("xb0", pltpu.VMEM((SEQ, COLS[0]), BF)),
        ("xb1", pltpu.VMEM((SEQ, COLS[1]), BF)),
        ("xb2", pltpu.VMEM((SEQ, COLS[2]), BF)),
        ("gmid", pltpu.VMEM((ROWS, D), F32)),
        ("w3", pltpu.VMEM((3, SEQ, D), BF)),
        ("relay_a", pltpu.VMEM((2, 64, D), BF)),
        ("recv_a", pltpu.VMEM((2, ROWS, D), BF)),
        ("relay_b", pltpu.VMEM((2, 64, D), BF)),
        ("recv_b", pltpu.VMEM((2, ROWS, D), BF)),
        ("r2", pltpu.VMEM((3, ROWS, ALL), BF)),
        ("final", pltpu.VMEM((ROWS, 1792), F32)),
        ("gacc", pltpu.VMEM((5, 8, 512), F32)),
        ("cos", pltpu.VMEM((SEQ, HD), F32)),
        ("sin", pltpu.VMEM((SEQ, HD), F32)),
        ("gsum", pltpu.VMEM((4, 8, 512), F32)),
        ("grecv", pltpu.VMEM((14, 8, 512), F32)),
        ("zs", dma((8, 24))),
        ("zr", dma((8, 24))),
        ("lsem", dma((13,))),
        ("osem", dma((10,))),
        ("xs", dma((18,))),
        ("xr", dma((18,))),
        ("p1xs", dma((48,))),
        ("p1xr", dma((48,))),
        ("p1ys", dma((24,))),
        ("p1yr", dma((24,))),
        ("p2xs", dma((12,))),
        ("p2xr", dma((12,))),
        ("p2ys", dma((12,))),
        ("p2yr", dma((12,))),
        ("lands", dma((24,))),
        ("gs", dma((10,))),
        ("ws", dma((26,))),
        ("wr", dma((26,))),
        ("gr", dma((10,))),
    ]
    names = [i[0] for i in ins] + [o[0] for o in outs] + [s[0] for s in scratch]
    results = pl.pallas_call(
        functools.partial(kernel, names),
        out_shape=[jax.ShapeDtypeStruct(o[1], o[2]) for o in outs],
        in_specs=[i[2] for i in ins],
        out_specs=[o[3] for o in outs],
        scratch_shapes=[s[1] for s in scratch],
        compiler_params=pltpu.CompilerParams(
            collective_id=0, has_side_effects=True, vmem_limit_bytes=63 * 1024 * 1024
        ),
        name="block",
    )(*[i[1] for i in ins])
    return arrange(*results[:4])


def arrange_kernel(out_in, tok_in, gains, shares, output, grad_tokens, gain1, qkv, out, gain2, gate_up, down, *scratch):
    out_v, tok_v, shares_v, sem = scratch
    down_at, gu_at, out_at, qkv_at = BASE

    def columns(core, first, count):
        return shares_v.at[core, :, first : first + count]

    def through(src, buf, dst, half):
        rows = slice(half * 64, half * 64 + 64)
        return (src.at[rows], buf.at[rows]), ((buf.at[rows], dst.at[rows]),)

    def of_shares(first, count, *stores):
        cols = slice(first, first + count)
        return (shares.at[:, :, cols], shares_v.at[:, :, cols]), stores

    moves = (
        through(out_in, out_v, output, 0),
        through(out_in, out_v, output, 1),
        through(tok_in, tok_v, grad_tokens, 0),
        through(tok_in, tok_v, grad_tokens, 1),
        of_shares(gu_at, FF, (columns(0, gu_at, FF), gate_up.at[0]), (columns(1, gu_at, FF), gate_up.at[1])),
        of_shares(
            qkv_at,
            768,
            (columns(0, qkv_at, 512), qkv.at[0]),
            (columns(0, qkv_at + 512, 256), qkv.at[1, :, 0:256]),
            (columns(1, qkv_at, 256), qkv.at[1, :, 256:512]),
            (columns(1, qkv_at + 256, 512), qkv.at[2]),
        ),
        of_shares(
            down_at,
            768,
            (columns(0, down_at, 768), down.at[:, 0:768]),
            (columns(1, down_at + 128, 640), down.at[:, 768:1408]),
        ),
        of_shares(
            out_at,
            256,
            (columns(0, out_at, 256), out.at[:, 0:256]),
            (columns(1, out_at, 256), out.at[:, 256:512]),
        ),
    )
    loads = [pltpu.make_async_copy(*move[0], sem.at[i]) for i, move in enumerate(moves)]
    for load in loads:
        load.start()
    for i in range(4):
        at = slice(i * 512, (i + 1) * 512)
        gain1[:, at] = gains[i : i + 1, :]
        gain2[:, at] = gains[4 + i : 5 + i, :]
    stores = []
    for load, move in zip(loads, moves):
        load.wait()
        for src, dst in move[1]:
            stores.append(pltpu.make_async_copy(src, dst, sem.at[len(moves) + len(stores)]))
            stores[-1].start()
    for store in stores:
        store.wait()


def arrange(output, grad_tokens, gains, shares):
    vmem = pl.BlockSpec(memory_space=pltpu.VMEM)
    hbm = pl.BlockSpec(memory_space=pl.ANY)
    outs = (
        ((ROWS, D), hbm),
        ((ROWS, D), hbm),
        ((1, D), vmem),
        ((3, 64, 512), hbm),
        ((64, 512), hbm),
        ((1, D), vmem),
        ((2, 64, FF), hbm),
        ((64, FF), hbm),
    )
    results = pl.pallas_call(
        arrange_kernel,
        out_shape=[jax.ShapeDtypeStruct(o[0], F32) for o in outs],
        in_specs=[hbm, hbm, vmem, hbm],
        out_specs=[o[1] for o in outs],
        scratch_shapes=[
            pltpu.VMEM((ROWS, D), F32),
            pltpu.VMEM((ROWS, D), F32),
            pltpu.VMEM((2, 64, ALL), F32),
            pltpu.SemaphoreType.DMA((22,)),
        ],
        compiler_params=pltpu.CompilerParams(vmem_limit_bytes=63 * 1024 * 1024),
        name="arrange",
    )(output, grad_tokens, gains, shares)
    output, grad_tokens, gain1, qkv, out, gain2, gate_up, down = results
    return output, grad_tokens, gain1.reshape(D), qkv, out.T, gain2.reshape(D), gate_up, down.T


def solution(mesh):
    placed = (
        P(("dp", "tensor"), None),
        P(),
        P(None, None, "tensor"),
        P("tensor", None),
        P(),
        P(None, None, "tensor"),
        P("tensor", None),
        P(("dp", "tensor"), None),
        P("dp"),
    )
    return jax.shard_map(
        block,
        mesh=mesh,
        in_specs=placed,
        out_specs=(
            P(("dp", "tensor"), None),
            P(("dp", "tensor"), None),
            P(),
            P(None, "dp", "tensor"),
            P("tensor", "dp"),
            P(),
            P(None, "dp", "tensor"),
            P("tensor", "dp"),
        ),
        check_vma=False,
    )
```

```python
import functools
import math

import jax
import jax.numpy as jnp
import numpy as np
from jax import lax
from jax.experimental import pallas as pl
from jax.experimental.pallas import tpu as pltpu
from jax.sharding import PartitionSpec as P

D = 2048
HD = 128
FF = 1408
ROWS = 128
SEQ = 512
HEADS = 4
EPS = 1e-05
BF = jnp.bfloat16
F32 = jnp.float32
MESH = pl.DeviceIdType.MESH
OFFS = (0, 3, 1, 2)
ORDER = ((0, 0), (0, 1), (1, 0), (2, 1), (1, 1), (2, 0), (3, 0), (3, 1))
UNIT = {half: i * 64 for i, half in enumerate(ORDER)}

CX = (384, 768, 128, 384)
CY = (384, 640, 128, 384)
COLS = tuple(a + b for a, b in zip(CX, CY))
BASE = (0, 768, 2176, 2432)
ALL = 3200


def nn(a, b):
    return lax.dot_general(a, b, (((1,), (0,)), ((), ())), preferred_element_type=F32)


def nt(a, b):
    return lax.dot_general(a, b, (((1,), (1,)), ((), ())), preferred_element_type=F32)


def tn(a, b):
    return lax.dot_general(a, b, (((0,), (0,)), ((), ())), preferred_element_type=F32)


def rotary_tables():
    half = HD // 2
    freq = np.exp(np.arange(half, dtype=np.float64) * (-2.0 * math.log(10000.0) / HD))
    angles = np.arange(SEQ, dtype=np.float64)[:, None] * freq
    cos, sin = np.cos(angles), np.sin(angles)
    return (
        np.concatenate([cos, cos], axis=1).astype(np.float32),
        np.concatenate([-sin, sin], axis=1).astype(np.float32),
    )


class Place:
    def __init__(self):
        self.dp = lax.axis_index("dp")
        self.t = lax.axis_index("tensor")
        self.c = self.dp % 2
        self.x = (self.dp // 2) % 4
        self.y = self.dp // 8

    def z(self, d):
        return (self.dp, (self.t + d) % 4)

    def xs(self, d):
        return (self.y * 8 + ((self.x + d) % 4) * 2 + self.c, self.t)

    def ys(self, d):
        return (((self.y + d) % 4) * 8 + self.x * 2 + self.c, self.t)

    def core(self):
        return (self.dp + 1 - 2 * self.c, self.t)


def remote(src, dst, ssem, rsem, device):
    return pltpu.make_async_remote_copy(
        src_ref=src, dst_ref=dst, send_sem=ssem, recv_sem=rsem, device_id=device, device_id_type=MESH
    )


def half_rows(place, slot, half):
    block = (place.t + OFFS[slot]) % 4
    return pl.ds(pl.multiple_of(block * 128 + half * 64, 64), 64)


def in_order(place, ref, cols):
    return jnp.concatenate([ref[half_rows(place, *half), cols] for half in ORDER], axis=0)


class Gather:
    def __init__(self, place, buf, ssem, rsem, relative):
        self.place, self.buf, self.ssem, self.rsem, self.relative = place, buf, ssem, rsem, relative

    def row(self, slot, half):
        if self.relative:
            return pl.ds(UNIT[slot, half], 64)
        return half_rows(self.place, slot, half)

    def copy(self, k):
        slot, half, to, there = (
            (0, 0, 1, 1),
            (0, 1, 1, 1),
            (0, 1, -1, 2),
            (0, 0, -1, 2),
            (1, 0, 1, 3),
            (2, 1, -1, 3),
        )[k]
        src = self.buf.at[self.row(slot, half)]
        dst = self.buf.at[self.row(there, half)] if self.relative else src
        return remote(src, dst, self.ssem.at[k], self.rsem.at[k], self.place.z(to))

    def start(self, *which):
        for k in which or (0, 2, 1, 3):
            self.copy(k).start()

    def relay(self):
        self.copy(0).wait_recv()
        self.copy(4).start()
        self.copy(2).wait_recv()
        self.copy(5).start()

    def near(self):
        self.copy(1).wait_recv()
        self.copy(3).wait_recv()

    def far(self):
        self.copy(4).wait_recv()
        self.copy(5).wait_recv()

    def done(self):
        for k in range(6):
            self.copy(k).wait_send()


class Scatter:
    def __init__(self, place, part, relays, recv, ssem, rsem):
        self.place, self.part, self.relays, self.recv = place, part, relays, recv
        self.ssem, self.rsem = ssem, rsem

    def rows(self, slot, half):
        return pl.ds(UNIT[slot, half], 64)

    def copy(self, k, n):
        part, relays, recv = self.part, self.relays, self.recv
        cols = pl.ds(pl.multiple_of(n * 512, 512), 512)
        src, dst, to = (
            (part.at[self.rows(3, 0), cols], relays.at[0, :, cols], 1),
            (part.at[self.rows(2, 1), cols], recv.at[0, self.rows(0, 1), cols], 1),
            (part.at[self.rows(3, 1), cols], relays.at[1, :, cols], -1),
            (part.at[self.rows(1, 0), cols], recv.at[1, self.rows(0, 0), cols], -1),
            (part.at[self.rows(2, 0), cols], recv.at[0, self.rows(0, 0), cols], 1),
            (part.at[self.rows(1, 1), cols], recv.at[1, self.rows(0, 1), cols], -1),
        )[k]
        sem = k * 4 + n
        return remote(src, dst, self.ssem.at[sem], self.rsem.at[sem], self.place.z(to))

    def start(self, n, *which):
        for k in which:
            self.copy(k, n).start()

    def relay(self, first, last):
        @pl.loop(first, last)
        def _(n):
            cols = pl.ds(pl.multiple_of(n * 512, 512), 512)
            for index, slot, half, out in ((0, 2, 0, 4), (1, 1, 1, 5)):
                self.copy(2 * index, n).wait_recv()
                rows = self.rows(slot, half)
                total = self.part[rows, cols].astype(F32) + self.relays[index, :, cols].astype(F32)
                self.part[rows, cols] = total.astype(BF)
                self.copy(out, n).start()

    def finish(self):
        @pl.loop(0, 4)
        def _(n):
            for k in (1, 3, 4, 5):
                self.copy(k, n).wait_recv()

    def total(self, rows):
        return (
            self.part[rows, :].astype(F32)
            + self.recv[0, rows, :].astype(F32)
            + self.recv[1, rows, :].astype(F32)
        )

    def done(self):
        @pl.loop(0, 4)
        def _(n):
            for k in range(6):
                self.copy(k, n).wait_send()


def sixteen(r):
    return pl.ds(pl.multiple_of(r * 16, 16), 16)


def own_rows(place, r):
    return pl.ds(pl.multiple_of(place.t * 128 + r * 16, 16), 16)


def kernel(names, *refs):
    ref = dict(zip(names, refs))
    place = Place()
    tok, cot, live = ref["tok"], ref["cot"], ref["lengths"]
    wq, wo, wgu, wd = ref["wq"], ref["wo"], ref["wgu"], ref["wd"]
    attn, qkv, probs, ctx = ref["attn"], ref["qkv"], ref["probs"], ref["ctx"]
    middle, mlp, masked, w3 = ref["middle"], ref["mlp"], ref["masked"], ref["w3"]
    pa, pb, branch = w3.at[0], w3.at[1], w3.at[2]
    hid, ggu, gctx, gproj, gmid = ref["hid"], ref["ggu"], ref["gctx"], ref["qkv"], ref["gmid"]
    cos_t, sin_t, gain1, gain2 = ref["cos"], ref["sin"], ref["gain1"], ref["gain2"]
    xa, xa0, xb0, xb1, xb2 = ref["xa"], ref["xa0"], ref["xb0"], ref["xb1"], ref["xb2"]
    r2, final, shares = ref["r2"], ref["final"], ref["shares"]
    gacc, grecv, gsum = ref["gacc"], ref["grecv"], ref["gsum"]
    zs, zr, lsem = ref["zs"], ref["zr"], ref["lsem"]
    live_rows = live[0]

    cot_load = pltpu.make_async_copy(cot, masked.at[0:ROWS], lsem.at[7])
    cot_load.start()

    loads = [pltpu.make_async_copy(ref["wq_h"].at[j], wq.at[:, j * 512 : (j + 1) * 512], lsem.at[j]) for j in range(3)]
    tables = [pltpu.make_async_copy(ref["cos_h"], cos_t, lsem.at[8])]
    tables.append(pltpu.make_async_copy(ref["sin_h"], sin_t, lsem.at[9]))
    loads.append(pltpu.make_async_copy(ref["wo_h"], wo, lsem.at[3]))
    loads += [pltpu.make_async_copy(ref["wgu_h"].at[j], wgu.at[:, j * FF : (j + 1) * FF], lsem.at[4 + j]) for j in range(2)]
    loads.append(pltpu.make_async_copy(ref["wd_h"], wd, lsem.at[6]))
    for load in tables + loads:
        load.start()

    barrier = pltpu.get_barrier_semaphore()
    partners = [place.z(d) for d in (1, 2, 3)]
    partners += [place.xs(d) for d in (1, 2, 3)] + [place.ys(d) for d in (1, 2, 3)] + [place.core()]
    for device in partners:
        pl.semaphore_signal(barrier, inc=1, device_id=device, device_id_type=MESH)

    @pl.loop(0, 8)
    def _(r):
        v = tok[sixteen(r), :].astype(F32)
        inv = lax.rsqrt(jnp.mean(v * v, axis=-1, keepdims=True) + EPS)
        attn[own_rows(place, r), :] = (v * inv * gain1[...]).astype(BF)

    pl.semaphore_wait(barrier, len(partners))

    ag1 = Gather(place, attn, zs.at[0], zr.at[0], False)
    agm = Gather(place, masked, zs.at[1], zr.at[1], True)
    ag2 = Gather(place, mlp, zs.at[2], zr.at[2], True)
    ag4 = Gather(place, branch, zs.at[3], zr.at[3], False)
    rs3 = Scatter(place, pa, ref["relay_a"], ref["recv_a"], zs.at[5], zr.at[5])
    rs4 = Scatter(place, pa, ref["relay_a"], ref["recv_a"], zs.at[6], zr.at[6])
    rs2 = Scatter(place, pb, ref["relay_b"], ref["recv_b"], zs.at[7], zr.at[7])

    ws, wr = ref["ws"], ref["wr"]
    halves = (slice(0, 1024), slice(1024, 2048))
    minor, major = (place.x, place.y), (place.y, place.x)

    def w_rows(half, at, count):
        first = (at * 2 + place.c) * 64
        if count == 16:
            first = first + minor[half] * 16
        return pl.ds(pl.multiple_of(first, 16), count)

    def w_first(half, d):
        rows, k = w_rows(half, major[half], 16), half * 3 + d - 1
        dst = w3.at[d - 1, rows, halves[half]]
        return remote(ref["wo_h"].at[rows, halves[half]], dst, ws.at[k], wr.at[k], place.z(d))

    def w_plane(half, phase, d):
        part = w3.at[:, w_rows(half, major[half], (16, 64)[phase]), halves[half]]
        k = 6 + (phase * 2 + half) * 3 + d - 1
        device = (place.xs, place.ys)[half ^ phase](d)
        return remote(part, part, ws.at[k], wr.at[k], device)

    def w_core(half, d):
        part = w3.at[:, w_rows(half, (major[half] + d) % 4, 64), halves[half]]
        return remote(part, part, ws.at[18 + half * 4 + d], wr.at[18 + half * 4 + d], place.core())

    both = [(half, d) for d in (1, 3, 2) for half in range(2)]
    for half, d in both:
        w_first(half, d).start()
    ag1.start()
    cot_load.wait()

    @pl.loop(0, 8)
    def _(r):
        at = place.t * ROWS + r * 16 + lax.broadcasted_iota(jnp.int32, (16, 1), 0)
        v = masked[sixteen(r), :].astype(F32)
        masked[sixteen(r), :] = jnp.where(at < live_rows, v, 0.0).astype(BF)

    def project(slot):
        block = (place.t + OFFS[slot]) % 4
        rows = pl.ds(pl.multiple_of(block * 128, 128), 128)
        for j in range(3):
            p = nn(attn[rows, :], wq[:, j * 512 : (j + 1) * 512])
            if j == 2:
                qkv[rows, 1024:1536] = p.astype(BF)
                continue
            for h in range(HEADS):
                v = p[:, h * HD : (h + 1) * HD]
                v = v * cos_t[rows, :] + pltpu.roll(v, 64, 1) * sin_t[rows, :]
                if j == 0:
                    v = v * HD ** (-0.5)
                qkv[rows, j * 512 + h * HD : j * 512 + (h + 1) * HD] = v.astype(BF)

    for load in tables + loads[:3]:
        load.wait()
    project(0)
    for half, d in both:
        w_first(half, d).wait_recv()
    for half, d in both:
        w_plane(half, 0, d).start()
    ag1.relay()
    for half, d in both:
        w_plane(half, 0, d).wait_recv()
    for half, d in both:
        w_plane(half, 1, d).start()
    for half in range(2):
        w_core(half, 0).start()
    ag1.near()
    agm.start(0, 2)
    project(1)
    project(2)
    ag1.far()
    project(3)
    for half, d in both[:4]:
        w_plane(half, 1, d).wait_recv()
        w_core(half, 4 - d).start()

    heads = ref["recv_a"].at[0]

    def to_rows(d, pair):
        src = ctx.at[pl.ds(pl.multiple_of(((place.t + d) % 4) * 128, 128), 128), pair * 256 : pair * 256 + 256]
        dst = heads.at[:, pl.ds(pl.multiple_of(place.t * 512 + pair * 256, 256), 256)]
        sem = pair * 3 + d - 1
        return remote(src, dst, zs.at[4, sem], zr.at[4, sem], place.z(d))

    def heads_forward(h):
        def cols(j):
            return pl.ds(pl.multiple_of(j * 512 + h * HD, HD), HD)

        for q in range(2):
            rows, keys = pl.ds(q * 256, 256), (q + 1) * 256
            scores = nt(qkv[rows, cols(0)], qkv[0:keys, cols(1)])
            at = q * 256 + lax.broadcasted_iota(jnp.int32, (256, keys), 0)
            key = lax.broadcasted_iota(jnp.int32, (256, keys), 1)
            scores = jnp.where((key <= at) & (key < live_rows), scores, -1e30)
            e = jnp.exp(scores - jnp.max(scores, axis=-1, keepdims=True))
            p = (e * (1.0 / jnp.sum(e, axis=-1, keepdims=True))).astype(BF)
            probs[h, rows, 0:keys] = p
            ctx[rows, cols(0)] = nn(p, qkv[0:keys, cols(2)]).astype(BF)

    for pair in range(2):
        pl.loop(2 * pair, 2 * pair + 2)(heads_forward)
        for d in (2, 1, 3):
            to_rows(d, pair).start()
    own = pl.ds(pl.multiple_of(place.t * 128, 128), 128)
    heads[:, pl.ds(pl.multiple_of(place.t * 512, 512), 512)] = ctx[own, :]
    for half, d in both[4:]:
        w_plane(half, 1, d).wait_recv()
        w_core(half, 4 - d).start()
    loads[3].wait()
    agm.start(1, 3)

    other = 1 - place.c
    xs, xr = ref["xs"], ref["xr"]

    def swap_a(group):
        src = (masked, mlp, branch, attn)[group]
        return remote(src, xa.at[group], xs.at[group], xr.at[group], place.core())

    def swap_branch(slot):
        block = (place.t + OFFS[slot]) % 4
        rows = pl.ds(pl.multiple_of(block * 128, 128), 128)
        sem = (2, 15, 16, 17)[slot]
        return remote(branch.at[rows], xa.at[2, rows], xs.at[sem], xr.at[sem], place.core())

    def swap_masked(part):
        rows = (slice(0, 384), slice(384, 512))[part]
        sem = (0, 14)[part]
        return remote(masked.at[rows], xa0.at[rows], xs.at[sem], xr.at[sem], place.core())

    def swap_b(k):
        rows = pl.ds((0, 256, 0, 256, 0, 0)[k], 256 if k < 4 else 512)
        if k < 2:
            src = hid.at[rows, pl.ds(pl.multiple_of(other * 640, 128), 768)]
        elif k < 4:
            src = ggu.at[rows, pl.ds(pl.multiple_of(other * FF, 128), FF)]
        elif k == 4:
            src = ctx.at[rows, pl.ds(pl.multiple_of(other * 256, 256), 256)]
        else:
            src = gproj.at[rows, pl.ds(pl.multiple_of(other * 768, 256), 768)]
        dst = (xb0, xb0, xb1, xb1, xb2, xb0)[k].at[rows]
        return remote(src, dst, xs.at[4 + k], xr.at[4 + k], place.core())

    swap_a(3).start()
    swap_b(4).start()

    for half in range(2):
        for d in range(4):
            w_core(half, d).wait_recv()
    w3_keep = pltpu.make_async_copy(w3, ref["w3_h"], lsem.at[8])
    w3_keep.start()
    for pair in range(2):
        for d in (1, 2, 3):
            to_rows(d, pair).wait_recv()

    @pl.loop(0, 4)
    def _(n):
        at = pl.ds(pl.multiple_of(n * 512, 512), 512)

        def share(d, weights):
            return nn(heads[:, pl.ds(pl.multiple_of(((place.t + d) % 4) * 512, 512), 512)], weights)

        out = share(0, wo[:, at]) + share(3, w3[0, :, at]) + share(2, w3[1, :, at]) + share(1, w3[2, :, at])
        middle[:, at] = tok[:, at].astype(F32) + out

    @pl.loop(0, 8)
    def _(r):
        rows = sixteen(r)
        v = middle[rows, :]
        inv = lax.rsqrt(jnp.mean(v * v, axis=-1, keepdims=True) + EPS)
        mlp[rows, :] = (v * inv * gain2[...]).astype(BF)

    for pair in range(2):
        for d in (1, 2, 3):
            to_rows(d, pair).wait_send()
    for half, d in both:
        w_first(half, d).wait_send()
        w_plane(half, 0, d).wait_send()
        w_plane(half, 1, d).wait_send()
    for half in range(2):
        for d in range(4):
            w_core(half, d).wait_send()
    ag2.start()
    for load in loads[4:]:
        load.wait()

    own_b = (
        hid.at[:, pl.ds(pl.multiple_of(place.c * 640, 128), 768)],
        ggu.at[:, pl.ds(pl.multiple_of(place.c * FF, 128), FF)],
        ctx.at[:, pl.ds(pl.multiple_of(place.c * 256, 256), 256)],
        gproj.at[:, pl.ds(pl.multiple_of(place.c * 768, 256), 768)],
    )
    own_a = (masked, mlp, branch, attn)
    other_a = (xa0, pb, wd.at[0:512], wd.at[512:1024])
    other_b = (xb0, xb1, xb2, xb0)
    osem = ref["osem"]

    def bring(group):
        return pltpu.make_async_copy(xa.at[group], other_a[group], osem.at[group])

    def fetch(group):
        if group == 2:
            for slot in range(1, 4):
                swap_branch(slot).wait_recv()
        else:
            swap_a(group).wait_recv()
        bring(group).start()

    def piece(group, axis, tile, first, count):
        if group == 3 and axis == 1:
            return mlp.at[pl.ds(first, count), pl.ds(pl.multiple_of(tile * 384, 128), 384)]
        base = (FF, 0, FF + 768, FF + 1024)[group]
        lo = base if axis == 0 else base + CX[group]
        width = CX[group] if axis == 0 else CY[group]
        rows = pl.ds(pl.multiple_of(tile * 512 + first, min(count, 128)), count)
        return wgu.at[rows, lo : lo + width]

    p1xs, p1xr, p1ys, p1yr = ref["p1xs"], ref["p1xr"], ref["p1ys"], ref["p1yr"]

    def relayed(group, axis):
        if group < 2:
            return ref[("relx", "rely")[axis] + str(group)]
        lo = ((768, 896), (0, 384))[group - 2][axis]
        return xb1.at[:, lo : lo + CX[group]]

    def arrived(group, axis, side):
        if group < 2:
            return ref[("recx", "recy")[axis] + str(group)].at[side]
        width = CX[group]
        lo = ((1536, 1792), (0, 768))[group - 2][axis] + side * width
        return xa0.at[:, pl.ds(lo if isinstance(lo, int) else pl.multiple_of(lo, 128), width)]

    def tile_of(step):
        return (place.y + jnp.where(step == 0, 2, jnp.where(step == 1, 1, jnp.where(step == 2, 3, 0)))) % 4

    def send_x(group, kind, step):
        tile, to = tile_of(step), 1 - 2 * (step % 2)
        rows = pl.ds(pl.multiple_of(tile * 128, 128), 128)
        if kind == 0:
            block, dst = place.x + 2, relayed(group, 0).at[rows]
        elif kind == 1:
            block, dst, to = place.x + 4 - to, arrived(group, 0, (1 + to) // 2).at[rows], -to
        else:
            block, dst = place.x + 4 + to, arrived(group, 0, (1 - to) // 2).at[rows]
        src = piece(group, 0, tile, pl.multiple_of((block % 4) * 128, 128), 128)
        sem = (group * 3 + kind) * 4 + step
        return remote(src, dst, p1xs.at[sem], p1xr.at[sem], place.xs(4 + to))

    def send_y(group, k):
        offset, first, dst, to = (
            (2, 0, relayed(group, 1).at[0:256], 1),
            (1, 256, arrived(group, 1, 0).at[256:512], 1),
            (2, 256, relayed(group, 1).at[256:512], 3),
            (3, 0, arrived(group, 1, 1).at[0:256], 3),
            (1, 0, arrived(group, 1, 0).at[0:256], 1),
            (3, 256, arrived(group, 1, 1).at[256:512], 3),
        )[k]
        src = piece(group, 1, (place.y + offset) % 4, first, 256)
        return remote(src, dst, p1ys.at[group * 6 + k], p1yr.at[group * 6 + k], place.ys(to))

    def gradient(group, step):
        tile = tile_of(step)
        at = pl.ds(pl.multiple_of(tile * 512, 512), 512)
        lo = 0
        for axis, width in ((0, CX[group]), (1, CY[group])):
            own, oth = own_b[group].at[:, lo : lo + width], other_b[group].at[:, lo : lo + width]
            out = tn(own_a[group][:, at], own[...]) + tn(other_a[group][:, at], oth[...])
            piece(group, axis, tile, 0, 512)[...] = out.astype(BF)
            lo += width
        send_x(group, 0, step).start()

        @pl.when(step == 0)
        def _():
            send_y(group, 0).start()
            send_y(group, 2).start()

    def near_x(group, step):
        send_x(group, 1, step).start()

    def near_y(group, step):
        for when in (1, 2):

            @pl.when(step == when)
            def _():
                send_y(group, 2 * when - 1).start()

    def all_near(group, *axes):
        @pl.loop(0, 4)
        def _(step):
            for axis in axes:
                (near_x, near_y)[axis](group, step)

    lands = ref["lands"]

    def mid_copies(group):
        if group > 1:
            return ()
        return (
            pltpu.make_async_copy(relayed(group, 0), hid.at[:, 0 : CX[group]], lands.at[16 + group]),
            pltpu.make_async_copy(relayed(group, 1), hid.at[:, 768 : 768 + CY[group]], lands.at[20 + group]),
        )

    def mid_start(group):
        for step in range(4):
            send_x(group, 0, step).wait_recv()
        for k in (0, 2):
            send_y(group, k).wait_recv()
        for copy in mid_copies(group):
            copy.start()

    def mid_end(group):
        for copy in mid_copies(group):
            copy.wait()

        def add(axis, tile, first, rows, lo, width, count):
            src = hid.at[:, lo : lo + width] if group < 2 else relayed(group, axis)

            @pl.loop(0, count // 32)
            def _(i):
                own = piece(group, axis, tile, pl.multiple_of(first + i * 32, 32), 32)
                got = src[pl.ds(pl.multiple_of(rows + i * 32, 32), 32), :]
                own[...] = (own[...].astype(F32) + got.astype(F32)).astype(BF)

        for step in range(4):
            to, tile = (1, 3)[step % 2], tile_of(step)
            add(0, tile, ((place.x + to) % 4) * 128, tile * 128, 0, CX[group], 128)
            send_x(group, 2, step).start()
        for k, offset, first in ((4, 1, 0), (5, 3, 256)):
            add(1, (place.y + offset) % 4, first, first, 768, CY[group], 256)
            send_y(group, k).start()

    def feed(first, count):
        rows = slice(first, first + count)
        for n0, n1 in ((0, 512), (512, 1024), (1024, 1408)):
            gate = nn(mlp[rows, :], wgu[:, n0:n1])
            up = nn(mlp[rows, :], wgu[:, FF + n0 : FF + n1])
            sig = jax.nn.sigmoid(gate)
            silu = gate * sig
            hid[rows, n0:n1] = (silu * up).astype(BF)
            ggu[rows, n0:n1] = (up * sig * (1.0 + gate * (1.0 - sig))).astype(BF)
            ggu[rows, FF + n0 : FF + n1] = silu.astype(BF)

    def feed_back(first, count):
        rows = slice(first, first + count)
        for n0, n1 in ((0, 512), (512, 1024), (1024, 1408)):
            grad = nt(masked[rows, :], wd[n0:n1, :])
            for lo in (0, FF):
                ggu[rows, lo + n0 : lo + n1] = (grad * ggu[rows, lo + n0 : lo + n1].astype(F32)).astype(BF)

    def feed_part(first, count, *sends):
        rows = slice(first, first + count)

        @pl.loop(0, 4)
        def _(n):
            at = pl.ds(pl.multiple_of(n * 512, 512), 512)
            rs3.part[rows, at] = nt(ggu[rows, :], wgu[at, :]).astype(BF)
            rs3.start(n, *sends)

    feed(0, 128)
    feed_back(0, 128)
    w3_keep.wait()
    feed_part(0, 128)
    w3_back = []
    for j in range(3):
        rows, cols = slice(j * 512, (j + 1) * 512), slice(j * 512, (j + 1) * 512)
        kept = ref["w3_h"].at[j]
        w3_back.append(pltpu.make_async_copy(kept.at[:, 0:1536], wq.at[rows], osem.at[4 + j]))
        w3_back.append(pltpu.make_async_copy(kept.at[:, 1536:2048], wq.at[1536:2048, cols], osem.at[7 + j]))
    for copy in w3_back:
        copy.start()
    ag2.relay()
    agm.near()
    agm.relay()
    swap_masked(0).start()
    feed(128, 128)
    feed_back(128, 128)
    feed_part(128, 128, 1, 3)
    swap_b(0).start()
    swap_b(2).start()
    ag2.near()
    ag2.far()
    swap_a(1).start()
    feed(256, 256)
    swap_b(1).start()
    agm.far()
    swap_masked(1).start()
    feed_back(256, 256)
    swap_b(3).start()
    fetch(1)
    late, taken = slice(256, 512), slice(FF, FF + COLS[0])

    @pl.loop(0, 4)
    def _(n):
        at = pl.ds(pl.multiple_of(n * 512, 512), 512)
        rs3.part[late, at] = nt(ggu[late, taken], wgu[at, taken]).astype(BF)

    swap_b(0).wait_recv()
    swap_b(1).wait_recv()
    swap_masked(0).wait_recv()
    swap_masked(1).wait_recv()

    @pl.loop(0, 2)
    def _(step):
        gradient(0, step)
        near_x(0, step)
        near_y(0, step)

    @pl.loop(0, 4)
    def _(n):
        at = pl.ds(pl.multiple_of(n * 512, 512), 512)
        part = nt(ggu[late, 0:FF], wgu[at, 0:FF]) + nt(ggu[late, FF + COLS[0] :], wgu[at, FF + COLS[0] :])
        rs3.part[late, at] = (part + rs3.part[late, at].astype(F32)).astype(BF)
        rs3.start(n, 0, 2)

    @pl.loop(2, 4)
    def _(step):
        gradient(0, step)
        near_x(0, step)
        near_y(0, step)

    rs3.relay(0, 3)
    bring(1).wait()
    swap_b(2).wait_recv()
    swap_b(3).wait_recv()

    def gate_up(step):
        gradient(1, step)
        near_x(1, step)
        near_y(1, step)

    gate_up(0)
    rs3.relay(3, 4)
    pl.loop(1, 3)(gate_up)
    p2xs, p2xr, p2ys, p2yr = ref["p2xs"], ref["p2xr"], ref["p2ys"], ref["p2yr"]

    def landing(group):
        copies = []
        for d in range(2 if group < 2 else 0):
            for axis in range(2):
                lo = d * FF + axis * 768
                width = CX[group] if axis == 0 else CY[group]
                sem = lands.at[group * 4 + d * 2 + axis]
                copies.append(pltpu.make_async_copy(arrived(group, axis, d), ggu.at[:, lo : lo + width], sem))
        return copies

    def send_2(group, axis, d):
        sem = group * 3 + d - 1
        own = pl.multiple_of(place.x * 128, 128)
        if axis == 0:
            src = piece(group, 0, (place.y + d) % 4, own, 128)
            dst = r2.at[d - 1, :, BASE[group] : BASE[group] + CX[group]]
            return remote(src, dst, p2xs.at[sem], p2xr.at[sem], place.ys(d))
        src = piece(group, 1, place.y, pl.multiple_of(((place.x + d) % 4) * 128, 128), 128)
        dst = r2.at[d - 1, :, BASE[group] + CX[group] : BASE[group] + COLS[group]]
        return remote(src, dst, p2ys.at[sem], p2yr.at[sem], place.xs(d))

    q2s, q2r = ref["q2s"], ref["q2r"]

    def send_3(group, axis, k):
        lo = BASE[group] + (0 if axis == 0 else CX[group])
        cols = slice(lo, lo + (CX[group] if axis == 0 else CY[group]))
        offset, first, slot, to = ((2, 0, 2, 1), (1, 64, 0, 1), (2, 64, 2, 3), (3, 0, 1, 3), (1, 0, 0, 1), (3, 64, 1, 3))[k]
        if axis == 0:
            src = piece(group, 0, (place.y + offset) % 4, pl.multiple_of(place.x * 128 + first, 64), 64)
        else:
            src = piece(group, 1, place.y, pl.multiple_of(((place.x + offset) % 4) * 128 + first, 64), 64)
        device = (place.ys, place.xs)[axis](to)
        sem = (group * 2 + axis) * 6 + k
        return remote(src, r2.at[slot, first : first + 64, cols], q2s.at[sem], q2r.at[sem], device)

    def mid_second(group):
        for axis in range(2):
            lo = BASE[group] + (0 if axis == 0 else CX[group])
            cols = slice(lo, lo + (CX[group] if axis == 0 else CY[group]))
            for k, out, offset, first in ((0, 4, 1, 0), (2, 5, 3, 64)):
                send_3(group, axis, k).wait_recv()
                if axis == 0:
                    own = piece(group, 0, (place.y + offset) % 4, pl.multiple_of(place.x * 128 + first, 64), 64)
                else:
                    own = piece(group, 1, place.y, pl.multiple_of(((place.x + offset) % 4) * 128 + first, 64), 64)
                got = r2[2, first : first + 64, cols]
                own[...] = (own[...].astype(F32) + got.astype(F32)).astype(BF)
                send_3(group, axis, out).start()

    def land(group):
        for step in range(4):
            for kind in (1, 2):
                send_x(group, kind, step).wait_recv()
        for k in (1, 3, 4, 5):
            send_y(group, k).wait_recv()
        for copy in landing(group):
            copy.start()

    def first_sum(group):
        for copy in landing(group):
            copy.wait()
        for axis in range(2):
            lo = axis * 768
            width = CX[group] if axis == 0 else CY[group]
            if group < 2:
                got = [ggu.at[:, d * FF + lo : d * FF + lo + width] for d in range(2)]
            else:
                got = [arrived(group, axis, d) for d in range(2)]

            @pl.loop(0, 16)
            def _(i):
                if axis == 0:
                    own = piece(group, 0, i // 4, pl.multiple_of(place.x * 128 + (i % 4) * 32, 32), 32)
                else:
                    own = piece(group, 1, place.y, pl.multiple_of(i * 32, 32), 32)
                rows = pl.ds(pl.multiple_of(i * 32, 32), 32)
                total = own[...].astype(F32)
                for d in range(2):
                    total = total + got[d][rows, :].astype(F32)
                own[...] = total.astype(BF)

            if group < 2:
                for k in (0, 2, 1, 3):
                    send_3(group, axis, k).start()
            else:
                for d in (2, 1, 3):
                    send_2(group, axis, d).start()

    def whole_of(group):
        return ((final, 0), (middle, 0), (final, 768), (final, 1024))[group]

    def ending(group):
        ref_at, first = whole_of(group)
        cols = slice(first, first + COLS[group])
        mine = ref_at.at[pl.ds(pl.multiple_of(place.c * 64, 64), 64), cols]
        theirs = ref_at.at[pl.ds(pl.multiple_of(other * 64, 64), 64), cols]
        dst = shares.at[place.c, :, BASE[group] : BASE[group] + COLS[group]]
        return (
            remote(theirs, dst, xs.at[10 + group], xr.at[10 + group], place.core()),
            pltpu.make_async_copy(mine, dst, lsem.at[9 + group]),
        )

    def second_sum(group):
        for axis in range(2):
            if group < 2:
                for k in (1, 3, 4, 5):
                    send_3(group, axis, k).wait_recv()
            else:
                for d in (1, 2, 3):
                    send_2(group, axis, d).wait_recv()
            lo = BASE[group] + (0 if axis == 0 else CX[group])
            width = CX[group] if axis == 0 else CY[group]
            whole, first = whole_of(group)
            first += lo - BASE[group]

            @pl.loop(0, 4)
            def _(i):
                rows = pl.ds(pl.multiple_of(i * 32, 32), 32)
                own = piece(group, axis, place.y, pl.multiple_of(place.x * 128 + i * 32, 32), 32)
                total = own[...].astype(F32)
                for d in range(2 if group < 2 else 3):
                    total = total + r2[d, rows, lo : lo + width].astype(F32)
                whole[rows, first : first + width] = total
        for copy in ending(group):
            copy.start()

    rs3.finish()

    def fold(v):
        return jnp.concatenate([v[:, i * 512 : (i + 1) * 512] for i in range(4)], axis=0)

    def mlp_back(r, total):
        rows = sixteen(r)
        grad = rs3.total(rows)
        v = middle[rows, :]
        inv = lax.rsqrt(jnp.mean(v * v, axis=-1, keepdims=True) + EPS)
        scaled = grad * gain2[...]
        back = (
            masked[rows, :].astype(F32)
            + inv * scaled
            - v * (inv * inv * inv) * jnp.mean(v * scaled, axis=-1, keepdims=True)
        )
        gmid[rows, :] = back
        branch[own_rows(place, r), :] = back.astype(BF)
        return total + jnp.sum(grad * v * inv, axis=0, keepdims=True)

    gain2_part = lax.fori_loop(0, 8, mlp_back, jnp.zeros((1, D), F32))
    gacc[0, 4:8, :] = fold(gain2_part)
    agm.done()
    swap_masked(0).wait_send()
    swap_masked(1).wait_send()
    for copy in w3_back:
        copy.wait()
    own = pl.ds(pl.multiple_of(place.t * 128, 128), 128)

    def to_heads(j):
        src = masked.at[128:256, j * 512 : (j + 1) * 512]
        return remote(src, gctx.at[own], zs.at[4, 6 + j], zr.at[4, 6 + j], place.z(3 - j))

    for j in (1, 0, 2):
        at = slice(j * 512, (j + 1) * 512)
        part = nt(branch[own, 0:1536], wq[at, :]) + nt(branch[own, 1536:2048], wq[1536:2048, at])
        masked[128:256, at] = part.astype(BF)
        to_heads(j).start()
    gctx[own, :] = nt(branch[own, :], wo[...]).astype(BF)
    ag4.start()
    for load in loads[:3]:
        load.start()
    swap_branch(0).start()
    rs3.done()

    gate_up(3)

    @pl.loop(0, 4)
    def _(n):
        at = pl.ds(pl.multiple_of(n * 512, 512), 512)
        rs2.part[:, at] = nn(hid[...], wd[:, at]).astype(BF)

    fetch(3)
    for k in (0, 1, 2, 3):
        swap_b(k).wait_send()
    mid_start(0)
    mid_end(0)
    mid_start(1)
    mid_end(1)
    ag4.relay()
    for pair in ((0, 2), (1, 3)):

        @pl.loop(0, 4)
        def _(n):
            rs2.start(n, *pair)

    for j in range(3):
        to_heads(j).wait_recv()

    def turn_back(v, rows):
        return v * cos_t[rows, :] - pltpu.roll(v, 64, 1) * sin_t[rows, :]

    def heads_back(h):
        def cols(j):
            return pl.ds(pl.multiple_of(j * 512 + h * HD, HD), HD)

        def part(q):
            rows, keys = pl.ds(q * 256, 256), (q + 1) * 256
            p = probs[h, rows, 0:keys]
            grad = gctx[rows, cols(0)]
            wide = p.astype(F32)
            gp = nt(grad, qkv[0:keys, cols(2)])
            gs = (wide * (gp - jnp.sum(wide * gp, axis=-1, keepdims=True))).astype(BF)
            gq = (turn_back(nn(gs, qkv[0:keys, cols(1)]), rows) * HD ** (-0.5)).astype(BF)
            return gq, tn(gs, qkv[rows, cols(0)]), tn(p, grad)

        q1, k1, v1 = part(1)
        q0, k0, v0 = part(0)
        lo, hi = slice(0, 256), slice(256, 512)
        k0, k1 = turn_back(k0 + k1[lo], lo).astype(BF), turn_back(k1[hi], hi).astype(BF)
        v0, v1 = (v0 + v1[lo]).astype(BF), v1[hi].astype(BF)
        for j, low, high in ((0, q0, q1), (1, k0, k1), (2, v0, v1)):
            gproj[lo, cols(j)] = low
            gproj[hi, cols(j)] = high

    pl.loop(0, HEADS)(heads_back)
    swap_branch(0).wait_recv()
    swap_b(5).start()
    land(0)
    for load in loads[:3]:
        load.wait()
    first_sum(0)
    swap_a(1).wait_send()
    ag2.done()
    bring(3).wait()
    swap_b(5).wait_recv()

    @pl.loop(0, 4)
    def _(step):
        gradient(3, step)

    all_near(3, 0, 1)
    ag4.near()
    ag4.far()
    for slot in (1, 2, 3):
        swap_branch(slot).start()
    @pl.loop(0, 4)
    def _(n):
        at = pl.ds(pl.multiple_of(n * 512, 512), 512)
        part = nt(in_order(place, gproj, slice(None)), wq[at, :])
        rs4.part[:, at] = part.astype(BF)
        seen = jnp.sum(part * in_order(place, attn, at).astype(F32), axis=0, keepdims=True)
        gsum[n] = jnp.broadcast_to(seen, (8, 512))

    for n in range(4):
        at = slice(n * 512, (n + 1) * 512)
        gacc[0, n : n + 1, :] = gsum[n, 0:1, :] / gain1[:, at]
    gs, gr = ref["gs"], ref["gr"]

    def spread(stage):
        count = 2 if stage == 3 else 4
        me = (place.t, place.x, place.y, place.c)[stage]
        out = []
        for d in range(1, count):
            device = (place.z, place.xs, place.ys, lambda _: place.core())[stage](d)
            k = stage * 3 + d - 1
            out.append(remote(gacc.at[stage], grecv.at[stage * 4 + me], gs.at[k], gr.at[k], device))
        return out, count, me

    def spread_start(stage):
        copies, _, me = spread(stage)
        grecv[stage * 4 + me] = gacc[stage]
        for copy in copies:
            copy.start()

    def spread_end(stage):
        copies, count, _ = spread(stage)
        for copy in copies:
            copy.wait_recv()
        total = grecv[stage * 4]
        for i in range(1, count):
            total = total + grecv[stage * 4 + i]
        gacc[stage + 1] = total

    spread_start(0)
    for pair in ((0, 2), (1, 3)):

        @pl.loop(0, 4)
        def _(n):
            rs4.start(n, *pair)

    rs2.relay(0, 4)
    mid_second(0)
    fetch(2)
    mid_start(3)
    mid_end(3)
    swap_b(4).wait_recv()
    bring(2).wait()

    @pl.loop(0, 4)
    def _(step):
        gradient(2, step)

    all_near(2, 0, 1)
    spread_end(0)
    spread_start(1)
    land(1)
    first_sum(1)
    mid_start(2)
    mid_end(2)
    land(3)
    first_sum(3)
    mid_second(1)
    rs4.relay(0, 4)
    spread_end(1)
    spread_start(2)
    rs2.finish()

    @pl.loop(0, 8)
    def _(r):
        rows = sixteen(r)
        middle[rows, :] = middle[rows, :] + rs2.total(rows)

    out_copy = pltpu.make_async_copy(middle, ref["output"], lsem.at[7])
    out_copy.start()
    second_sum(0)
    land(2)
    first_sum(2)
    out_copy.wait()
    second_sum(1)
    spread_end(2)
    spread_start(3)
    rs4.finish()

    @pl.loop(0, 8)
    def _(r):
        rows = sixteen(r)
        grad = rs4.total(rows)
        v = tok[rows, :].astype(F32)
        inv = lax.rsqrt(jnp.mean(v * v, axis=-1, keepdims=True) + EPS)
        scaled = grad * gain1[...]
        gmid[rows, :] = (
            gmid[rows, :]
            + inv * scaled
            - v * (inv * inv * inv) * jnp.mean(v * scaled, axis=-1, keepdims=True)
        )

    tok_copy = pltpu.make_async_copy(gmid, ref["grad_tokens"], lsem.at[8])
    tok_copy.start()
    spread_end(3)
    ref["gains"][...] = gacc[4]
    second_sum(3)
    second_sum(2)

    for j in range(3):
        to_heads(j).wait_send()
    for gather in (ag1, ag4):
        gather.done()
    rs4.done()
    rs2.done()
    swap_a(3).wait_send()
    for slot in range(4):
        swap_branch(slot).wait_send()
    for k in (4, 5):
        swap_b(k).wait_send()
    for group in range(4):
        for step in range(4):
            for kind in range(3):
                send_x(group, kind, step).wait_send()
        for k in range(6):
            send_y(group, k).wait_send()
        for axis in range(2):
            if group < 2:
                for k in range(6):
                    send_3(group, axis, k).wait_send()
            else:
                for d in (1, 2, 3):
                    send_2(group, axis, d).wait_send()
    for stage in range(4):
        for copy in spread(stage)[0]:
            copy.wait_send()
    tok_copy.wait()
    for group in range(4):
        for copy in ending(group):
            copy.wait()


def block(tokens, gain_attn, w_qkv, w_out, gain_mlp, w_gate_up, w_down, cotangent, lengths):
    cos_t, sin_t = rotary_tables()
    vmem = pl.BlockSpec(memory_space=pltpu.VMEM)
    smem = pl.BlockSpec(memory_space=pltpu.SMEM)
    hbm = pl.BlockSpec(memory_space=pl.ANY)
    ins = [
        ("tok", tokens, vmem),
        ("gain1", gain_attn.reshape(1, D), vmem),
        ("wq_h", w_qkv, hbm),
        ("wo_h", w_out, hbm),
        ("gain2", gain_mlp.reshape(1, D), vmem),
        ("wgu_h", w_gate_up, hbm),
        ("wd_h", w_down, hbm),
        ("cot", cotangent, hbm),
        ("lengths", lengths, smem),
        ("cos_h", jnp.asarray(cos_t), hbm),
        ("sin_h", jnp.asarray(sin_t), hbm),
    ]
    outs = [
        ("output", (ROWS, D), F32, hbm),
        ("grad_tokens", (ROWS, D), F32, hbm),
        ("gains", (8, 512), F32, vmem),
        ("shares", (2, 64, ALL), F32, hbm),
        ("xa", (4, SEQ, D), BF, hbm),
        ("w3_h", (3, SEQ, D), BF, hbm),
    ]
    outs += [(f"relx{g}", (SEQ, CX[g]), BF, hbm) for g in range(2)]
    outs += [(f"rely{g}", (SEQ, CY[g]), BF, hbm) for g in range(2)]
    outs += [(f"recx{g}", (2, SEQ, CX[g]), BF, hbm) for g in range(2)]
    outs += [(f"recy{g}", (2, SEQ, CY[g]), BF, hbm) for g in range(2)]
    dma = pltpu.SemaphoreType.DMA
    scratch = [
        ("wq", pltpu.VMEM((D, 1536), BF)),
        ("wo", pltpu.VMEM((512, D), BF)),
        ("wgu", pltpu.VMEM((D, 2 * FF), BF)),
        ("wd", pltpu.VMEM((FF, D), BF)),
        ("attn", pltpu.VMEM((SEQ, D), BF)),
        ("qkv", pltpu.VMEM((SEQ, 1536), BF)),
        ("probs", pltpu.VMEM((HEADS, SEQ, SEQ), BF)),
        ("ctx", pltpu.VMEM((SEQ, 512), BF)),
        ("middle", pltpu.VMEM((ROWS, D), F32)),
        ("mlp", pltpu.VMEM((SEQ, D), BF)),
        ("masked", pltpu.VMEM((SEQ, D), BF)),
        ("hid", pltpu.VMEM((SEQ, FF), BF)),
        ("ggu", pltpu.VMEM((SEQ, 2 * FF), BF)),
        ("gctx", pltpu.VMEM((SEQ, 512), BF)),
        ("xa0", pltpu.VMEM((SEQ, D), BF)),
        ("xb0", pltpu.VMEM((SEQ, COLS[0]), BF)),
        ("xb1", pltpu.VMEM((SEQ, COLS[1]), BF)),
        ("xb2", pltpu.VMEM((SEQ, COLS[2]), BF)),
        ("gmid", pltpu.VMEM((ROWS, D), F32)),
        ("w3", pltpu.VMEM((3, SEQ, D), BF)),
        ("relay_a", pltpu.VMEM((2, 64, D), BF)),
        ("recv_a", pltpu.VMEM((2, ROWS, D), BF)),
        ("relay_b", pltpu.VMEM((2, 64, D), BF)),
        ("recv_b", pltpu.VMEM((2, ROWS, D), BF)),
        ("r2", pltpu.VMEM((3, ROWS, ALL), BF)),
        ("final", pltpu.VMEM((ROWS, 1792), F32)),
        ("gacc", pltpu.VMEM((5, 8, 512), F32)),
        ("cos", pltpu.VMEM((SEQ, HD), F32)),
        ("sin", pltpu.VMEM((SEQ, HD), F32)),
        ("gsum", pltpu.VMEM((4, 8, 512), F32)),
        ("grecv", pltpu.VMEM((14, 8, 512), F32)),
        ("zs", dma((8, 24))),
        ("zr", dma((8, 24))),
        ("lsem", dma((13,))),
        ("osem", dma((10,))),
        ("xs", dma((18,))),
        ("xr", dma((18,))),
        ("p1xs", dma((48,))),
        ("p1xr", dma((48,))),
        ("p1ys", dma((24,))),
        ("p1yr", dma((24,))),
        ("q2s", dma((24,))),
        ("q2r", dma((24,))),
        ("p2xs", dma((12,))),
        ("p2xr", dma((12,))),
        ("p2ys", dma((12,))),
        ("p2yr", dma((12,))),
        ("lands", dma((24,))),
        ("gs", dma((10,))),
        ("ws", dma((26,))),
        ("wr", dma((26,))),
        ("gr", dma((10,))),
    ]
    names = [i[0] for i in ins] + [o[0] for o in outs] + [s[0] for s in scratch]
    results = pl.pallas_call(
        functools.partial(kernel, names),
        out_shape=[jax.ShapeDtypeStruct(o[1], o[2]) for o in outs],
        in_specs=[i[2] for i in ins],
        out_specs=[o[3] for o in outs],
        scratch_shapes=[s[1] for s in scratch],
        compiler_params=pltpu.CompilerParams(
            collective_id=0, has_side_effects=True, vmem_limit_bytes=63 * 1024 * 1024
        ),
        name="block",
    )(*[i[1] for i in ins])
    return arrange(*results[:4])


def arrange_kernel(out_in, tok_in, gains, shares, output, grad_tokens, gain1, qkv, out, gain2, gate_up, down, *scratch):
    out_v, tok_v, shares_v, sem = scratch
    down_at, gu_at, out_at, qkv_at = BASE

    def columns(core, first, count):
        return shares_v.at[core, :, first : first + count]

    def through(src, buf, dst, half):
        rows = slice(half * 64, half * 64 + 64)
        return (src.at[rows], buf.at[rows]), ((buf.at[rows], dst.at[rows]),)

    def of_shares(first, count, *stores):
        cols = slice(first, first + count)
        return (shares.at[:, :, cols], shares_v.at[:, :, cols]), stores

    moves = (
        through(out_in, out_v, output, 0),
        through(out_in, out_v, output, 1),
        through(tok_in, tok_v, grad_tokens, 0),
        through(tok_in, tok_v, grad_tokens, 1),
        of_shares(gu_at, FF, (columns(0, gu_at, FF), gate_up.at[0]), (columns(1, gu_at, FF), gate_up.at[1])),
        of_shares(
            qkv_at,
            768,
            (columns(0, qkv_at, 512), qkv.at[0]),
            (columns(0, qkv_at + 512, 256), qkv.at[1, :, 0:256]),
            (columns(1, qkv_at, 256), qkv.at[1, :, 256:512]),
            (columns(1, qkv_at + 256, 512), qkv.at[2]),
        ),
        of_shares(
            down_at,
            768,
            (columns(0, down_at, 768), down.at[:, 0:768]),
            (columns(1, down_at + 128, 640), down.at[:, 768:1408]),
        ),
        of_shares(
            out_at,
            256,
            (columns(0, out_at, 256), out.at[:, 0:256]),
            (columns(1, out_at, 256), out.at[:, 256:512]),
        ),
    )
    loads = [pltpu.make_async_copy(*move[0], sem.at[i]) for i, move in enumerate(moves)]
    for load in loads:
        load.start()
    for i in range(4):
        at = slice(i * 512, (i + 1) * 512)
        gain1[:, at] = gains[i : i + 1, :]
        gain2[:, at] = gains[4 + i : 5 + i, :]
    stores = []
    for load, move in zip(loads, moves):
        load.wait()
        for src, dst in move[1]:
            stores.append(pltpu.make_async_copy(src, dst, sem.at[len(moves) + len(stores)]))
            stores[-1].start()
    for store in stores:
        store.wait()


def arrange(output, grad_tokens, gains, shares):
    vmem = pl.BlockSpec(memory_space=pltpu.VMEM)
    hbm = pl.BlockSpec(memory_space=pl.ANY)
    outs = (
        ((ROWS, D), hbm),
        ((ROWS, D), hbm),
        ((1, D), vmem),
        ((3, 64, 512), hbm),
        ((64, 512), hbm),
        ((1, D), vmem),
        ((2, 64, FF), hbm),
        ((64, FF), hbm),
    )
    results = pl.pallas_call(
        arrange_kernel,
        out_shape=[jax.ShapeDtypeStruct(o[0], F32) for o in outs],
        in_specs=[hbm, hbm, vmem, hbm],
        out_specs=[o[1] for o in outs],
        scratch_shapes=[
            pltpu.VMEM((ROWS, D), F32),
            pltpu.VMEM((ROWS, D), F32),
            pltpu.VMEM((2, 64, ALL), F32),
            pltpu.SemaphoreType.DMA((22,)),
        ],
        compiler_params=pltpu.CompilerParams(vmem_limit_bytes=63 * 1024 * 1024),
        name="arrange",
    )(output, grad_tokens, gains, shares)
    output, grad_tokens, gain1, qkv, out, gain2, gate_up, down = results
    return output, grad_tokens, gain1.reshape(D), qkv, out.T, gain2.reshape(D), gate_up, down.T


def solution(mesh):
    placed = (
        P(("dp", "tensor"), None),
        P(),
        P(None, None, "tensor"),
        P("tensor", None),
        P(),
        P(None, None, "tensor"),
        P("tensor", None),
        P(("dp", "tensor"), None),
        P("dp"),
    )
    return jax.shard_map(
        block,
        mesh=mesh,
        in_specs=placed,
        out_specs=(
            P(("dp", "tensor"), None),
            P(("dp", "tensor"), None),
            P(),
            P(None, "dp", "tensor"),
            P("tensor", "dp"),
            P(),
            P(None, "dp", "tensor"),
            P("tensor", "dp"),
        ),
        check_vma=False,
    )
```

```python
import functools
import math

import jax
import jax.numpy as jnp
import numpy as np
from jax import lax
from jax.experimental import pallas as pl
from jax.experimental.pallas import tpu as pltpu
from jax.sharding import PartitionSpec as P

D = 2048
HD = 128
FF = 1408
ROWS = 128
SEQ = 512
HEADS = 4
EPS = 1e-05
BF = jnp.bfloat16
F32 = jnp.float32
MESH = pl.DeviceIdType.MESH
OFFS = (0, 3, 1, 2)
ORDER = ((0, 0), (0, 1), (1, 0), (2, 1), (1, 1), (2, 0), (3, 0), (3, 1))
UNIT = {half: i * 64 for i, half in enumerate(ORDER)}

CX = (384, 768, 128, 384)
CY = (384, 640, 128, 384)
COLS = tuple(a + b for a, b in zip(CX, CY))
BASE = (0, 768, 2176, 2432)
ALL = 3200


def nn(a, b):
    return lax.dot_general(a, b, (((1,), (0,)), ((), ())), preferred_element_type=F32)


def nt(a, b):
    return lax.dot_general(a, b, (((1,), (1,)), ((), ())), preferred_element_type=F32)


def tn(a, b):
    return lax.dot_general(a, b, (((0,), (0,)), ((), ())), preferred_element_type=F32)


def rotary_tables():
    half = HD // 2
    freq = np.exp(np.arange(half, dtype=np.float64) * (-2.0 * math.log(10000.0) / HD))
    angles = np.arange(SEQ, dtype=np.float64)[:, None] * freq
    cos, sin = np.cos(angles), np.sin(angles)
    return (
        np.concatenate([cos, cos], axis=1).astype(np.float32),
        np.concatenate([-sin, sin], axis=1).astype(np.float32),
    )


class Place:
    def __init__(self):
        self.dp = lax.axis_index("dp")
        self.t = lax.axis_index("tensor")
        self.c = self.dp % 2
        self.x = (self.dp // 2) % 4
        self.y = self.dp // 8

    def z(self, d):
        return (self.dp, (self.t + d) % 4)

    def xs(self, d):
        return (self.y * 8 + ((self.x + d) % 4) * 2 + self.c, self.t)

    def ys(self, d):
        return (((self.y + d) % 4) * 8 + self.x * 2 + self.c, self.t)

    def core(self):
        return (self.dp + 1 - 2 * self.c, self.t)


def remote(src, dst, ssem, rsem, device):
    return pltpu.make_async_remote_copy(
        src_ref=src, dst_ref=dst, send_sem=ssem, recv_sem=rsem, device_id=device, device_id_type=MESH
    )


def half_rows(place, slot, half):
    block = (place.t + OFFS[slot]) % 4
    return pl.ds(pl.multiple_of(block * 128 + half * 64, 64), 64)


def in_order(place, ref, cols):
    return jnp.concatenate([ref[half_rows(place, *half), cols] for half in ORDER], axis=0)


class Gather:
    def __init__(self, place, buf, ssem, rsem, relative):
        self.place, self.buf, self.ssem, self.rsem, self.relative = place, buf, ssem, rsem, relative

    def row(self, slot, half):
        if self.relative:
            return pl.ds(UNIT[slot, half], 64)
        return half_rows(self.place, slot, half)

    def copy(self, k):
        slot, half, to, there = (
            (0, 0, 1, 1),
            (0, 1, 1, 1),
            (0, 1, -1, 2),
            (0, 0, -1, 2),
            (1, 0, 1, 3),
            (2, 1, -1, 3),
        )[k]
        src = self.buf.at[self.row(slot, half)]
        dst = self.buf.at[self.row(there, half)] if self.relative else src
        return remote(src, dst, self.ssem.at[k], self.rsem.at[k], self.place.z(to))

    def start(self, *which):
        for k in which or (0, 2, 1, 3):
            self.copy(k).start()

    def relay(self):
        self.copy(0).wait_recv()
        self.copy(4).start()
        self.copy(2).wait_recv()
        self.copy(5).start()

    def near(self):
        self.copy(1).wait_recv()
        self.copy(3).wait_recv()

    def far(self):
        self.copy(4).wait_recv()
        self.copy(5).wait_recv()

    def done(self):
        for k in range(6):
            self.copy(k).wait_send()


class Scatter:
    def __init__(self, place, part, relays, recv, ssem, rsem):
        self.place, self.part, self.relays, self.recv = place, part, relays, recv
        self.ssem, self.rsem = ssem, rsem

    def rows(self, slot, half):
        return pl.ds(UNIT[slot, half], 64)

    def copy(self, k, n):
        part, relays, recv = self.part, self.relays, self.recv
        cols = pl.ds(pl.multiple_of(n * 512, 512), 512)
        src, dst, to = (
            (part.at[self.rows(3, 0), cols], relays.at[0, :, cols], 1),
            (part.at[self.rows(2, 1), cols], recv.at[0, self.rows(0, 1), cols], 1),
            (part.at[self.rows(3, 1), cols], relays.at[1, :, cols], -1),
            (part.at[self.rows(1, 0), cols], recv.at[1, self.rows(0, 0), cols], -1),
            (part.at[self.rows(2, 0), cols], recv.at[0, self.rows(0, 0), cols], 1),
            (part.at[self.rows(1, 1), cols], recv.at[1, self.rows(0, 1), cols], -1),
        )[k]
        sem = k * 4 + n
        return remote(src, dst, self.ssem.at[sem], self.rsem.at[sem], self.place.z(to))

    def start(self, n, *which):
        for k in which:
            self.copy(k, n).start()

    def relay(self, first, last):
        @pl.loop(first, last)
        def _(n):
            cols = pl.ds(pl.multiple_of(n * 512, 512), 512)
            for index, slot, half, out in ((0, 2, 0, 4), (1, 1, 1, 5)):
                self.copy(2 * index, n).wait_recv()
                rows = self.rows(slot, half)
                total = self.part[rows, cols].astype(F32) + self.relays[index, :, cols].astype(F32)
                self.part[rows, cols] = total.astype(BF)
                self.copy(out, n).start()

    def finish(self):
        @pl.loop(0, 4)
        def _(n):
            for k in (1, 3, 4, 5):
                self.copy(k, n).wait_recv()

    def total(self, rows):
        return (
            self.part[rows, :].astype(F32)
            + self.recv[0, rows, :].astype(F32)
            + self.recv[1, rows, :].astype(F32)
        )

    def done(self):
        @pl.loop(0, 4)
        def _(n):
            for k in range(6):
                self.copy(k, n).wait_send()


def sixteen(r):
    return pl.ds(pl.multiple_of(r * 16, 16), 16)


def own_rows(place, r):
    return pl.ds(pl.multiple_of(place.t * 128 + r * 16, 16), 16)


def kernel(names, *refs):
    ref = dict(zip(names, refs))
    place = Place()
    tok, cot, live = ref["tok"], ref["cot"], ref["lengths"]
    wq, wo, wgu, wd = ref["wq"], ref["wo"], ref["wgu"], ref["wd"]
    attn, qkv, probs, ctx = ref["attn"], ref["qkv"], ref["probs"], ref["ctx"]
    middle, mlp, masked, w3 = ref["middle"], ref["mlp"], ref["masked"], ref["w3"]
    pa, pb, branch = w3.at[0], w3.at[1], w3.at[2]
    hid, ggu, gctx, gproj, gmid = ref["hid"], ref["ggu"], ref["gctx"], ref["qkv"], ref["gmid"]
    cos_t, sin_t, gain1, gain2 = ref["cos"], ref["sin"], ref["gain1"], ref["gain2"]
    xa, xa0, xb0, xb1, xb2 = ref["xa"], ref["xa0"], ref["xb0"], ref["xb1"], ref["xb2"]
    r2, final, shares = ref["r2"], ref["final"], ref["shares"]
    gacc, grecv, gsum = ref["gacc"], ref["grecv"], ref["gsum"]
    zs, zr, lsem = ref["zs"], ref["zr"], ref["lsem"]
    live_rows = live[0]

    cot_load = pltpu.make_async_copy(cot, masked.at[0:ROWS], lsem.at[7])
    cot_load.start()

    loads = [pltpu.make_async_copy(ref["wq_h"].at[j], wq.at[:, j * 512 : (j + 1) * 512], lsem.at[j]) for j in range(3)]
    tables = [pltpu.make_async_copy(ref["cos_h"], cos_t, lsem.at[8])]
    tables.append(pltpu.make_async_copy(ref["sin_h"], sin_t, lsem.at[9]))
    loads.append(pltpu.make_async_copy(ref["wo_h"], wo, lsem.at[3]))
    loads += [pltpu.make_async_copy(ref["wgu_h"].at[j], wgu.at[:, j * FF : (j + 1) * FF], lsem.at[4 + j]) for j in range(2)]
    loads.append(pltpu.make_async_copy(ref["wd_h"], wd, lsem.at[6]))
    for load in tables + loads:
        load.start()

    barrier = pltpu.get_barrier_semaphore()
    partners = [place.z(d) for d in (1, 2, 3)]
    partners += [place.xs(d) for d in (1, 2, 3)] + [place.ys(d) for d in (1, 2, 3)] + [place.core()]
    for device in partners:
        pl.semaphore_signal(barrier, inc=1, device_id=device, device_id_type=MESH)

    @pl.loop(0, 8)
    def _(r):
        v = tok[sixteen(r), :].astype(F32)
        inv = lax.rsqrt(jnp.mean(v * v, axis=-1, keepdims=True) + EPS)
        attn[own_rows(place, r), :] = (v * inv * gain1[...]).astype(BF)

    pl.semaphore_wait(barrier, len(partners))

    ag1 = Gather(place, attn, zs.at[0], zr.at[0], False)
    agm = Gather(place, masked, zs.at[1], zr.at[1], True)
    ag2 = Gather(place, mlp, zs.at[2], zr.at[2], True)
    ag4 = Gather(place, branch, zs.at[3], zr.at[3], False)
    rs3 = Scatter(place, pa, ref["relay_a"], ref["recv_a"], zs.at[5], zr.at[5])
    rs4 = Scatter(place, pa, ref["relay_a"], ref["recv_a"], zs.at[6], zr.at[6])
    rs2 = Scatter(place, pb, ref["relay_b"], ref["recv_b"], zs.at[7], zr.at[7])

    ws, wr = ref["ws"], ref["wr"]
    halves = (slice(0, 1024), slice(1024, 2048))
    minor, major = (place.x, place.y), (place.y, place.x)

    def w_rows(half, at, count):
        first = (at * 2 + place.c) * 64
        if count == 16:
            first = first + minor[half] * 16
        return pl.ds(pl.multiple_of(first, 16), count)

    def w_first(half, d):
        rows, k = w_rows(half, major[half], 16), half * 3 + d - 1
        dst = w3.at[d - 1, rows, halves[half]]
        return remote(ref["wo_h"].at[rows, halves[half]], dst, ws.at[k], wr.at[k], place.z(d))

    def w_plane(half, phase, d):
        part = w3.at[:, w_rows(half, major[half], (16, 64)[phase]), halves[half]]
        k = 6 + (phase * 2 + half) * 3 + d - 1
        device = (place.xs, place.ys)[half ^ phase](d)
        return remote(part, part, ws.at[k], wr.at[k], device)

    def w_core(half, d):
        part = w3.at[:, w_rows(half, (major[half] + d) % 4, 64), halves[half]]
        return remote(part, part, ws.at[18 + half * 4 + d], wr.at[18 + half * 4 + d], place.core())

    both = [(half, d) for d in (1, 3, 2) for half in range(2)]
    for half, d in both:
        w_first(half, d).start()
    ag1.start()
    cot_load.wait()

    @pl.loop(0, 8)
    def _(r):
        at = place.t * ROWS + r * 16 + lax.broadcasted_iota(jnp.int32, (16, 1), 0)
        v = masked[sixteen(r), :].astype(F32)
        masked[sixteen(r), :] = jnp.where(at < live_rows, v, 0.0).astype(BF)

    def project(slot):
        block = (place.t + OFFS[slot]) % 4
        rows = pl.ds(pl.multiple_of(block * 128, 128), 128)
        for j in range(3):
            p = nn(attn[rows, :], wq[:, j * 512 : (j + 1) * 512])
            if j == 2:
                qkv[rows, 1024:1536] = p.astype(BF)
                continue
            for h in range(HEADS):
                v = p[:, h * HD : (h + 1) * HD]
                v = v * cos_t[rows, :] + pltpu.roll(v, 64, 1) * sin_t[rows, :]
                if j == 0:
                    v = v * HD ** (-0.5)
                qkv[rows, j * 512 + h * HD : j * 512 + (h + 1) * HD] = v.astype(BF)

    for load in tables + loads[:3]:
        load.wait()
    project(0)
    for half, d in both:
        w_first(half, d).wait_recv()
    for half, d in both:
        w_plane(half, 0, d).start()
    ag1.relay()
    for half, d in both:
        w_plane(half, 0, d).wait_recv()
    for half, d in both:
        w_plane(half, 1, d).start()
    for half in range(2):
        w_core(half, 0).start()
    ag1.near()
    agm.start(0, 2)
    project(1)
    project(2)
    ag1.far()
    project(3)
    for half, d in both[:4]:
        w_plane(half, 1, d).wait_recv()
        w_core(half, 4 - d).start()

    heads = ref["recv_a"].at[0]

    def to_rows(d, pair):
        src = ctx.at[pl.ds(pl.multiple_of(((place.t + d) % 4) * 128, 128), 128), pair * 256 : pair * 256 + 256]
        dst = heads.at[:, pl.ds(pl.multiple_of(place.t * 512 + pair * 256, 256), 256)]
        sem = pair * 3 + d - 1
        return remote(src, dst, zs.at[4, sem], zr.at[4, sem], place.z(d))

    def heads_forward(h):
        def cols(j):
            return pl.ds(pl.multiple_of(j * 512 + h * HD, HD), HD)

        for q in range(2):
            rows, keys = pl.ds(q * 256, 256), (q + 1) * 256
            scores = nt(qkv[rows, cols(0)], qkv[0:keys, cols(1)])
            at = q * 256 + lax.broadcasted_iota(jnp.int32, (256, keys), 0)
            key = lax.broadcasted_iota(jnp.int32, (256, keys), 1)
            scores = jnp.where((key <= at) & (key < live_rows), scores, -1e30)
            e = jnp.exp(scores - jnp.max(scores, axis=-1, keepdims=True))
            p = (e * (1.0 / jnp.sum(e, axis=-1, keepdims=True))).astype(BF)
            probs[h, rows, 0:keys] = p
            ctx[rows, cols(0)] = nn(p, qkv[0:keys, cols(2)]).astype(BF)

    for pair in range(2):
        pl.loop(2 * pair, 2 * pair + 2)(heads_forward)
        for d in (2, 1, 3):
            to_rows(d, pair).start()
    own = pl.ds(pl.multiple_of(place.t * 128, 128), 128)
    heads[:, pl.ds(pl.multiple_of(place.t * 512, 512), 512)] = ctx[own, :]
    for half, d in both[4:]:
        w_plane(half, 1, d).wait_recv()
        w_core(half, 4 - d).start()
    loads[3].wait()
    agm.start(1, 3)

    other = 1 - place.c
    xs, xr = ref["xs"], ref["xr"]

    def swap_a(group):
        src = (masked, mlp, branch, attn)[group]
        return remote(src, xa.at[group], xs.at[group], xr.at[group], place.core())

    def swap_branch(slot):
        block = (place.t + OFFS[slot]) % 4
        rows = pl.ds(pl.multiple_of(block * 128, 128), 128)
        sem = (2, 15, 16, 17)[slot]
        return remote(branch.at[rows], xa.at[2, rows], xs.at[sem], xr.at[sem], place.core())

    def swap_masked(part):
        rows = (slice(0, 384), slice(384, 512))[part]
        sem = (0, 14)[part]
        return remote(masked.at[rows], xa0.at[rows], xs.at[sem], xr.at[sem], place.core())

    def swap_b(k):
        rows = pl.ds((0, 256, 0, 256, 0, 0)[k], 256 if k < 4 else 512)
        if k < 2:
            src = hid.at[rows, pl.ds(pl.multiple_of(other * 640, 128), 768)]
        elif k < 4:
            src = ggu.at[rows, pl.ds(pl.multiple_of(other * FF, 128), FF)]
        elif k == 4:
            src = ctx.at[rows, pl.ds(pl.multiple_of(other * 256, 256), 256)]
        else:
            src = gproj.at[rows, pl.ds(pl.multiple_of(other * 768, 256), 768)]
        dst = (xb0, xb0, xb1, xb1, xb2, xb0)[k].at[rows]
        return remote(src, dst, xs.at[4 + k], xr.at[4 + k], place.core())

    swap_a(3).start()
    swap_b(4).start()

    for half in range(2):
        for d in range(4):
            w_core(half, d).wait_recv()
    w3_keep = pltpu.make_async_copy(w3, ref["w3_h"], lsem.at[8])
    w3_keep.start()
    for pair in range(2):
        for d in (1, 2, 3):
            to_rows(d, pair).wait_recv()

    @pl.loop(0, 4)
    def _(n):
        at = pl.ds(pl.multiple_of(n * 512, 512), 512)

        def share(d, weights):
            return nn(heads[:, pl.ds(pl.multiple_of(((place.t + d) % 4) * 512, 512), 512)], weights)

        out = share(0, wo[:, at]) + share(3, w3[0, :, at]) + share(2, w3[1, :, at]) + share(1, w3[2, :, at])
        middle[:, at] = tok[:, at].astype(F32) + out

    @pl.loop(0, 8)
    def _(r):
        rows = sixteen(r)
        v = middle[rows, :]
        inv = lax.rsqrt(jnp.mean(v * v, axis=-1, keepdims=True) + EPS)
        mlp[rows, :] = (v * inv * gain2[...]).astype(BF)

    for pair in range(2):
        for d in (1, 2, 3):
            to_rows(d, pair).wait_send()
    for half, d in both:
        w_first(half, d).wait_send()
        w_plane(half, 0, d).wait_send()
        w_plane(half, 1, d).wait_send()
    for half in range(2):
        for d in range(4):
            w_core(half, d).wait_send()
    ag2.start()
    for load in loads[4:]:
        load.wait()

    own_b = (
        hid.at[:, pl.ds(pl.multiple_of(place.c * 640, 128), 768)],
        ggu.at[:, pl.ds(pl.multiple_of(place.c * FF, 128), FF)],
        ctx.at[:, pl.ds(pl.multiple_of(place.c * 256, 256), 256)],
        gproj.at[:, pl.ds(pl.multiple_of(place.c * 768, 256), 768)],
    )
    own_a = (masked, mlp, branch, attn)
    other_a = (xa0, pb, wd.at[0:512], wd.at[512:1024])
    other_b = (xb0, xb1, xb2, xb0)
    osem = ref["osem"]

    def bring(group):
        return pltpu.make_async_copy(xa.at[group], other_a[group], osem.at[group])

    def fetch(group):
        if group == 2:
            for slot in range(1, 4):
                swap_branch(slot).wait_recv()
        else:
            swap_a(group).wait_recv()
        bring(group).start()

    def piece(group, axis, tile, first, count):
        if group == 3 and axis == 1:
            return mlp.at[pl.ds(first, count), pl.ds(pl.multiple_of(tile * 384, 128), 384)]
        base = (FF, 0, FF + 768, FF + 1024)[group]
        lo = base if axis == 0 else base + CX[group]
        width = CX[group] if axis == 0 else CY[group]
        rows = pl.ds(pl.multiple_of(tile * 512 + first, min(count, 128)), count)
        return wgu.at[rows, lo : lo + width]

    p1xs, p1xr, p1ys, p1yr = ref["p1xs"], ref["p1xr"], ref["p1ys"], ref["p1yr"]

    def relayed(group, axis):
        if group < 2:
            return ref[("relx", "rely")[axis] + str(group)]
        lo = ((768, 896), (0, 384))[group - 2][axis]
        return xb1.at[:, lo : lo + CX[group]]

    def arrived(group, axis, side):
        if group < 2:
            return ref[("recx", "recy")[axis] + str(group)].at[side]
        width = CX[group]
        lo = ((1536, 1792), (0, 768))[group - 2][axis] + side * width
        return xa0.at[:, pl.ds(lo if isinstance(lo, int) else pl.multiple_of(lo, 128), width)]

    def tile_of(step):
        return (place.y + jnp.where(step == 0, 2, jnp.where(step == 1, 1, jnp.where(step == 2, 3, 0)))) % 4

    def send_x(group, kind, step):
        tile, to = tile_of(step), 1 - 2 * (step % 2)
        rows = pl.ds(pl.multiple_of(tile * 128, 128), 128)
        if kind == 0:
            block, dst = place.x + 2, relayed(group, 0).at[rows]
        elif kind == 1:
            block, dst, to = place.x + 4 - to, arrived(group, 0, (1 + to) // 2).at[rows], -to
        else:
            block, dst = place.x + 4 + to, arrived(group, 0, (1 - to) // 2).at[rows]
        src = piece(group, 0, tile, pl.multiple_of((block % 4) * 128, 128), 128)
        sem = (group * 3 + kind) * 4 + step
        return remote(src, dst, p1xs.at[sem], p1xr.at[sem], place.xs(4 + to))

    def send_y(group, k):
        offset, first, dst, to = (
            (2, 0, relayed(group, 1).at[0:256], 1),
            (1, 256, arrived(group, 1, 0).at[256:512], 1),
            (2, 256, relayed(group, 1).at[256:512], 3),
            (3, 0, arrived(group, 1, 1).at[0:256], 3),
            (1, 0, arrived(group, 1, 0).at[0:256], 1),
            (3, 256, arrived(group, 1, 1).at[256:512], 3),
        )[k]
        src = piece(group, 1, (place.y + offset) % 4, first, 256)
        return remote(src, dst, p1ys.at[group * 6 + k], p1yr.at[group * 6 + k], place.ys(to))

    def gradient(group, step):
        tile = tile_of(step)
        at = pl.ds(pl.multiple_of(tile * 512, 512), 512)
        lo = 0
        for axis, width in ((0, CX[group]), (1, CY[group])):
            own, oth = own_b[group].at[:, lo : lo + width], other_b[group].at[:, lo : lo + width]
            out = tn(own_a[group][:, at], own[...]) + tn(other_a[group][:, at], oth[...])
            piece(group, axis, tile, 0, 512)[...] = out.astype(BF)
            lo += width
        send_x(group, 0, step).start()

        @pl.when(step == 0)
        def _():
            send_y(group, 0).start()
            send_y(group, 2).start()

    def near_x(group, step):
        send_x(group, 1, step).start()

    def near_y(group, step):
        for when in (1, 2):

            @pl.when(step == when)
            def _():
                send_y(group, 2 * when - 1).start()

    def all_near(group, *axes):
        @pl.loop(0, 4)
        def _(step):
            for axis in axes:
                (near_x, near_y)[axis](group, step)

    lands = ref["lands"]

    def mid_copies(group):
        if group > 1:
            return ()
        return (
            pltpu.make_async_copy(relayed(group, 0), hid.at[:, 0 : CX[group]], lands.at[16 + group]),
            pltpu.make_async_copy(relayed(group, 1), hid.at[:, 768 : 768 + CY[group]], lands.at[20 + group]),
        )

    def mid_start(group):
        for step in range(4):
            send_x(group, 0, step).wait_recv()
        for k in (0, 2):
            send_y(group, k).wait_recv()
        for copy in mid_copies(group):
            copy.start()

    def mid_end(group):
        for copy in mid_copies(group):
            copy.wait()

        def add(axis, tile, first, rows, lo, width, count):
            src = hid.at[:, lo : lo + width] if group < 2 else relayed(group, axis)

            @pl.loop(0, count // 32)
            def _(i):
                own = piece(group, axis, tile, pl.multiple_of(first + i * 32, 32), 32)
                got = src[pl.ds(pl.multiple_of(rows + i * 32, 32), 32), :]
                own[...] = (own[...].astype(F32) + got.astype(F32)).astype(BF)

        for step in range(4):
            to, tile = (1, 3)[step % 2], tile_of(step)
            add(0, tile, ((place.x + to) % 4) * 128, tile * 128, 0, CX[group], 128)
            send_x(group, 2, step).start()
        for k, offset, first in ((4, 1, 0), (5, 3, 256)):
            add(1, (place.y + offset) % 4, first, first, 768, CY[group], 256)
            send_y(group, k).start()

    def feed(first, count):
        rows = slice(first, first + count)
        for n0, n1 in ((0, 512), (512, 1024), (1024, 1408)):
            gate = nn(mlp[rows, :], wgu[:, n0:n1])
            up = nn(mlp[rows, :], wgu[:, FF + n0 : FF + n1])
            sig = jax.nn.sigmoid(gate)
            silu = gate * sig
            hid[rows, n0:n1] = (silu * up).astype(BF)
            ggu[rows, n0:n1] = (up * sig * (1.0 + gate * (1.0 - sig))).astype(BF)
            ggu[rows, FF + n0 : FF + n1] = silu.astype(BF)

    def feed_back(first, count):
        rows = slice(first, first + count)
        for n0, n1 in ((0, 512), (512, 1024), (1024, 1408)):
            grad = nt(masked[rows, :], wd[n0:n1, :])
            for lo in (0, FF):
                ggu[rows, lo + n0 : lo + n1] = (grad * ggu[rows, lo + n0 : lo + n1].astype(F32)).astype(BF)

    def feed_part(first, count, *sends):
        rows = slice(first, first + count)

        @pl.loop(0, 4)
        def _(n):
            at = pl.ds(pl.multiple_of(n * 512, 512), 512)
            rs3.part[rows, at] = nt(ggu[rows, :], wgu[at, :]).astype(BF)
            rs3.start(n, *sends)

    feed(0, 128)
    feed_back(0, 128)
    w3_keep.wait()
    feed_part(0, 128)
    w3_back = []
    for j in range(3):
        rows, cols = slice(j * 512, (j + 1) * 512), slice(j * 512, (j + 1) * 512)
        kept = ref["w3_h"].at[j]
        w3_back.append(pltpu.make_async_copy(kept.at[:, 0:1536], wq.at[rows], osem.at[4 + j]))
        w3_back.append(pltpu.make_async_copy(kept.at[:, 1536:2048], wq.at[1536:2048, cols], osem.at[7 + j]))
    for copy in w3_back:
        copy.start()
    ag2.relay()
    agm.near()
    agm.relay()
    swap_masked(0).start()
    feed(128, 128)
    feed_back(128, 128)
    feed_part(128, 128, 1, 3)
    swap_b(0).start()
    swap_b(2).start()
    ag2.near()
    ag2.far()
    swap_a(1).start()
    feed(256, 256)
    swap_b(1).start()
    agm.far()
    swap_masked(1).start()
    feed_back(256, 256)
    swap_b(3).start()
    fetch(1)
    late, taken = slice(256, 512), slice(FF, FF + COLS[0])

    @pl.loop(0, 4)
    def _(n):
        at = pl.ds(pl.multiple_of(n * 512, 512), 512)
        rs3.part[late, at] = nt(ggu[late, taken], wgu[at, taken]).astype(BF)

    swap_b(0).wait_recv()
    swap_b(1).wait_recv()
    swap_masked(0).wait_recv()
    swap_masked(1).wait_recv()

    @pl.loop(0, 2)
    def _(step):
        gradient(0, step)
        near_x(0, step)
        near_y(0, step)

    @pl.loop(0, 4)
    def _(n):
        at = pl.ds(pl.multiple_of(n * 512, 512), 512)
        part = nt(ggu[late, 0:FF], wgu[at, 0:FF]) + nt(ggu[late, FF + COLS[0] :], wgu[at, FF + COLS[0] :])
        rs3.part[late, at] = (part + rs3.part[late, at].astype(F32)).astype(BF)
        rs3.start(n, 0, 2)

    @pl.loop(2, 4)
    def _(step):
        gradient(0, step)
        near_x(0, step)
        near_y(0, step)

    rs3.relay(0, 3)
    bring(1).wait()
    swap_b(2).wait_recv()
    swap_b(3).wait_recv()

    def gate_up(step):
        gradient(1, step)
        near_x(1, step)
        near_y(1, step)

    gate_up(0)
    rs3.relay(3, 4)
    pl.loop(1, 3)(gate_up)
    p2xs, p2xr, p2ys, p2yr = ref["p2xs"], ref["p2xr"], ref["p2ys"], ref["p2yr"]

    def landing(group):
        copies = []
        for d in range(2 if group < 2 else 0):
            for axis in range(2):
                lo = d * FF + axis * 768
                width = CX[group] if axis == 0 else CY[group]
                sem = lands.at[group * 4 + d * 2 + axis]
                copies.append(pltpu.make_async_copy(arrived(group, axis, d), ggu.at[:, lo : lo + width], sem))
        return copies

    def send_2(group, axis, d):
        sem = group * 3 + d - 1
        own = pl.multiple_of(place.x * 128, 128)
        if axis == 0:
            src = piece(group, 0, (place.y + d) % 4, own, 128)
            dst = r2.at[d - 1, :, BASE[group] : BASE[group] + CX[group]]
            return remote(src, dst, p2xs.at[sem], p2xr.at[sem], place.ys(d))
        src = piece(group, 1, place.y, pl.multiple_of(((place.x + d) % 4) * 128, 128), 128)
        dst = r2.at[d - 1, :, BASE[group] + CX[group] : BASE[group] + COLS[group]]
        return remote(src, dst, p2ys.at[sem], p2yr.at[sem], place.xs(d))

    q2s, q2r = ref["q2s"], ref["q2r"]

    def send_3(group, axis, k):
        lo = BASE[group] + (0 if axis == 0 else CX[group])
        cols = slice(lo, lo + (CX[group] if axis == 0 else CY[group]))
        offset, first, slot, to = ((2, 0, 2, 1), (1, 64, 0, 1), (2, 64, 2, 3), (3, 0, 1, 3), (1, 0, 0, 1), (3, 64, 1, 3))[k]
        if axis == 0:
            src = piece(group, 0, (place.y + offset) % 4, pl.multiple_of(place.x * 128 + first, 64), 64)
        else:
            src = piece(group, 1, place.y, pl.multiple_of(((place.x + offset) % 4) * 128 + first, 64), 64)
        device = (place.ys, place.xs)[axis](to)
        sem = (group * 2 + axis) * 6 + k
        return remote(src, r2.at[slot, first : first + 64, cols], q2s.at[sem], q2r.at[sem], device)

    def mid_second(group):
        for axis in range(2):
            lo = BASE[group] + (0 if axis == 0 else CX[group])
            cols = slice(lo, lo + (CX[group] if axis == 0 else CY[group]))
            for k, out, offset, first in ((0, 4, 1, 0), (2, 5, 3, 64)):
                send_3(group, axis, k).wait_recv()
                if axis == 0:
                    own = piece(group, 0, (place.y + offset) % 4, pl.multiple_of(place.x * 128 + first, 64), 64)
                else:
                    own = piece(group, 1, place.y, pl.multiple_of(((place.x + offset) % 4) * 128 + first, 64), 64)
                got = r2[2, first : first + 64, cols]
                own[...] = (own[...].astype(F32) + got.astype(F32)).astype(BF)
                send_3(group, axis, out).start()

    def land(group):
        for step in range(4):
            for kind in (1, 2):
                send_x(group, kind, step).wait_recv()
        for k in (1, 3, 4, 5):
            send_y(group, k).wait_recv()
        for copy in landing(group):
            copy.start()

    def first_sum(group):
        for copy in landing(group):
            copy.wait()
        for axis in range(2):
            lo = axis * 768
            width = CX[group] if axis == 0 else CY[group]
            if group < 2:
                got = [ggu.at[:, d * FF + lo : d * FF + lo + width] for d in range(2)]
            else:
                got = [arrived(group, axis, d) for d in range(2)]

            @pl.loop(0, 16)
            def _(i):
                if axis == 0:
                    own = piece(group, 0, i // 4, pl.multiple_of(place.x * 128 + (i % 4) * 32, 32), 32)
                else:
                    own = piece(group, 1, place.y, pl.multiple_of(i * 32, 32), 32)
                rows = pl.ds(pl.multiple_of(i * 32, 32), 32)
                total = own[...].astype(F32)
                for d in range(2):
                    total = total + got[d][rows, :].astype(F32)
                own[...] = total.astype(BF)

            if group < 2:
                for k in (0, 2, 1, 3):
                    send_3(group, axis, k).start()
            else:
                for d in (2, 1, 3):
                    send_2(group, axis, d).start()

    def whole_of(group):
        return ((final, 0), (middle, 0), (final, 768), (final, 1024))[group]

    def ending(group):
        ref_at, first = whole_of(group)
        cols = slice(first, first + COLS[group])
        mine = ref_at.at[pl.ds(pl.multiple_of(place.c * 64, 64), 64), cols]
        theirs = ref_at.at[pl.ds(pl.multiple_of(other * 64, 64), 64), cols]
        dst = shares.at[place.c, :, BASE[group] : BASE[group] + COLS[group]]
        return (
            remote(theirs, dst, xs.at[10 + group], xr.at[10 + group], place.core()),
            pltpu.make_async_copy(mine, dst, lsem.at[9 + group]),
        )

    def second_sum(group):
        for axis in range(2):
            if group < 2:
                for k in (1, 3, 4, 5):
                    send_3(group, axis, k).wait_recv()
            else:
                for d in (1, 2, 3):
                    send_2(group, axis, d).wait_recv()
            lo = BASE[group] + (0 if axis == 0 else CX[group])
            width = CX[group] if axis == 0 else CY[group]
            whole, first = whole_of(group)
            first += lo - BASE[group]

            @pl.loop(0, 4)
            def _(i):
                rows = pl.ds(pl.multiple_of(i * 32, 32), 32)
                own = piece(group, axis, place.y, pl.multiple_of(place.x * 128 + i * 32, 32), 32)
                total = own[...].astype(F32)
                for d in range(2 if group < 2 else 3):
                    total = total + r2[d, rows, lo : lo + width].astype(F32)
                whole[rows, first : first + width] = total
        for copy in ending(group):
            copy.start()

    rs3.finish()

    def fold(v):
        return jnp.concatenate([v[:, i * 512 : (i + 1) * 512] for i in range(4)], axis=0)

    def mlp_back(r, total):
        rows = sixteen(r)
        grad = rs3.total(rows)
        v = middle[rows, :]
        inv = lax.rsqrt(jnp.mean(v * v, axis=-1, keepdims=True) + EPS)
        scaled = grad * gain2[...]
        back = (
            masked[rows, :].astype(F32)
            + inv * scaled
            - v * (inv * inv * inv) * jnp.mean(v * scaled, axis=-1, keepdims=True)
        )
        gmid[rows, :] = back
        branch[own_rows(place, r), :] = back.astype(BF)
        return total + jnp.sum(grad * v * inv, axis=0, keepdims=True)

    gain2_part = lax.fori_loop(0, 8, mlp_back, jnp.zeros((1, D), F32))
    gacc[0, 4:8, :] = fold(gain2_part)
    agm.done()
    swap_masked(0).wait_send()
    swap_masked(1).wait_send()
    for copy in w3_back:
        copy.wait()
    own = pl.ds(pl.multiple_of(place.t * 128, 128), 128)

    def to_heads(j):
        src = masked.at[128:256, j * 512 : (j + 1) * 512]
        return remote(src, gctx.at[own], zs.at[4, 6 + j], zr.at[4, 6 + j], place.z(3 - j))

    for j in (1, 0, 2):
        at = slice(j * 512, (j + 1) * 512)
        part = nt(branch[own, 0:1536], wq[at, :]) + nt(branch[own, 1536:2048], wq[1536:2048, at])
        masked[128:256, at] = part.astype(BF)
        to_heads(j).start()
    gctx[own, :] = nt(branch[own, :], wo[...]).astype(BF)
    ag4.start()
    for load in loads[:3]:
        load.start()
    swap_branch(0).start()
    rs3.done()

    gate_up(3)

    @pl.loop(0, 4)
    def _(n):
        at = pl.ds(pl.multiple_of(n * 512, 512), 512)
        rs2.part[:, at] = nn(hid[...], wd[:, at]).astype(BF)

    fetch(3)
    for k in (0, 1, 2, 3):
        swap_b(k).wait_send()
    mid_start(0)
    mid_end(0)
    mid_start(1)
    mid_end(1)
    ag4.relay()
    for pair in ((0, 2), (1, 3)):

        @pl.loop(0, 4)
        def _(n):
            rs2.start(n, *pair)

    for j in range(3):
        to_heads(j).wait_recv()

    def turn_back(v, rows):
        return v * cos_t[rows, :] - pltpu.roll(v, 64, 1) * sin_t[rows, :]

    def heads_back(h):
        def cols(j):
            return pl.ds(pl.multiple_of(j * 512 + h * HD, HD), HD)

        def part(q):
            rows, keys = pl.ds(q * 256, 256), (q + 1) * 256
            p = probs[h, rows, 0:keys]
            grad = gctx[rows, cols(0)]
            wide = p.astype(F32)
            gp = nt(grad, qkv[0:keys, cols(2)])
            gs = (wide * (gp - jnp.sum(wide * gp, axis=-1, keepdims=True))).astype(BF)
            gq = (turn_back(nn(gs, qkv[0:keys, cols(1)]), rows) * HD ** (-0.5)).astype(BF)
            return gq, tn(gs, qkv[rows, cols(0)]), tn(p, grad)

        q1, k1, v1 = part(1)
        q0, k0, v0 = part(0)
        lo, hi = slice(0, 256), slice(256, 512)
        k0, k1 = turn_back(k0 + k1[lo], lo).astype(BF), turn_back(k1[hi], hi).astype(BF)
        v0, v1 = (v0 + v1[lo]).astype(BF), v1[hi].astype(BF)
        for j, low, high in ((0, q0, q1), (1, k0, k1), (2, v0, v1)):
            gproj[lo, cols(j)] = low
            gproj[hi, cols(j)] = high

    pl.loop(0, HEADS)(heads_back)
    swap_branch(0).wait_recv()
    swap_b(5).start()
    land(0)
    for load in loads[:3]:
        load.wait()
    first_sum(0)
    swap_a(1).wait_send()
    ag2.done()
    bring(3).wait()
    swap_b(5).wait_recv()

    @pl.loop(0, 4)
    def _(step):
        gradient(3, step)

    all_near(3, 0, 1)
    ag4.near()
    ag4.far()
    for slot in (1, 2, 3):
        swap_branch(slot).start()
    @pl.loop(0, 4)
    def _(n):
        at = pl.ds(pl.multiple_of(n * 512, 512), 512)
        part = nt(in_order(place, gproj, slice(None)), wq[at, :])
        rs4.part[:, at] = part.astype(BF)
        seen = jnp.sum(part * in_order(place, attn, at).astype(F32), axis=0, keepdims=True)
        gsum[n] = jnp.broadcast_to(seen, (8, 512))

    for n in range(4):
        at = slice(n * 512, (n + 1) * 512)
        gacc[0, n : n + 1, :] = gsum[n, 0:1, :] / gain1[:, at]
    gs, gr = ref["gs"], ref["gr"]

    def spread(stage):
        count = 2 if stage == 3 else 4
        me = (place.t, place.x, place.y, place.c)[stage]
        out = []
        for d in range(1, count):
            device = (place.z, place.xs, place.ys, lambda _: place.core())[stage](d)
            k = stage * 3 + d - 1
            out.append(remote(gacc.at[stage], grecv.at[stage * 4 + me], gs.at[k], gr.at[k], device))
        return out, count, me

    def spread_start(stage):
        copies, _, me = spread(stage)
        grecv[stage * 4 + me] = gacc[stage]
        for copy in copies:
            copy.start()

    def spread_end(stage):
        copies, count, _ = spread(stage)
        for copy in copies:
            copy.wait_recv()
        total = grecv[stage * 4]
        for i in range(1, count):
            total = total + grecv[stage * 4 + i]
        gacc[stage + 1] = total

    spread_start(0)
    for pair in ((0, 2), (1, 3)):

        @pl.loop(0, 4)
        def _(n):
            rs4.start(n, *pair)

    rs2.relay(0, 4)
    mid_second(0)
    fetch(2)
    mid_start(3)
    mid_end(3)
    swap_b(4).wait_recv()
    bring(2).wait()

    @pl.loop(0, 4)
    def _(step):
        gradient(2, step)

    all_near(2, 0, 1)
    spread_end(0)
    spread_start(1)
    land(1)
    first_sum(1)
    mid_start(2)
    mid_end(2)
    land(3)
    first_sum(3)
    mid_second(1)
    rs4.relay(0, 4)
    spread_end(1)
    spread_start(2)
    rs2.finish()

    @pl.loop(0, 8)
    def _(r):
        rows = sixteen(r)
        middle[rows, :] = middle[rows, :] + rs2.total(rows)

    out_copy = pltpu.make_async_copy(middle, ref["output"], lsem.at[7])
    out_copy.start()
    second_sum(0)
    land(2)
    first_sum(2)
    out_copy.wait()
    second_sum(1)
    spread_end(2)
    spread_start(3)
    second_sum(3)
    second_sum(2)
    rs4.finish()

    def tok_copy(r):
        rows = sixteen(r)
        return pltpu.make_async_copy(gmid.at[rows], ref["grad_tokens"].at[rows], lsem.at[13 + r])

    @pl.loop(0, 8)
    def _(r):
        rows = sixteen(r)
        grad = rs4.total(rows)
        v = tok[rows, :].astype(F32)
        inv = lax.rsqrt(jnp.mean(v * v, axis=-1, keepdims=True) + EPS)
        scaled = grad * gain1[...]
        gmid[rows, :] = (
            gmid[rows, :]
            + inv * scaled
            - v * (inv * inv * inv) * jnp.mean(v * scaled, axis=-1, keepdims=True)
        )
        tok_copy(r).start()

    spread_end(3)
    ref["gains"][...] = gacc[4]

    for j in range(3):
        to_heads(j).wait_send()
    for gather in (ag1, ag4):
        gather.done()
    rs4.done()
    rs2.done()
    swap_a(3).wait_send()
    for slot in range(4):
        swap_branch(slot).wait_send()
    for k in (4, 5):
        swap_b(k).wait_send()
    for group in range(4):
        for step in range(4):
            for kind in range(3):
                send_x(group, kind, step).wait_send()
        for k in range(6):
            send_y(group, k).wait_send()
        for axis in range(2):
            if group < 2:
                for k in range(6):
                    send_3(group, axis, k).wait_send()
            else:
                for d in (1, 2, 3):
                    send_2(group, axis, d).wait_send()
    for stage in range(4):
        for copy in spread(stage)[0]:
            copy.wait_send()
    for r in range(8):
        tok_copy(r).wait()
    for group in range(4):
        for copy in ending(group):
            copy.wait()


def block(tokens, gain_attn, w_qkv, w_out, gain_mlp, w_gate_up, w_down, cotangent, lengths):
    cos_t, sin_t = rotary_tables()
    vmem = pl.BlockSpec(memory_space=pltpu.VMEM)
    smem = pl.BlockSpec(memory_space=pltpu.SMEM)
    hbm = pl.BlockSpec(memory_space=pl.ANY)
    ins = [
        ("tok", tokens, vmem),
        ("gain1", gain_attn.reshape(1, D), vmem),
        ("wq_h", w_qkv, hbm),
        ("wo_h", w_out, hbm),
        ("gain2", gain_mlp.reshape(1, D), vmem),
        ("wgu_h", w_gate_up, hbm),
        ("wd_h", w_down, hbm),
        ("cot", cotangent, hbm),
        ("lengths", lengths, smem),
        ("cos_h", jnp.asarray(cos_t), hbm),
        ("sin_h", jnp.asarray(sin_t), hbm),
    ]
    outs = [
        ("output", (ROWS, D), F32, hbm),
        ("grad_tokens", (ROWS, D), F32, hbm),
        ("gains", (8, 512), F32, vmem),
        ("shares", (2, 64, ALL), F32, hbm),
        ("xa", (4, SEQ, D), BF, hbm),
        ("w3_h", (3, SEQ, D), BF, hbm),
    ]
    outs += [(f"relx{g}", (SEQ, CX[g]), BF, hbm) for g in range(2)]
    outs += [(f"rely{g}", (SEQ, CY[g]), BF, hbm) for g in range(2)]
    outs += [(f"recx{g}", (2, SEQ, CX[g]), BF, hbm) for g in range(2)]
    outs += [(f"recy{g}", (2, SEQ, CY[g]), BF, hbm) for g in range(2)]
    dma = pltpu.SemaphoreType.DMA
    scratch = [
        ("wq", pltpu.VMEM((D, 1536), BF)),
        ("wo", pltpu.VMEM((512, D), BF)),
        ("wgu", pltpu.VMEM((D, 2 * FF), BF)),
        ("wd", pltpu.VMEM((FF, D), BF)),
        ("attn", pltpu.VMEM((SEQ, D), BF)),
        ("qkv", pltpu.VMEM((SEQ, 1536), BF)),
        ("probs", pltpu.VMEM((HEADS, SEQ, SEQ), BF)),
        ("ctx", pltpu.VMEM((SEQ, 512), BF)),
        ("middle", pltpu.VMEM((ROWS, D), F32)),
        ("mlp", pltpu.VMEM((SEQ, D), BF)),
        ("masked", pltpu.VMEM((SEQ, D), BF)),
        ("hid", pltpu.VMEM((SEQ, FF), BF)),
        ("ggu", pltpu.VMEM((SEQ, 2 * FF), BF)),
        ("gctx", pltpu.VMEM((SEQ, 512), BF)),
        ("xa0", pltpu.VMEM((SEQ, D), BF)),
        ("xb0", pltpu.VMEM((SEQ, COLS[0]), BF)),
        ("xb1", pltpu.VMEM((SEQ, COLS[1]), BF)),
        ("xb2", pltpu.VMEM((SEQ, COLS[2]), BF)),
        ("gmid", pltpu.VMEM((ROWS, D), F32)),
        ("w3", pltpu.VMEM((3, SEQ, D), BF)),
        ("relay_a", pltpu.VMEM((2, 64, D), BF)),
        ("recv_a", pltpu.VMEM((2, ROWS, D), BF)),
        ("relay_b", pltpu.VMEM((2, 64, D), BF)),
        ("recv_b", pltpu.VMEM((2, ROWS, D), BF)),
        ("r2", pltpu.VMEM((3, ROWS, ALL), BF)),
        ("final", pltpu.VMEM((ROWS, 1792), F32)),
        ("gacc", pltpu.VMEM((5, 8, 512), F32)),
        ("cos", pltpu.VMEM((SEQ, HD), F32)),
        ("sin", pltpu.VMEM((SEQ, HD), F32)),
        ("gsum", pltpu.VMEM((4, 8, 512), F32)),
        ("grecv", pltpu.VMEM((14, 8, 512), F32)),
        ("zs", dma((8, 24))),
        ("zr", dma((8, 24))),
        ("lsem", dma((21,))),
        ("osem", dma((10,))),
        ("xs", dma((18,))),
        ("xr", dma((18,))),
        ("p1xs", dma((48,))),
        ("p1xr", dma((48,))),
        ("p1ys", dma((24,))),
        ("p1yr", dma((24,))),
        ("q2s", dma((24,))),
        ("q2r", dma((24,))),
        ("p2xs", dma((12,))),
        ("p2xr", dma((12,))),
        ("p2ys", dma((12,))),
        ("p2yr", dma((12,))),
        ("lands", dma((24,))),
        ("gs", dma((10,))),
        ("ws", dma((26,))),
        ("wr", dma((26,))),
        ("gr", dma((10,))),
    ]
    names = [i[0] for i in ins] + [o[0] for o in outs] + [s[0] for s in scratch]
    results = pl.pallas_call(
        functools.partial(kernel, names),
        out_shape=[jax.ShapeDtypeStruct(o[1], o[2]) for o in outs],
        in_specs=[i[2] for i in ins],
        out_specs=[o[3] for o in outs],
        scratch_shapes=[s[1] for s in scratch],
        compiler_params=pltpu.CompilerParams(
            collective_id=0, has_side_effects=True, vmem_limit_bytes=63 * 1024 * 1024
        ),
        name="block",
    )(*[i[1] for i in ins])
    return arrange(*results[:4])


def arrange_kernel(out_in, tok_in, gains, shares, output, grad_tokens, gain1, qkv, out, gain2, gate_up, down, *scratch):
    out_v, tok_v, shares_v, sem = scratch
    down_at, gu_at, out_at, qkv_at = BASE

    def columns(core, first, count):
        return shares_v.at[core, :, first : first + count]

    def through(src, buf, dst, half):
        rows = slice(half * 64, half * 64 + 64)
        return (src.at[rows], buf.at[rows]), ((buf.at[rows], dst.at[rows]),)

    def of_shares(first, count, *stores):
        cols = slice(first, first + count)
        return (shares.at[:, :, cols], shares_v.at[:, :, cols]), stores

    moves = (
        through(out_in, out_v, output, 0),
        through(out_in, out_v, output, 1),
        through(tok_in, tok_v, grad_tokens, 0),
        through(tok_in, tok_v, grad_tokens, 1),
        of_shares(gu_at, FF, (columns(0, gu_at, FF), gate_up.at[0]), (columns(1, gu_at, FF), gate_up.at[1])),
        of_shares(
            qkv_at,
            768,
            (columns(0, qkv_at, 512), qkv.at[0]),
            (columns(0, qkv_at + 512, 256), qkv.at[1, :, 0:256]),
            (columns(1, qkv_at, 256), qkv.at[1, :, 256:512]),
            (columns(1, qkv_at + 256, 512), qkv.at[2]),
        ),
        of_shares(
            down_at,
            768,
            (columns(0, down_at, 768), down.at[:, 0:768]),
            (columns(1, down_at + 128, 640), down.at[:, 768:1408]),
        ),
        of_shares(
            out_at,
            256,
            (columns(0, out_at, 256), out.at[:, 0:256]),
            (columns(1, out_at, 256), out.at[:, 256:512]),
        ),
    )
    loads = [pltpu.make_async_copy(*move[0], sem.at[i]) for i, move in enumerate(moves)]
    for load in loads:
        load.start()
    for i in range(4):
        at = slice(i * 512, (i + 1) * 512)
        gain1[:, at] = gains[i : i + 1, :]
        gain2[:, at] = gains[4 + i : 5 + i, :]
    stores = []
    for load, move in zip(loads, moves):
        load.wait()
        for src, dst in move[1]:
            stores.append(pltpu.make_async_copy(src, dst, sem.at[len(moves) + len(stores)]))
            stores[-1].start()
    for store in stores:
        store.wait()


def arrange(output, grad_tokens, gains, shares):
    vmem = pl.BlockSpec(memory_space=pltpu.VMEM)
    hbm = pl.BlockSpec(memory_space=pl.ANY)
    outs = (
        ((ROWS, D), hbm),
        ((ROWS, D), hbm),
        ((1, D), vmem),
        ((3, 64, 512), hbm),
        ((64, 512), hbm),
        ((1, D), vmem),
        ((2, 64, FF), hbm),
        ((64, FF), hbm),
    )
    results = pl.pallas_call(
        arrange_kernel,
        out_shape=[jax.ShapeDtypeStruct(o[0], F32) for o in outs],
        in_specs=[hbm, hbm, vmem, hbm],
        out_specs=[o[1] for o in outs],
        scratch_shapes=[
            pltpu.VMEM((ROWS, D), F32),
            pltpu.VMEM((ROWS, D), F32),
            pltpu.VMEM((2, 64, ALL), F32),
            pltpu.SemaphoreType.DMA((22,)),
        ],
        compiler_params=pltpu.CompilerParams(vmem_limit_bytes=63 * 1024 * 1024),
        name="arrange",
    )(output, grad_tokens, gains, shares)
    output, grad_tokens, gain1, qkv, out, gain2, gate_up, down = results
    return output, grad_tokens, gain1.reshape(D), qkv, out.T, gain2.reshape(D), gate_up, down.T


def solution(mesh):
    placed = (
        P(("dp", "tensor"), None),
        P(),
        P(None, None, "tensor"),
        P("tensor", None),
        P(),
        P(None, None, "tensor"),
        P("tensor", None),
        P(("dp", "tensor"), None),
        P("dp"),
    )
    return jax.shard_map(
        block,
        mesh=mesh,
        in_specs=placed,
        out_specs=(
            P(("dp", "tensor"), None),
            P(("dp", "tensor"), None),
            P(),
            P(None, "dp", "tensor"),
            P("tensor", "dp"),
            P(),
            P(None, "dp", "tensor"),
            P("tensor", "dp"),
        ),
        check_vma=False,
    )
```
